32 devices in a mesh: dp: 8 (over z, x), tensor: 4 (over y, core).
Axes of the slice: x: 2, y: 2, z: 4, core: 2. Of those that a mesh axis runs over, the one named last changes fastest.
Arguments:
- inputs: bfloat16 [16384, 1024], P(('dp', 'tensor')), may hold values from -6 to 6
- cotangent: bfloat16 [16384, 1024], P(('dp', 'tensor')), may hold values from -6 to 6
- lengths: int32 [8, 8], P('dp'), may hold values from 1 to 2041, as said below
- adapter_index: int32 [8], P('dp'), may hold values from 0 to 7
- w_qkv: bfloat16 [3, 1024, 1024], P(None, 'dp', 'tensor'), may hold values from -0.1875 to 0.1875
- w_out: bfloat16 [1024, 1024], P('tensor', 'dp'), may hold values from -4 to 4
- w_fc1: bfloat16 [1024, 4096], P('dp', 'tensor'), may hold values from -0.1875 to 0.1875
- w_fc2: bfloat16 [4096, 1024], P('tensor', 'dp'), may hold values from -0.09375 to 0.09375
- ln1_gain: bfloat16 [1024], P('dp'), may hold values from 0.5 to 1.5
- ln1_bias: bfloat16 [1024], P('dp'), may hold values from -2.5 to 2.5
- ln2_gain: bfloat16 [1024], P('dp'), may hold values from 0.5 to 1.5
- ln2_bias: bfloat16 [1024], P('dp'), may hold values from -2.5 to 2.5
- down_qkv: bfloat16 [3, 8, 1024, 16], P(None, None, 'dp'), may hold values from -0.1875 to 0.1875
- up_qkv: bfloat16 [3, 8, 16, 1024], P(None, None, 'dp', 'tensor'), may hold values from -0.75 to 0.75
- down_out: bfloat16 [8, 1024, 16], P(None, 'tensor', 'dp'), may hold values from -0.1875 to 0.1875
- up_out: bfloat16 [8, 16, 1024], P(None, None, 'dp'), may hold values from -0.75 to 0.75
- down_fc1: bfloat16 [8, 1024, 16], P(None, 'dp'), may hold values from -0.1875 to 0.1875
- up_fc1: bfloat16 [8, 16, 4096], P(None, 'dp', 'tensor'), may hold values from -0.75 to 0.75
- down_fc2: bfloat16 [8, 4096, 16], P(None, 'tensor', 'dp'), may hold values from -0.09375 to 0.09375
- up_fc2: bfloat16 [8, 16, 1024], P(None, None, 'dp'), may hold values from -0.75 to 0.75
Outputs:
- output: bfloat16 [16384, 1024], P(('dp', 'tensor'))
- grad_input: float32 [16384, 1024], P(('dp', 'tensor'))
- grad_down_qkv: float32 [3, 8, 1024, 16], P(None, None, ('dp', 'tensor'))
- grad_up_qkv: float32 [3, 8, 16, 1024], P(None, None, 'dp', 'tensor')
- grad_down_out: float32 [8, 1024, 16], P(None, 'tensor', 'dp')
- grad_up_out: float32 [8, 16, 1024], P(None, None, ('dp', 'tensor'))
- grad_down_fc1: float32 [8, 1024, 16], P(None, ('dp', 'tensor'))
- grad_up_fc1: float32 [8, 16, 4096], P(None, 'dp', 'tensor')
- grad_down_fc2: float32 [8, 4096, 16], P(None, 'tensor', 'dp')
- grad_up_fc2: float32 [8, 16, 1024], P(None, None, ('dp', 'tensor'))
The draws below stay inside these ranges and needn't reach their ends.
Inputs may be any that keep to these rules, and one draw needn't show every extreme that they name: Each row holds 8 document lengths that sum to 2048.
All inputs are finite; a program needn't handle non-finite values.
Results may differ from the reference program's by a relative error of at most 0.022.
Values may be sent and summed in bfloat16 or wider, within the bound.
No kernel may reach another device: no remote copies, remote signals or barrier semaphores. Data moves between devices by JAX's collectives and lax.ppermute only.
A program may use at most 192 MiB of HBM per device.

```python
import jax
import jax.numpy as jnp
from jax import lax

D = 1024
H = 16
HD = 64
FF = 4096
R = 16
NSET = 8
NDOC = 8
SEQ = 2048
SEQS = 8
TOKENS = 16384
N_TENSOR = 4


def draw_lengths(key, part):
    key = jax.random.fold_in(key, 11)
    first_key, second_key, spot_key, row_key = jax.random.split(key, 4)
    shard_rows = SEQ // N_TENSOR
    limit = max(1, shard_rows // NDOC)
    first = jax.random.randint(first_key, (SEQS, NDOC), 0, limit)
    second = jax.random.randint(second_key, (SEQS, NDOC), 0, limit)
    short_docs = 1 + first * second // limit
    chosen_row = jax.random.randint(row_key, (), 0, SEQS)
    row_places = jnp.arange(SEQS, dtype=jnp.int32)[:, None]
    short_docs = jnp.where(row_places == chosen_row, 1, short_docs)
    spot = jax.random.randint(spot_key, (SEQS, 1), 1, NDOC - 1)
    places = jnp.arange(NDOC, dtype=jnp.int32)[None, :]
    others = jnp.where(places == spot, 0, short_docs)
    long_doc = SEQ - jnp.sum(others, axis=1, keepdims=True)
    return jnp.where(places == spot, long_doc, others).astype(jnp.int32)


def place_ends(drawn, own_key, smallest, top_value):
    spot = [jax.random.randint(jax.random.fold_in(own_key, axis), (), 0, length) for axis, length in enumerate(drawn.shape)]
    main_axis = drawn.shape.index(max(drawn.shape))
    next_to = spot[:main_axis] + [(spot[main_axis] + 1) % drawn.shape[main_axis]] + spot[main_axis + 1:]
    return drawn.at[tuple(spot)].set(smallest).at[tuple(next_to)].set(top_value)


def shard_levels(own_key, shape, cuts, least, top_value):
    factor_of, own = 1.0, jax.random.fold_in(own_key, 6)
    for position, blocks in cuts:
        draws = jnp.exp(jax.random.uniform(jax.random.fold_in(own, position), (blocks,), jnp.float32, least / len(cuts), top_value / len(cuts)))
        factor_of = factor_of * jnp.repeat(draws, shape[position] // blocks).reshape([-1 if axis == position else 1 for axis in range(len(shape))])
    return factor_of


def normal_values(stream_key, shape, deviation, most, shards=(), kind=jnp.bfloat16):
    factor_of = shard_levels(stream_key, shape, shards, -0.22, 0.18) if shards else 1.0
    entries = jax.random.normal(stream_key, shape, jnp.float32) * deviation * factor_of
    return jnp.minimum(jnp.maximum(entries, -most), most).astype(kind)


def setup_inputs(seed: int = 0) -> dict:
    key_list = jax.random.split(jax.random.key(seed), 21)
    inputs = normal_values(key_list[0], (TOKENS, D), 1.0, 6.0, ((0, 32),))
    cotangent = normal_values(key_list[1], (TOKENS, D), 1.0, 6.0, ((0, 32),))
    lengths = draw_lengths(jax.random.fold_in(key_list[20], 71), 0)
    adapter_index = place_ends(jax.random.randint(key_list[3], (SEQS,), 0, NSET), jax.random.fold_in(key_list[3], 1), 0, NSET - 1).astype(jnp.int32)
    w_qkv = normal_values(key_list[4], (3, D, D), D ** -0.5, 0.1875, ((1, 8), (2, 4)))
    w_out = normal_values(key_list[5], (D, D), (max(1, (4 * D) // SEQ)) ** -0.5, 4.0, ((0, 4), (1, 8)))
    w_fc1 = normal_values(key_list[6], (D, FF), D ** -0.5, 0.1875, ((0, 8), (1, 4)))
    w_fc2 = normal_values(key_list[7], (FF, D), FF ** -0.5, 0.09375, ((0, 4), (1, 8)))
    ln1_gain = jnp.clip(1.0 + 0.1 * jax.random.normal(key_list[8], (D,), jnp.float32), 0.5, 1.5).astype(jnp.bfloat16)
    ln1_bias = normal_values(key_list[9], (D,), 0.3, 2.5, ((0, 8),))
    ln2_gain = jnp.clip(1.0 + 0.1 * jax.random.normal(key_list[10], (D,), jnp.float32), 0.5, 1.5).astype(jnp.bfloat16)
    ln2_bias = normal_values(key_list[11], (D,), 0.3, 2.5, ((0, 8),))
    down_qkv = normal_values(key_list[12], (3, NSET, D, R), D ** -0.5, 0.1875, ((2, 8),))
    up_qkv = normal_values(key_list[13], (3, NSET, R, D), (4 * R) ** -0.5, 0.75, ((2, 8), (3, 4)))
    down_out = normal_values(key_list[14], (NSET, D, R), D ** -0.5, 0.1875, ((1, 4), (2, 8)))
    up_out = normal_values(key_list[15], (NSET, R, D), (4 * R) ** -0.5, 0.75, ((2, 8),))
    down_fc1 = normal_values(key_list[16], (NSET, D, R), D ** -0.5, 0.1875, ((1, 8),))
    up_fc1 = normal_values(key_list[17], (NSET, R, FF), (4 * R) ** -0.5, 0.75, ((1, 8), (2, 4)))
    down_fc2 = normal_values(key_list[18], (NSET, FF, R), FF ** -0.5, 0.09375, ((1, 4), (2, 8)))
    up_fc2 = normal_values(key_list[19], (NSET, R, D), (4 * R) ** -0.5, 0.75, ((2, 8),))
    return dict(inputs=inputs, cotangent=cotangent, lengths=lengths, adapter_index=adapter_index, w_qkv=w_qkv, w_out=w_out, w_fc1=w_fc1, w_fc2=w_fc2, ln1_gain=ln1_gain, ln1_bias=ln1_bias, ln2_gain=ln2_gain, ln2_bias=ln2_bias, down_qkv=down_qkv, up_qkv=up_qkv, down_out=down_out, up_out=up_out, down_fc1=down_fc1, up_fc1=up_fc1, down_fc2=down_fc2, up_fc2=up_fc2)


HIGHEST = lax.Precision.HIGHEST
NEG = -1000000000.0
EPS = 1e-05

@jax.custom_vjp
def low(v):
    return lax.optimization_barrier(v.astype(jnp.bfloat16)).astype(jnp.float32)

@jax.custom_vjp
def low_back(v):
    return v

def low_keep(v):
    return (low(v), None)

def low_pass(kept, grad):
    return (grad,)

def back_keep(v):
    return (v, None)

def back_low(kept, grad):
    return (low(grad),)
low.defvjp(low_keep, low_pass)
low_back.defvjp(back_keep, back_low)

def product(left, right):
    return jnp.dot(left, right, precision=HIGHEST)

def norm_rows(values, gain, shift):
    center = values - lax.optimization_barrier(jnp.mean(values, axis=-1, keepdims=True))
    variance = lax.optimization_barrier(jnp.mean(center * center, axis=-1, keepdims=True))
    return center * lax.rsqrt(variance + EPS) * gain + shift

def segment_ids(doc_lengths, total):
    ends = jnp.cumsum(doc_lengths.astype(jnp.int32)).astype(jnp.int32)
    places = jnp.arange(total, dtype=jnp.int32)
    return lax.optimization_barrier(jnp.sum((places[:, None] >= ends[None, :]).astype(jnp.int32), axis=1)).astype(jnp.int32)

def attend(queries, key_rows, value_rows, segments):
    block_rows = min(512, SEQ)
    count = SEQ // block_rows
    scale = HD ** (-0.5)

    def one_block(pieces):
        query_block, query_segs = pieces
        scores = jnp.einsum('qhd,khd->hqk', query_block, key_rows, precision=HIGHEST) * scale
        scores = low_back(scores)
        scores = jnp.where((query_segs[:, None] == segments[None, :])[None], scores, NEG)
        row_max = lax.optimization_barrier(jnp.max(scores, axis=-1, keepdims=True))
        exp_scores = jnp.exp(scores - row_max)
        attn_prob = exp_scores / lax.optimization_barrier(jnp.sum(exp_scores, axis=-1, keepdims=True))
        return jnp.einsum('hqk,khd->qhd', low(attn_prob), value_rows, precision=HIGHEST)
    mixed = lax.map(jax.checkpoint(one_block), (queries.reshape(count, block_rows, H, HD), segments.reshape(count, block_rows)))
    return mixed.reshape(SEQ, H * HD)

def choose(set_onehot, table, axis):
    return jnp.tensordot(set_onehot, table, axes=([0], [axis]), precision=HIGHEST)

def one_sequence(seq_rows, segments, set_onehot, weights):
    w_qkv, w_out, w_fc1, w_fc2, ln1_gain, ln1_bias, ln2_gain, ln2_bias, down_qkv, up_qkv, down_out, up_out, down_fc1, up_fc1, down_fc2, up_fc2 = weights
    sel_down_qkv = choose(set_onehot, down_qkv, 1)
    sel_up_qkv = choose(set_onehot, up_qkv, 1)
    projected = []
    for which in range(3):
        small = low(low_back(product(seq_rows, sel_down_qkv[which])))
        full = product(seq_rows, w_qkv[which]) + product(small, sel_up_qkv[which])
        projected.append(low(low_back(full)).reshape(SEQ, H, HD))
    att = low(low_back(attend(projected[0], projected[1], projected[2], segments)))
    u_out = low(low_back(product(att, choose(set_onehot, down_out, 0))))
    branch_a = low_back(product(att, w_out) + product(u_out, choose(set_onehot, up_out, 0)))
    normed = norm_rows(seq_rows + branch_a, ln1_gain, ln1_bias)
    normed_low = low(normed)
    u_fc1 = low(low_back(product(normed_low, choose(set_onehot, down_fc1, 0))))
    pre_gelu = low_back(product(normed_low, w_fc1) + product(u_fc1, choose(set_onehot, up_fc1, 0)))
    hidden_act = low(jax.nn.gelu(pre_gelu, approximate=False))
    u_fc2 = low(low_back(product(hidden_act, choose(set_onehot, down_fc2, 0))))
    branch_f = low_back(product(hidden_act, w_fc2) + product(u_fc2, choose(set_onehot, up_fc2, 0)))
    return norm_rows(normed + branch_f, ln2_gain, ln2_bias)

def reference(inputs, cotangent, lengths, adapter_index, w_qkv, w_out, w_fc1, w_fc2, ln1_gain, ln1_bias, ln2_gain, ln2_bias, down_qkv, up_qkv, down_out, up_out, down_fc1, up_fc1, down_fc2, up_fc2):
    weights = tuple((table.astype(jnp.float32) for table in (w_qkv, w_out, w_fc1, w_fc2, ln1_gain, ln1_bias, ln2_gain, ln2_bias, down_qkv, up_qkv, down_out, up_out, down_fc1, up_fc1, down_fc2, up_fc2)))
    all_segments = jax.vmap(lambda doc_row: segment_ids(doc_row, SEQ))(lengths)
    onehots = (adapter_index[:, None] == jnp.arange(NSET, dtype=jnp.int32)[None, :]).astype(jnp.float32)
    seq_inputs = inputs.astype(jnp.float32).reshape(SEQS, SEQ, D)

    def forward(layer_in, layer_weights):

        def advance(running, pieces):
            seq_rows, segments, set_onehot = pieces
            return (running, one_sequence(seq_rows, segments, set_onehot, layer_weights))
        _, outs = lax.scan(advance, jnp.zeros((), jnp.float32), (layer_in, all_segments, onehots))
        return outs
    layer_out, backward = jax.vjp(forward, seq_inputs, weights)
    grad_rows, grads = backward(cotangent.astype(jnp.float32).reshape(SEQS, SEQ, D))
    return (layer_out.reshape(TOKENS, D).astype(jnp.bfloat16), grad_rows.reshape(TOKENS, D), grads[8], grads[9], grads[10], grads[11], grads[12], grads[13], grads[14], grads[15])
```

```python
import functools

import jax
import jax.numpy as jnp
from jax import lax
from jax.experimental import pallas as pl
from jax.experimental.pallas import tpu as pltpu
from jax.sharding import PartitionSpec as P

HD = 64
EPS = 1e-05
NEG = -1000000000.0
LOG2E = 1.4426950408889634
BF = jnp.bfloat16
F32 = jnp.float32
VMEM_LIMIT = 60 * 2**20


def mm(left, right):
    return jnp.dot(left, right, preferred_element_type=F32)


def mm_nt(left, right):
    return lax.dot_general(left, right, (((1,), (1,)), ((), ())), preferred_element_type=F32)


def transpose_small(value):
    return value.astype(F32).T.astype(BF)


def segment_ids(doc_lengths, total):
    ends = jnp.cumsum(doc_lengths)
    places = jnp.arange(total, dtype=jnp.int32)
    return jnp.sum((places[:, None] >= ends[None, :]).astype(jnp.int32), axis=1)


def attend_forward_kernel(
    heads, block, chunk, q_ref, k_ref, v_ref, segq_ref, segk_ref,
    att_ref, e_ref, l_ref, keys_wide, values_t, scores,
):
    length = k_ref.shape[0]

    @pl.when(pl.program_id(0) == 0)
    def _():
        onehot = (lax.broadcasted_iota(jnp.int32, (length, 128), 1) == segk_ref[...]).astype(BF)
        ones = (lax.broadcasted_iota(jnp.int32, (16, length), 0) == 0).astype(BF)
        flipped = v_ref[...].T
        for h in range(heads):
            key = k_ref[:, h * HD : (h + 1) * HD]
            keys_wide[h, :, 0:HD] = key
            keys_wide[h, :, HD : 2 * HD] = key
            keys_wide[h, :, 2 * HD :] = onehot
            values_t[h, 0:HD, :] = flipped[h * HD : (h + 1) * HD, :]
            values_t[h, HD:, :] = ones

    flipped_q = q_ref[...].astype(F32).T * (HD ** (-0.5) * LOG2E)
    mask = jnp.where(
        lax.broadcasted_iota(jnp.int32, (128, block), 0) == segq_ref[...], 0.0, NEG
    ).astype(BF)
    mixed = []
    for h in range(heads):
        query = flipped_q[h * HD : (h + 1) * HD, :]
        high = query.astype(BF)
        low = (query - high.astype(F32)).astype(BF)
        right = jnp.concatenate([high, low, mask], axis=0)
        top = None
        for c in range(length // chunk):
            part = mm(keys_wide[h, c * chunk : (c + 1) * chunk, :], right)
            scores[h, c * chunk : (c + 1) * chunk, :] = part
            part = jnp.max(part.reshape(chunk // 8, 8, block), axis=0)
            top = part if top is None else jnp.maximum(top, part)
        top = jnp.max(top, axis=0, keepdims=True)
        total = None
        for c in range(length // chunk):
            e = jnp.exp2(scores[h, c * chunk : (c + 1) * chunk, :] - top).astype(BF)
            e_ref[h, 0, c * chunk : (c + 1) * chunk, :] = e
            part = mm(values_t[h, :, c * chunk : (c + 1) * chunk], e)
            total = part if total is None else total + part
        row_sum = total[HD : HD + 1, :]
        l_ref[h, 0] = jnp.broadcast_to(row_sum, (8, block))
        mixed.append(total[0:HD, :] / row_sum)
    att_ref[...] = jnp.concatenate(mixed, axis=0).T.astype(BF)


def attend_forward(q, k, v, segments, group, heads):
    length = q.shape[0]
    width = heads * HD
    block = min(512, length)
    chunk = min(512, length)
    count = length // block
    return pl.pallas_call(
        functools.partial(attend_forward_kernel, heads, block, chunk),
        grid=(count,),
        in_specs=[
            pl.BlockSpec((block, width), lambda i: (i, group)),
            pl.BlockSpec((length, width), lambda i: (0, group)),
            pl.BlockSpec((length, width), lambda i: (0, group)),
            pl.BlockSpec((1, block), lambda i: (0, i)),
            pl.BlockSpec((length, 1), lambda i: (0, 0)),
        ],
        out_specs=[
            pl.BlockSpec((block, width), lambda i: (i, 0)),
            pl.BlockSpec((heads, 1, length, block), lambda i: (0, i, 0, 0)),
            pl.BlockSpec((heads, 1, 8, block), lambda i: (0, i, 0, 0)),
        ],
        out_shape=[
            jax.ShapeDtypeStruct((length, width), BF),
            jax.ShapeDtypeStruct((heads, count, length, block), BF),
            jax.ShapeDtypeStruct((heads, count, 8, block), F32),
        ],
        scratch_shapes=[
            pltpu.VMEM((heads, length, 256), BF),
            pltpu.VMEM((heads, HD + 16, length), BF),
            pltpu.VMEM((heads, length, block), F32),
        ],
        compiler_params=pltpu.CompilerParams(
            vmem_limit_bytes=VMEM_LIMIT, dimension_semantics=("arbitrary",)
        ),
        cost_estimate=pl.CostEstimate(
            flops=4 * heads * length * length * 256,
            bytes_accessed=heads * length * length * 2,
            transcendentals=heads * length * length,
        ),
        name="attend_forward",
    )(q, k, v, segments[None, :], segments[:, None])


def attend_backward_kernel(
    heads, block, chunk, q_ref, k_ref, v_ref, o_ref, do_ref, e_ref, l_ref,
    dq_ref, dk_ref, dv_ref, values_wide, keys_t, dk_sum, dv_sum,
):
    length = k_ref.shape[0]
    width = heads * HD
    i = pl.program_id(0)

    @pl.when(i == 0)
    def _():
        ones = (lax.broadcasted_iota(jnp.int32, (length, 128), 1) < 2).astype(BF)
        for h in range(heads):
            value = v_ref[:, h * HD : (h + 1) * HD]
            values_wide[h, :, 0:HD] = value
            values_wide[h, :, HD : 2 * HD] = value
            values_wide[h, :, 2 * HD :] = ones
        keys_t[...] = k_ref[...].T
        dk_sum[...] = jnp.zeros_like(dk_sum)
        dv_sum[...] = jnp.zeros_like(dv_sum)

    q = q_ref[...]
    flipped_do = do_ref[...].astype(F32).T
    flipped_o = o_ref[...].astype(F32).T
    lane = lax.broadcasted_iota(jnp.int32, (block, width), 1)
    row = lax.broadcasted_iota(jnp.int32, (128, block), 0)
    grads = []
    for h in range(heads):
        own = slice(h * HD, (h + 1) * HD)
        inverse = 1.0 / l_ref[h, 0, 0:1, :]
        dot = -jnp.sum(flipped_do[own] * flipped_o[own], axis=0, keepdims=True) * inverse
        scaled = flipped_do[own] * inverse
        high = scaled.astype(BF)
        low = (scaled - high.astype(F32)).astype(BF)
        dot_high = dot.astype(BF)
        dot_low = (dot - dot_high.astype(F32)).astype(BF)
        dots = jnp.where(row == 0, dot_high, jnp.where(row == 1, dot_low, jnp.zeros_like(dot_low)))
        right = jnp.concatenate([high, low, dots], axis=0)
        do_rows = high.T
        if heads == 2:
            empty = jnp.zeros_like(do_rows)
            do_rows = jnp.concatenate([do_rows, empty] if h == 0 else [empty, do_rows], axis=1)
        query = jnp.where((lane >= h * HD) & (lane < (h + 1) * HD), q, jnp.zeros_like(q))
        total = None
        for c in range(length // chunk):
            rows = slice(c * chunk, (c + 1) * chunk)
            e = e_ref[h, 0, rows, :]
            part = mm(values_wide[h, rows, :], right)
            ds = (e.astype(F32) * part).astype(BF)
            dv_sum[rows, :] += mm(e, do_rows)
            dk_sum[rows, :] += mm(ds, query)
            part = mm(keys_t[own, rows], ds)
            total = part if total is None else total + part
        grads.append(total * HD ** (-0.5))
    dq_ref[...] = jnp.concatenate(grads, axis=0).T.astype(BF)

    @pl.when(i == pl.num_programs(0) - 1)
    def _():
        dk_ref[...] = (dk_sum[...] * HD ** (-0.5)).astype(BF)
        dv_ref[...] = dv_sum[...].astype(BF)


def attend_backward(q, k, v, att, d_att, e, row_sum, group, heads):
    length = q.shape[0]
    width = heads * HD
    block = e.shape[3]
    chunk = min(512, length)
    count = length // block
    whole = pl.BlockSpec((length, width), lambda i: (0, group))
    return pl.pallas_call(
        functools.partial(attend_backward_kernel, heads, block, chunk),
        grid=(count,),
        in_specs=[
            pl.BlockSpec((block, width), lambda i: (i, group)),
            whole,
            whole,
            pl.BlockSpec((block, width), lambda i: (i, 0)),
            pl.BlockSpec((block, width), lambda i: (i, group)),
            pl.BlockSpec((heads, 1, length, block), lambda i: (0, i, 0, 0)),
            pl.BlockSpec((heads, 1, 8, block), lambda i: (0, i, 0, 0)),
        ],
        out_specs=[
            pl.BlockSpec((block, width), lambda i: (i, 0)),
            pl.BlockSpec((length, width), lambda i: (0, 0)),
            pl.BlockSpec((length, width), lambda i: (0, 0)),
        ],
        out_shape=[jax.ShapeDtypeStruct((length, width), BF)] * 3,
        scratch_shapes=[
            pltpu.VMEM((heads, length, 256), BF),
            pltpu.VMEM((width, length), BF),
            pltpu.VMEM((length, width), F32),
            pltpu.VMEM((length, width), F32),
        ],
        compiler_params=pltpu.CompilerParams(
            vmem_limit_bytes=VMEM_LIMIT, dimension_semantics=("arbitrary",)
        ),
        cost_estimate=pl.CostEstimate(
            flops=8 * heads * length * length * 256,
            bytes_accessed=heads * length * length * 2,
            transcendentals=0,
        ),
        name="attend_backward",
    )(q, k, v, att, d_att, e, row_sum)


def normal_parts(z):
    density = jnp.exp2(z * z * (-0.5 * LOG2E))
    t = 1.0 / (1.0 + (0.3275911 * 0.5**0.5) * jnp.abs(z))
    poly = t * (
        0.254829592 * 0.5
        + t
        * (
            -0.284496736 * 0.5
            + t * (1.421413741 * 0.5 + t * (-1.453152027 * 0.5 + t * (1.061405429 * 0.5)))
        )
    )
    tail = poly * density
    return jnp.where(z < 0.0, tail, 1.0 - tail), density * 0.3989422804014327


def normalize(values):
    center = values - jnp.mean(values, axis=-1, keepdims=True)
    scale = lax.rsqrt(jnp.mean(center * center, axis=-1, keepdims=True) + EPS)
    return center * scale, scale


def normalize_back(e, normal, scale):
    return scale * (
        e
        - jnp.mean(e, axis=-1, keepdims=True)
        - normal * jnp.mean(e * normal, axis=-1, keepdims=True)
    )


def middle_kernel(
    cuts, hidden_block, perm_ref, att_ref, x_ref, cot_ref, wo_hbm, w1_hbm, w2_hbm,
    down_out, up_out, down_fc1, up_fc1, down_fc2, up_fc2, gain1, bias1, gain2, bias2,
    *rest,
):
    out_ref, dy1_ref = rest[0:2]
    d_att_refs = rest[2 : 2 + cuts]
    (
        g_up_fc2, g_down_fc2, g_up_fc1, g_down_fc1, g_up_out, g_down_out,
        wo, w1, w2, hidden, slope, normal1, normed, low_rows, total, wo_sem, w1_sem, w2_sem,
    ) = rest[2 + cuts :]
    rows, model = x_ref.shape
    units = w1.shape[1]

    def fetch(source, a, b, target, row, col, sem):
        height, width = source.shape[2:]
        return pltpu.make_async_copy(
            source.at[a, b],
            target.at[pl.ds(row * height, height), pl.ds(col * width, width)],
            sem,
        )

    outer, inner = wo_hbm.shape[:2]
    for b in range(inner):
        for a in range(outer):
            fetch(wo_hbm, a, perm_ref[b] if inner > 1 else 0, wo, b, a, wo_sem).start()
    for b in range(w1_hbm.shape[1]):
        for a in range(w1_hbm.shape[0]):
            fetch(w1_hbm, a, b, w1, a, b, w1_sem.at[b]).start()
        for a in range(w2_hbm.shape[0]):
            fetch(w2_hbm, a, b, w2, b, a, w2_sem.at[b]).start()

    pltpu.make_async_copy(wo, wo, wo_sem).wait()
    att = att_ref[...]
    u_out = mm_nt(att, down_out[...]).astype(BF)
    first = x_ref[...].astype(F32) + mm(att, wo[...]) + mm(u_out, up_out[...])
    normal, scale1 = normalize(first)
    normal1[...] = normal
    full = normal * gain1[...].astype(F32) + bias1[...].astype(F32)
    normed[...] = full
    low_rows[...] = full.astype(BF)
    u_fc1 = mm_nt(low_rows[...], down_fc1[...]).astype(BF)

    blocks = units // hidden_block
    per_cut = w1_hbm.shape[3] // hidden_block

    def before(i):
        cols = slice(i * hidden_block, (i + 1) * hidden_block)
        if i % per_cut == 0:
            part = w1_hbm.shape[3]
            b = i // per_cut
            view = w1.at[:, b * part : (b + 1) * part]
            pltpu.make_async_copy(view, view, w1_sem.at[b]).wait()
            part = w2_hbm.shape[2]
            view = w2.at[b * part : (b + 1) * part, :]
            pltpu.make_async_copy(view, view, w2_sem.at[b]).wait()
        return mm(low_rows[...], w1[:, cols]) + mm(u_fc1, up_fc1[:, cols])

    z = before(0)
    u_sum = None
    for i in range(blocks):
        cols = slice(i * hidden_block, (i + 1) * hidden_block)
        following = before(i + 1) if i + 1 < blocks else None
        phi_sum, phi = normal_parts(z)
        act = (z * phi_sum).astype(BF)
        hidden[:, cols] = act
        slope[:, cols] = phi_sum + z * phi
        part = mm(act, w2[cols, :])
        total[...] = part if i == 0 else total[...] + part
        part = mm_nt(act, down_fc2[:, cols])
        u_sum = part if u_sum is None else u_sum + part
        z = following
    u_fc2 = u_sum.astype(BF)
    second = normed[...] + total[...] + mm(u_fc2, up_fc2[...])
    normal2, scale2 = normalize(second)
    gain = gain2[...].astype(F32)
    out_ref[...] = (normal2 * gain + bias2[...].astype(F32)).astype(BF)
    d_second = normalize_back(cot_ref[...].astype(F32) * gain, normal2, scale2)
    total[...] = d_second
    d_ffn = d_second.astype(BF)
    d_u2 = mm_nt(d_ffn, up_fc2[...]).astype(BF)
    d_u2_t = transpose_small(d_u2)
    g_up_fc2[...] = mm(transpose_small(u_fc2), d_ffn).astype(BF)
    u_fc1_t = transpose_small(u_fc1)

    def before_back(i):
        cols = slice(i * hidden_block, (i + 1) * hidden_block)
        return mm_nt(d_ffn, w2[cols, :]) + mm(d_u2, down_fc2[:, cols])

    d_hidden = before_back(0)
    u_sum = None
    for i in range(blocks):
        cols = slice(i * hidden_block, (i + 1) * hidden_block)
        following = before_back(i + 1) if i + 1 < blocks else None
        d_pre = (d_hidden * slope[:, cols]).astype(BF)
        g_down_fc2[:, cols] = mm(d_u2_t, hidden[:, cols]).astype(BF)
        g_up_fc1[:, cols] = mm(u_fc1_t, d_pre).astype(BF)
        total[...] += mm_nt(d_pre, w1[:, cols])
        part = mm_nt(d_pre, up_fc1[:, cols])
        u_sum = part if u_sum is None else u_sum + part
        d_hidden = following
    d_u1 = u_sum.astype(BF)
    d_normed = total[...] + mm(d_u1, down_fc1[...])
    g_down_fc1[...] = mm(transpose_small(d_u1), low_rows[...]).astype(BF)
    d_first = normalize_back(d_normed * gain1[...].astype(F32), normal1[...], scale1)
    dy1_ref[...] = d_first
    d_a = d_first.astype(BF)
    d_uo = mm_nt(d_a, up_out[...]).astype(BF)
    g_up_out[...] = mm(transpose_small(u_out), d_a).astype(BF)
    g_down_out[...] = mm(transpose_small(d_uo), att).astype(BF)
    d_att = (mm_nt(d_a, wo[...]) + mm(d_uo, down_out[...])).astype(BF)
    width = model // cuts
    for k in range(cuts):
        d_att_refs[k][...] = d_att[:, k * width : (k + 1) * width]


def middle(perm, att, x, cot, wo, w1, w2, adapters, norms):
    rows, model = x.shape
    units = w1.shape[1] * w1.shape[3]
    rank = adapters[0].shape[0]
    cuts = perm.shape[0]
    hidden_block = min(512, w1.shape[3])
    vmem = pl.BlockSpec(memory_space=pltpu.VMEM)
    anywhere = pl.BlockSpec(memory_space=pl.ANY)
    wide = jax.ShapeDtypeStruct((rank, units), BF)
    narrow = jax.ShapeDtypeStruct((rank, model), BF)
    out_shape = (
        [jax.ShapeDtypeStruct((rows, model), BF), jax.ShapeDtypeStruct((rows, model), F32)]
        + [jax.ShapeDtypeStruct((rows, model // cuts), BF)] * cuts
        + [narrow, wide, wide, narrow, narrow, narrow]
    )
    return pl.pallas_call(
        functools.partial(middle_kernel, cuts, hidden_block),
        in_specs=[pl.BlockSpec(memory_space=pltpu.SMEM)]
        + [vmem] * 3
        + [anywhere] * 3
        + [vmem] * 10,
        out_specs=[vmem] * len(out_shape),
        out_shape=out_shape,
        scratch_shapes=[
            pltpu.VMEM((model, model), BF),
            pltpu.VMEM((model, units), BF),
            pltpu.VMEM((units, model), BF),
            pltpu.VMEM((rows, units), BF),
            pltpu.VMEM((rows, units), F32),
            pltpu.VMEM((rows, model), F32),
            pltpu.VMEM((rows, model), F32),
            pltpu.VMEM((rows, model), BF),
            pltpu.VMEM((rows, model), F32),
            pltpu.SemaphoreType.DMA,
            pltpu.SemaphoreType.DMA((w1.shape[1],)),
            pltpu.SemaphoreType.DMA((w2.shape[1],)),
        ],
        compiler_params=pltpu.CompilerParams(vmem_limit_bytes=VMEM_LIMIT),
        cost_estimate=pl.CostEstimate(
            flops=2 * rows * model * (2 * model + 4 * units),
            bytes_accessed=2 * model * (model + 2 * units),
            transcendentals=2 * rows * units,
        ),
        name="middle",
    )(perm, att, x, cot, wo, w1, w2, *adapters, *norms)


def blocks_or_whole(gathered, rows_axis):
    outer, inner, height, width = gathered.shape
    if width % 128 == 0:
        return gathered
    if rows_axis == "dp":
        whole = gathered.transpose(0, 2, 1, 3).reshape(outer * height, inner * width)
    else:
        whole = gathered.transpose(1, 2, 0, 3).reshape(inner * height, outer * width)
    return whole[None, None]


def shards(
    inputs, cotangent, lengths, adapter_index, w_qkv, w_out, w_fc1, w_fc2,
    ln1_gain, ln1_bias, ln2_gain, ln2_bias, down_qkv, up_qkv, down_out, up_out,
    down_fc1, up_fc1, down_fc2, up_fc2,
):
    n_dp = lax.axis_size("dp")
    n_t = lax.axis_size("tensor")
    every = ("dp", "tensor")
    mine = lax.axis_index("tensor")
    rows, model = inputs.shape
    length = rows * n_t
    n_set = down_qkv.shape[1]
    rank = down_qkv.shape[3]
    r_dp = rank // n_dp
    r_t = rank // n_t
    d_dp = model // n_dp
    c_t = model // n_t
    f_t = w_fc1.shape[1]
    f_all = f_t * n_t

    def swap(value, bit):
        return lax.ppermute(value, "tensor", [(i, i ^ bit) for i in range(n_t)])

    bits = []
    bit = n_t // 2
    while bit:
        bits.append(bit)
        bit //= 2
    order = [0]
    for bit in bits:
        order = order + [k ^ bit for k in order]
    perm = jnp.array(order, jnp.int32) ^ mine

    rows_all = inputs
    for bit in bits:
        rows_all = jnp.concatenate([rows_all, swap(rows_all, bit)], axis=0)
    w_qkv_all = lax.all_gather(w_qkv, "dp", axis=0)
    wo_all = lax.all_gather(w_out, every, axis=0)
    w1_all = lax.all_gather(w_fc1, every, axis=0)
    w2_all = lax.all_gather(w_fc2, every, axis=0)

    index_all = lax.all_gather(adapter_index, "dp", axis=0, tiled=True)
    onehot_all = (index_all[:, None] == jnp.arange(n_set, dtype=jnp.int32)[None, :]).astype(BF)

    def part_of_rank(value, axis):
        return lax.dynamic_slice_in_dim(value, mine * r_t, r_t, axis)

    tables = [
        part_of_rank(down_qkv.transpose(1, 0, 3, 2), 2),
        up_qkv.transpose(1, 0, 2, 3),
        down_out.transpose(0, 2, 1),
        part_of_rank(up_out, 1),
        part_of_rank(down_fc1.transpose(0, 2, 1), 1),
        up_fc1,
        down_fc2.transpose(0, 2, 1),
        part_of_rank(up_fc2, 1),
    ]
    sizes = [t.size // n_set for t in tables]
    table = jnp.concatenate([t.reshape(n_set, -1) for t in tables], axis=1)
    chosen = mm(onehot_all, table).astype(BF)
    norm_part = jnp.stack([ln1_gain, ln1_bias, ln2_gain, ln2_bias]).reshape(1, -1)
    chosen = jnp.concatenate([chosen, jnp.broadcast_to(norm_part, (n_dp, norm_part.size))], axis=1)
    sent = jnp.broadcast_to(chosen[:, None, :], (n_dp, n_t, chosen.shape[1])).reshape(n_dp * n_t, -1)
    came = lax.all_to_all(sent, every, 0, 0, tiled=True).reshape(n_dp, n_t, -1)
    pieces = []
    start = 0
    for size in sizes:
        pieces.append(came[:, :, start : start + size])
        start += size
    norms = came[:, 0, start:].reshape(n_dp, 4, d_dp).transpose(1, 0, 2).reshape(4, 1, model)

    def from_rank_parts(piece):
        return piece.reshape(n_dp, n_t, r_t, d_dp).transpose(1, 2, 0, 3).reshape(rank, model)

    def from_blocks(piece, width):
        return piece.reshape(n_dp, n_t, r_dp, width).transpose(0, 2, 1, 3).reshape(rank, n_t * width)

    sel_down_qkv = (
        pieces[0].reshape(n_dp, n_t, 3, r_t, d_dp).transpose(2, 1, 3, 0, 4).reshape(3 * rank, model)
    )
    up_mine = lax.dynamic_index_in_dim(pieces[1], mine, 1, keepdims=False)
    sel_up_qkv = up_mine.reshape(n_dp, 3, r_dp, c_t).transpose(1, 0, 2, 3).reshape(3, rank, c_t)

    def reorder(value):
        cols = value.reshape(rank, n_t, c_t)
        return jnp.concatenate(
            [lax.dynamic_index_in_dim(cols, perm[k], 1, keepdims=False) for k in range(n_t)], axis=1
        )

    where = jnp.array([order.index(k) for k in range(n_t)], jnp.int32)

    def restore(value):
        cols = value.reshape(rank, n_t, c_t)
        return jnp.concatenate(
            [
                lax.dynamic_index_in_dim(cols, where[k ^ mine], 1, keepdims=False)
                for k in range(n_t)
            ],
            axis=1,
        )

    adapters = [
        reorder(from_blocks(pieces[2], c_t)),
        from_rank_parts(pieces[3]),
        from_rank_parts(pieces[4]),
        from_blocks(pieces[5], f_t),
        from_blocks(pieces[6], f_t),
        from_rank_parts(pieces[7]),
    ]

    w_cols = w_qkv_all.transpose(1, 0, 2, 3).reshape(3, model, c_t)
    u_in = mm_nt(rows_all, sel_down_qkv).astype(BF)
    qkv = [
        (mm(rows_all, w_cols[j]) + mm(u_in[:, j * rank : (j + 1) * rank], sel_up_qkv[j])).astype(BF)
        for j in range(3)
    ]
    segments = segment_ids(lengths[0], length).reshape(n_t, rows)
    segments = jnp.concatenate(
        [lax.dynamic_index_in_dim(segments, perm[k], 0, keepdims=False) for k in range(n_t)]
    )
    heads = c_t // HD
    group_heads = 2 if heads % 2 == 0 else 1
    groups = heads // group_heads
    kept = []
    att_parts = [[] for _ in range(n_t)]
    for g in range(groups):
        att, e, row_sum = attend_forward(*qkv, segments, g, group_heads)
        kept.append((att, e, row_sum))
        for k in range(n_t):
            block = att[k * rows : (k + 1) * rows]
            att_parts[k].append(block if order[k] == 0 else swap(block, order[k]))
    att_own = jnp.concatenate([part for parts in att_parts for part in parts], axis=1)

    wo_blocks = wo_all.reshape(n_dp, n_t, c_t, d_dp)
    if d_dp % 128 == 0:
        wo_blocks = blocks_or_whole(wo_blocks, "tensor")
    else:
        wo_blocks = blocks_or_whole(jnp.take(wo_blocks, perm, axis=1), "tensor")
    w1_blocks = blocks_or_whole(w1_all.reshape(n_dp, n_t, d_dp, f_t), "dp")
    w2_blocks = blocks_or_whole(w2_all.reshape(n_dp, n_t, f_t, d_dp), "tensor")
    if w1_blocks.shape[1] != w2_blocks.shape[1]:
        w1_blocks = (
            w1_all.reshape(n_dp, n_t, d_dp, f_t)
            .transpose(0, 2, 1, 3)
            .reshape(1, 1, model, f_all)
        )
    done = middle(
        perm, att_own, inputs, cotangent, wo_blocks, w1_blocks, w2_blocks, adapters, list(norms)
    )
    output, d_first = done[0:2]
    d_att_blocks = done[2 : 2 + n_t]
    g_up_fc2, g_down_fc2, g_up_fc1, g_down_fc1, g_up_out, g_down_out = done[2 + n_t :]

    def share_cols(value):
        lead = value.size // model
        return (
            value.reshape(lead, n_dp, n_t, model // (n_dp * n_t))
            .transpose(1, 2, 0, 3)
            .reshape(n_dp * n_t, -1)
        )

    def share_blocks(value):
        width = value.shape[1] // n_t
        return (
            value.reshape(n_dp, r_dp, n_t, width).transpose(0, 2, 1, 3).reshape(n_dp * n_t, -1)
        )

    def exchange(parts):
        widths = [p.shape[1] for p in parts]
        got = lax.all_to_all(jnp.concatenate(parts, axis=1), every, 0, 0, tiled=True)
        return got, widths

    early, early_widths = exchange(
        [
            share_blocks(restore(g_down_out)),
            share_cols(g_up_out),
            share_cols(g_down_fc1),
            share_blocks(g_up_fc1),
            share_blocks(g_down_fc2),
            share_cols(g_up_fc2),
        ]
    )

    d_att_all = jnp.concatenate(
        [
            d_att_blocks[k] if order[k] == 0 else swap(d_att_blocks[k], order[k])
            for k in range(n_t)
        ],
        axis=0,
    )
    grads = [
        attend_backward(*qkv, kept[g][0], d_att_all, kept[g][1], kept[g][2], g, group_heads)
        for g in range(groups)
    ]
    d_qkv = [jnp.concatenate([grads[g][j] for g in range(groups)], axis=1) for j in range(3)]
    d_u_in = jnp.concatenate([mm_nt(d_qkv[j], sel_up_qkv[j]) for j in range(3)], axis=1).astype(BF)

    def rows_part(begin, end):
        part = mm(d_u_in[begin:end], sel_down_qkv)
        for j in range(3):
            part = part + mm_nt(d_qkv[j][begin:end], w_cols[j])
        return part

    span = length
    parts = None
    for bit in reversed(bits):
        half = span // 2
        if parts is None:
            far = swap(rows_part(half, span).astype(BF), bit)
            parts = rows_part(0, half) + far.astype(F32)
        else:
            far = swap(parts[half:].astype(BF), bit)
            parts = parts[:half] + far.astype(F32)
        span = half
    if parts is None:
        parts = rows_part(0, length)
    grad_input = d_first + parts

    tn = (((0,), (0,)), ((), ()))
    g_up_qkv = jnp.stack(
        [
            lax.dot_general(
                u_in[:, j * rank : (j + 1) * rank], d_qkv[j], tn, preferred_element_type=F32
            )
            for j in range(3)
        ]
    ).astype(BF)
    g_down_qkv = lax.dot_general(d_u_in, rows_all, tn, preferred_element_type=F32).astype(BF)
    up_share = (
        g_up_qkv.reshape(3, n_dp, r_dp, c_t).transpose(1, 0, 2, 3).reshape(n_dp, 1, -1)
    )
    up_share = jnp.broadcast_to(up_share, (n_dp, n_t, up_share.shape[2])).reshape(n_dp * n_t, -1)
    late, late_widths = exchange([share_cols(g_down_qkv), up_share])

    by_sender = jnp.broadcast_to(onehot_all[:, None, :], (n_dp, n_t, n_set)).reshape(-1, n_set)
    same_cols = (jnp.arange(n_dp * n_t, dtype=jnp.int32) % n_t == mine).astype(BF)

    def total(got, weights):
        return lax.dot_general(weights, got, tn, preferred_element_type=F32)

    early_sum = total(early, by_sender)
    pieces = []
    start = 0
    for width in early_widths:
        pieces.append(early_sum[:, start : start + width])
        start += width
    d_all = model // (n_dp * n_t)
    sum_down_out = pieces[0].reshape(n_set, r_dp, c_t).transpose(0, 2, 1)
    sum_up_out = pieces[1].reshape(n_set, rank, d_all)
    sum_down_fc1 = pieces[2].reshape(n_set, rank, d_all).transpose(0, 2, 1)
    sum_up_fc1 = pieces[3].reshape(n_set, r_dp, f_t)
    sum_down_fc2 = pieces[4].reshape(n_set, r_dp, f_t).transpose(0, 2, 1)
    sum_up_fc2 = pieces[5].reshape(n_set, rank, d_all)
    sum_down_qkv = (
        total(late[:, : late_widths[0]], by_sender)
        .reshape(n_set, 3, rank, d_all)
        .transpose(1, 0, 3, 2)
    )
    sum_up_qkv = (
        total(late[:, late_widths[0] :], by_sender * same_cols[:, None])
        .reshape(n_set, 3, r_dp, c_t)
        .transpose(1, 0, 2, 3)
    )
    return (
        output,
        grad_input,
        sum_down_qkv,
        sum_up_qkv,
        sum_down_out,
        sum_up_out,
        sum_down_fc1,
        sum_up_fc1,
        sum_down_fc2,
        sum_up_fc2,
    )


def solution(mesh):
    both = ("dp", "tensor")
    in_specs = (
        P(both, None),
        P(both, None),
        P("dp", None),
        P("dp"),
        P(None, "dp", "tensor"),
        P("tensor", "dp"),
        P("dp", "tensor"),
        P("tensor", "dp"),
        P("dp"),
        P("dp"),
        P("dp"),
        P("dp"),
        P(None, None, "dp", None),
        P(None, None, "dp", "tensor"),
        P(None, "tensor", "dp"),
        P(None, None, "dp"),
        P(None, "dp", None),
        P(None, "dp", "tensor"),
        P(None, "tensor", "dp"),
        P(None, None, "dp"),
    )
    out_specs = (
        P(both, None),
        P(both, None),
        P(None, None, both, None),
        P(None, None, "dp", "tensor"),
        P(None, "tensor", "dp"),
        P(None, None, both),
        P(None, both, None),
        P(None, "dp", "tensor"),
        P(None, "tensor", "dp"),
        P(None, None, both),
    )
    return jax.shard_map(shards, mesh=mesh, in_specs=in_specs, out_specs=out_specs, check_vma=False)
```

```python
import functools

import jax
import jax.numpy as jnp
from jax import lax
from jax.experimental import pallas as pl
from jax.experimental.pallas import tpu as pltpu
from jax.sharding import PartitionSpec as P

HD = 64
EPS = 1e-05
NEG = -1000000000.0
LOG2E = 1.4426950408889634
BF = jnp.bfloat16
F32 = jnp.float32
VMEM_LIMIT = 60 * 2**20
BRIEF = pl.CostEstimate(flops=1, bytes_accessed=1, transcendentals=0)


def mm(left, right):
    return jnp.dot(left, right, preferred_element_type=F32)


def mm_nt(left, right):
    return lax.dot_general(left, right, (((1,), (1,)), ((), ())), preferred_element_type=F32)


def transpose_small(value):
    return value.astype(F32).T.astype(BF)


def token_place(index, rows, cuts, mine):
    shift = rows.bit_length() - 1
    bits = cuts.bit_length() - 1
    block = index >> shift
    reverse = jnp.zeros_like(block)
    for i in range(bits):
        reverse = reverse | (((block >> i) & 1) << (bits - 1 - i))
    return ((reverse ^ mine) << shift) | (index & (rows - 1))


def attend_forward_kernel(
    heads, block, chunk, rows, first, kept, cut_range, lengths_ref, q_ref, k_ref, v_ref, *rest
):
    length = k_ref.shape[0]
    cuts = length // rows
    rest = rest[kept:]
    att_ref, e_ref, l_ref = rest[0:3]
    cut_refs = rest[3 : 3 + len(cut_range)]
    keys_wide, values_t, scores = rest[3 + len(cut_range) :]
    mine = lax.axis_index("tensor")
    step = pl.program_id(0) + first
    ends = [lengths_ref[0, 0]]
    for d in range(1, lengths_ref.shape[1]):
        ends.append(ends[-1] + lengths_ref[0, d])

    @pl.when(step == first)
    def _():
        lane = lax.broadcasted_iota(jnp.int32, (1, 128), 1)
        begin = jnp.zeros_like(lane)
        end = jnp.zeros_like(lane)
        for d in range(len(ends)):
            begin = jnp.where(lane == d, ends[d - 1] if d else 0, begin)
            end = jnp.where(lane == d, ends[d], end)
        place = token_place(
            lax.broadcasted_iota(jnp.int32, (length, 128), 0), rows, cuts, mine
        )
        onehot = jnp.where((place >= begin) & (place < end), 1.0, 0.0).astype(BF)
        ones = (lax.broadcasted_iota(jnp.int32, (16, length), 0) == 0).astype(BF)
        flipped = v_ref[...].T
        for h in range(heads):
            key = k_ref[:, h * HD : (h + 1) * HD]
            keys_wide[h, :, 0:HD] = key
            keys_wide[h, :, HD : 2 * HD] = key
            keys_wide[h, :, 2 * HD :] = onehot
            values_t[h, 0:HD, :] = flipped[h * HD : (h + 1) * HD, :]
            values_t[h, HD:, :] = ones

    flipped_q = q_ref[...].astype(F32).T * (HD ** (-0.5) * LOG2E)
    place = token_place(
        lax.broadcasted_iota(jnp.int32, (1, block), 1) + step * block, rows, cuts, mine
    )
    segment = jnp.zeros_like(place)
    for end in ends:
        segment = segment + (place >= end).astype(jnp.int32)
    mask = jnp.where(
        lax.broadcasted_iota(jnp.int32, (128, block), 0) == segment, 0.0, NEG
    ).astype(BF)
    mixed = []
    for h in range(heads):
        query = flipped_q[h * HD : (h + 1) * HD, :]
        high = query.astype(BF)
        low = (query - high.astype(F32)).astype(BF)
        right = jnp.concatenate([high, low, mask], axis=0)
        top = None
        for c in range(length // chunk):
            part = mm(keys_wide[h, c * chunk : (c + 1) * chunk, :], right)
            scores[h, c * chunk : (c + 1) * chunk, :] = part
            part = jnp.max(part.reshape(chunk // 8, 8, block), axis=0)
            top = part if top is None else jnp.maximum(top, part)
        top = jnp.max(top, axis=0, keepdims=True)
        total = None
        for c in range(length // chunk):
            e = jnp.exp2(scores[h, c * chunk : (c + 1) * chunk, :] - top).astype(BF)
            e_ref[h, 0, c * chunk : (c + 1) * chunk, :] = e
            part = mm(values_t[h, :, c * chunk : (c + 1) * chunk], e)
            total = part if total is None else total + part
        row_sum = total[HD : HD + 1, :]
        l_ref[h, 0] = jnp.broadcast_to(row_sum, (8, block))
        mixed.append(total[0:HD, :] / row_sum)
    att = jnp.concatenate(mixed, axis=0).T.astype(BF)
    att_ref[...] = att
    for i, k in enumerate(cut_range):

        @pl.when(step == k * rows // block)
        def _():
            begin = k * rows % block
            cut_refs[i][...] = att[begin : begin + rows, :]


def attend_forward(q, k, v, lengths, group, heads, rows, part, parts, kept):
    length = q.shape[0]
    width = heads * HD
    block = min(512, length)
    chunk = min(512, length)
    count = length // block
    steps = count // parts
    first = part * steps
    per_part = steps * block // rows
    cut_range = range(part * per_part, (part + 1) * per_part)
    own_specs = [
        pl.BlockSpec((block, width), lambda i: (i + first, 0)),
        pl.BlockSpec((heads, 1, length, block), lambda i: (0, i + first, 0, 0)),
        pl.BlockSpec((heads, 1, 8, block), lambda i: (0, i + first, 0, 0)),
    ]
    return pl.pallas_call(
        functools.partial(
            attend_forward_kernel, heads, block, chunk, rows, first, len(kept), cut_range
        ),
        grid=(steps,),
        in_specs=[
            pl.BlockSpec(memory_space=pltpu.SMEM),
            pl.BlockSpec((block, width), lambda i: (i + first, group)),
            pl.BlockSpec((length, width), lambda i: (0, group)),
            pl.BlockSpec((length, width), lambda i: (0, group)),
        ]
        + [pl.BlockSpec(memory_space=pl.ANY)] * len(kept),
        out_specs=own_specs + [pl.BlockSpec((rows, width), lambda i: (0, 0))] * per_part,
        out_shape=[
            jax.ShapeDtypeStruct((length, width), BF),
            jax.ShapeDtypeStruct((heads, count, length, block), BF),
            jax.ShapeDtypeStruct((heads, count, 8, block), F32),
        ]
        + [jax.ShapeDtypeStruct((rows, width), BF)] * per_part,
        scratch_shapes=[
            pltpu.VMEM((heads, length, 256), BF),
            pltpu.VMEM((heads, HD + 16, length), BF),
            pltpu.VMEM((heads, length, block), F32),
        ],
        input_output_aliases={4 + i: i for i in range(len(kept))},
        compiler_params=pltpu.CompilerParams(
            vmem_limit_bytes=VMEM_LIMIT, dimension_semantics=("arbitrary",)
        ),
        cost_estimate=BRIEF,
        name="attend_forward",
    )(lengths, q, k, v, *kept)


def attend_backward_kernel(
    heads, block, chunk, cuts, q_ref, k_ref, v_ref, o_ref, e_ref, l_ref, *rest
):
    cut_refs = rest[0:cuts]
    dq_ref, dk_ref, dv_ref, do_rows_ref, values_wide, keys_t, dk_sum, dv_sum = rest[cuts:]
    length = k_ref.shape[0]
    rows = length // cuts
    width = heads * HD
    i = pl.program_id(0)
    for k in range(cuts):

        @pl.when(i == k * rows // block)
        def _():
            begin = k * rows % block
            do_rows_ref[begin : begin + rows, :] = cut_refs[k][...]

    @pl.when(i == 0)
    def _():
        ones = (lax.broadcasted_iota(jnp.int32, (length, 128), 1) < 2).astype(BF)
        for h in range(heads):
            value = v_ref[:, h * HD : (h + 1) * HD]
            values_wide[h, :, 0:HD] = value
            values_wide[h, :, HD : 2 * HD] = value
            values_wide[h, :, 2 * HD :] = ones
        keys_t[...] = k_ref[...].T
        dk_sum[...] = jnp.zeros_like(dk_sum)
        dv_sum[...] = jnp.zeros_like(dv_sum)

    q = q_ref[...]
    flipped_do = do_rows_ref[...].astype(F32).T
    flipped_o = o_ref[...].astype(F32).T
    lane = lax.broadcasted_iota(jnp.int32, (block, width), 1)
    row = lax.broadcasted_iota(jnp.int32, (128, block), 0)
    grads = []
    for h in range(heads):
        own = slice(h * HD, (h + 1) * HD)
        inverse = 1.0 / l_ref[h, 0, 0:1, :]
        dot = -jnp.sum(flipped_do[own] * flipped_o[own], axis=0, keepdims=True) * inverse
        scaled = flipped_do[own] * inverse
        high = scaled.astype(BF)
        low = (scaled - high.astype(F32)).astype(BF)
        dot_high = dot.astype(BF)
        dot_low = (dot - dot_high.astype(F32)).astype(BF)
        dots = jnp.where(row == 0, dot_high, jnp.where(row == 1, dot_low, jnp.zeros_like(dot_low)))
        right = jnp.concatenate([high, low, dots], axis=0)
        do_rows = high.T
        if heads == 2:
            empty = jnp.zeros_like(do_rows)
            do_rows = jnp.concatenate([do_rows, empty] if h == 0 else [empty, do_rows], axis=1)
        query = jnp.where((lane >= h * HD) & (lane < (h + 1) * HD), q, jnp.zeros_like(q))
        total = None
        for c in range(length // chunk):
            rows = slice(c * chunk, (c + 1) * chunk)
            e = e_ref[h, 0, rows, :]
            part = mm(values_wide[h, rows, :], right)
            ds = (e.astype(F32) * part).astype(BF)
            dv_sum[rows, :] += mm(e, do_rows)
            dk_sum[rows, :] += mm(ds, query)
            part = mm(keys_t[own, rows], ds)
            total = part if total is None else total + part
        grads.append(total * HD ** (-0.5))
    dq_ref[...] = jnp.concatenate(grads, axis=0).T.astype(BF)

    @pl.when(i == pl.num_programs(0) - 1)
    def _():
        dk_ref[...] = (dk_sum[...] * HD ** (-0.5)).astype(BF)
        dv_ref[...] = dv_sum[...].astype(BF)


def attend_backward(q, k, v, att, d_att, e, row_sum, group, heads):
    length = q.shape[0]
    width = heads * HD
    block = e.shape[3]
    cuts = len(d_att)
    rows = length // cuts
    chunk = min(512, length)
    count = length // block
    whole = pl.BlockSpec((length, width), lambda i: (0, group))
    return pl.pallas_call(
        functools.partial(attend_backward_kernel, heads, block, chunk, cuts),
        grid=(count,),
        in_specs=[
            pl.BlockSpec((block, width), lambda i: (i, group)),
            whole,
            whole,
            pl.BlockSpec((block, width), lambda i: (i, 0)),
            pl.BlockSpec((heads, 1, length, block), lambda i: (0, i, 0, 0)),
            pl.BlockSpec((heads, 1, 8, block), lambda i: (0, i, 0, 0)),
        ]
        + [pl.BlockSpec((rows, width), lambda i: (0, group))] * cuts,
        out_specs=[
            pl.BlockSpec((block, width), lambda i: (i, 0)),
            pl.BlockSpec((length, width), lambda i: (0, 0)),
            pl.BlockSpec((length, width), lambda i: (0, 0)),
        ],
        out_shape=[jax.ShapeDtypeStruct((length, width), BF)] * 3,
        scratch_shapes=[
            pltpu.VMEM((block, width), BF),
            pltpu.VMEM((heads, length, 256), BF),
            pltpu.VMEM((width, length), BF),
            pltpu.VMEM((length, width), F32),
            pltpu.VMEM((length, width), F32),
        ],
        compiler_params=pltpu.CompilerParams(
            vmem_limit_bytes=VMEM_LIMIT, dimension_semantics=("arbitrary",)
        ),
        cost_estimate=BRIEF,
        name="attend_backward",
    )(q, k, v, att, e, row_sum, *d_att)


def normal_parts(z):
    density = jnp.exp2(z * z * (-0.5 * LOG2E))
    t = 1.0 / (1.0 + (0.3275911 * 0.5**0.5) * jnp.abs(z))
    poly = t * (
        0.254829592 * 0.5
        + t
        * (
            -0.284496736 * 0.5
            + t * (1.421413741 * 0.5 + t * (-1.453152027 * 0.5 + t * (1.061405429 * 0.5)))
        )
    )
    tail = poly * density
    return jnp.where(z < 0.0, tail, 1.0 - tail), density * 0.3989422804014327


def normalize(values):
    center = values - jnp.mean(values, axis=-1, keepdims=True)
    scale = lax.rsqrt(jnp.mean(center * center, axis=-1, keepdims=True) + EPS)
    return center * scale, scale


def normalize_back(e, normal, scale):
    return scale * (
        e
        - jnp.mean(e, axis=-1, keepdims=True)
        - normal * jnp.mean(e * normal, axis=-1, keepdims=True)
    )


def assemble_kernel(rank, share, sets, down_ref, up_ref):
    ranks = 3 * rank
    count, tail = sets.shape[0], sets.shape[1] - ranks
    for k in range(count):
        down_ref[:, k * 128 : (k + 1) * 128] = sets[k, 0:ranks, :]
    row = lax.broadcasted_iota(jnp.int32, (ranks, tail), 0)
    source = lax.broadcasted_iota(jnp.int32, (ranks, tail), 1)
    for j in range(3):
        for half in range(2):
            total = None
            for k in range(count):
                wanted = row < 0
                for r in range(share):
                    target = j * rank + k * share + r
                    wanted = wanted | (
                        (row == target) & (source == (j * share + r) * 2 + half)
                    )
                part = mm(jnp.where(wanted, 1.0, 0.0).astype(BF), sets[k, ranks:, :])
                total = part if total is None else total + part
            begin = (j * 2 + half) * 128
            up_ref[:, begin : begin + 128] = total.astype(BF)


def assemble(sets, rank, share):
    count = sets.shape[0]
    vmem = pl.BlockSpec(memory_space=pltpu.VMEM)
    return pl.pallas_call(
        functools.partial(assemble_kernel, rank, share),
        in_specs=[vmem],
        out_specs=[vmem] * 2,
        out_shape=[
            jax.ShapeDtypeStruct((3 * rank, count * 128), BF),
            jax.ShapeDtypeStruct((3 * rank, 6 * 128), BF),
        ],
        name="assemble",
    )(sets)


def place_rows(source, j, height, target, row, sem):
    return pltpu.make_async_copy(
        source.at[j * height : (j + 1) * height, :],
        target.at[pl.ds(row * height, height), :],
        sem,
    )


def ring_rows():
    n_dp = lax.axis_size("dp")
    mine = lax.axis_index("dp")
    found = []
    for d in (mine, mine ^ 1):
        found += [(d + n_dp - 2 * j) % n_dp for j in range(n_dp // 2)]
    return found


def project_kernel(parts, counts, height, down_ref, up_ref, *rest):
    places = ring_rows() if len(counts) > 1 else [0]
    x_hbm = rest[0:parts]
    w_hbm = rest[parts : parts + len(counts)]
    q_ref, k_ref, v_ref, u_ref, w_ref, x, x_sem, w_sem = rest[parts + len(counts) :]
    block = 0
    for i, count in enumerate(counts):
        for j in range(count):
            place_rows(w_hbm[i], j, height, w_ref, places[block], w_sem).start()
            block += 1
    copies = []
    begin = 0
    for i in range(parts):
        rows = x_hbm[i].shape[0]
        copies.append(pltpu.make_async_copy(x_hbm[i], x.at[begin : begin + rows], x_sem.at[i]))
        copies[-1].start()
        begin += rows
    pltpu.make_async_copy(w_ref, w_ref, w_sem).wait()
    begin = 0
    width = q_ref.shape[1]
    for i in range(parts):
        rows = x_hbm[i].shape[0]
        copies[i].wait()
        step = min(512, rows)
        for r in range(begin, begin + rows, step):
            here = x[r : r + step, :]
            u = mm_nt(here, down_ref[...]).astype(BF)
            u_ref[r : r + step, :] = u
            for j, out in enumerate((q_ref, k_ref, v_ref)):
                cols = slice(j * width, (j + 1) * width)
                out[r : r + step, :] = (mm(here, w_ref[:, cols]) + mm(u, up_ref[:, cols])).astype(BF)
        begin += rows


def project(height, down, up, xs, ws):
    model = xs[0].shape[1]
    length = sum(x.shape[0] for x in xs)
    width = up.shape[1] // 3
    counts = [w.shape[0] // height for w in ws]
    vmem = pl.BlockSpec(memory_space=pltpu.VMEM)
    return pl.pallas_call(
        functools.partial(project_kernel, len(xs), counts, height),
        in_specs=[vmem, vmem] + [pl.BlockSpec(memory_space=pl.ANY)] * (len(xs) + len(ws)),
        out_specs=[vmem] * 5,
        out_shape=[jax.ShapeDtypeStruct((length, width), BF)] * 3
        + [
            jax.ShapeDtypeStruct((length, down.shape[0]), BF),
            jax.ShapeDtypeStruct((model, 3 * width), BF),
        ],
        scratch_shapes=[
            pltpu.VMEM((length, model), BF),
            pltpu.SemaphoreType.DMA((len(xs),)),
            pltpu.SemaphoreType.DMA,
        ],
        compiler_params=pltpu.CompilerParams(vmem_limit_bytes=VMEM_LIMIT),
        cost_estimate=BRIEF,
        name="project",
    )(down, up, *xs, *ws)


def unproject_kernel(
    parts, groups, u_ref, w_ref, down_ref, up_ref, *rest
):
    x_refs = rest[0:parts]
    grads = rest[parts : parts + 3 * groups]
    out_ref, g_up_ref, g_down_ref = rest[parts + 3 * groups :]
    width = w_ref.shape[1] // 3
    total = None
    g_down = None
    g_up = [None] * 3
    begin = 0
    for i in range(parts):
        rows = x_refs[i].shape[0]
        here = slice(begin, begin + rows)
        values = [
            jnp.concatenate([grads[g * 3 + j][here, :] for g in range(groups)], axis=1)
            for j in range(3)
        ]
        d_u = None
        for j in range(3):
            cols = slice(j * width, (j + 1) * width)
            part = mm_nt(values[j], up_ref[:, cols])
            d_u = part if d_u is None else d_u + part
        d_u = d_u.astype(BF)
        total = mm(d_u, down_ref[...])
        for j in range(3):
            total = total + mm_nt(values[j], w_ref[:, j * width : (j + 1) * width])
        out_ref[here, :] = total.astype(out_ref.dtype)
        part = mm(transpose_small(d_u), x_refs[i][...])
        g_down = part if g_down is None else g_down + part
        u_t = transpose_small(u_ref[here, :])
        for j in range(3):
            part = mm(u_t, values[j])
            g_up[j] = part if g_up[j] is None else g_up[j] + part
        begin += rows
    g_down_ref[...] = g_down
    for j in range(3):
        g_up_ref[:, j * width : (j + 1) * width] = g_up[j]


def unproject(grads, u, w, down, up, xs, half, halves, dtype):
    length = u.shape[0]
    model = w.shape[0]
    width = w.shape[1] // 3
    rows = length // halves
    ranks = down.shape[0]
    grads = [value for group in grads for value in group]
    vmem = pl.BlockSpec(memory_space=pltpu.VMEM)
    return pl.pallas_call(
        functools.partial(unproject_kernel, len(xs), len(grads) // 3),
        grid=(1,),
        in_specs=[pl.BlockSpec((rows, ranks), lambda i: (half, 0))]
        + [vmem] * (3 + len(xs))
        + [pl.BlockSpec((rows, g.shape[1]), lambda i: (half, 0)) for g in grads],
        out_specs=[vmem] * 3,
        out_shape=[
            jax.ShapeDtypeStruct((rows, model), dtype),
            jax.ShapeDtypeStruct((ranks, 3 * width), F32),
            jax.ShapeDtypeStruct((ranks, model), F32),
        ],
        compiler_params=pltpu.CompilerParams(vmem_limit_bytes=VMEM_LIMIT),
        cost_estimate=BRIEF,
        name="unproject",
    )(u, w, down, up, *xs, *grads)


def middle_kernel(
    cuts, parts, counts, counts2, sizes, hidden_block, x_ref, cot_ref,
    down_out, up_out, down_fc1, up_fc1, down_fc2, up_fc2, gain1, bias1, gain2, bias2, *rest
):
    att_hbm = rest[0:parts]
    rest = rest[parts:]
    first_hbm = rest[0 : len(counts)]
    rest = rest[len(counts) :]
    second_hbm = rest[0 : len(counts2)]
    rest = rest[len(counts2) :]
    out_ref, dy1_ref = rest[0:2]
    d_att_refs = rest[2 : 2 + cuts]
    (
        g_up_fc2, g_down_fc2, g_up_fc1, g_down_fc1, g_up_out, g_down_out,
        att_own, wo_t, w1, w2_t, hidden, slope, normal1, normed, low_rows, total,
        att_sem, wo_sem, w1_sem, w2_sem,
    ) = rest[2 + cuts :]
    rows, model = x_ref.shape
    units = w1.shape[1]
    height, wide, narrow = sizes
    mine = lax.axis_index("tensor")
    n_t = lax.axis_size("tensor")
    order = cut_order(n_t)
    places = spread_places() if sum(counts) > 1 else [(0, 0)]
    places2 = places

    def fetch(source, j, begin, width, target, row, col, sem):
        pltpu.make_async_copy(
            source.at[j * height : (j + 1) * height, begin : begin + width],
            target.at[
                pl.ds(pl.multiple_of(row * height, height), height),
                pl.ds(pl.multiple_of(col * width, width), width),
            ],
            sem,
        ).start()

    def each_block(counts, places):
        block = 0
        for i, count in enumerate(counts):
            for j in range(count):
                yield (i, j) + places[block]
                block += 1

    if parts > 1:
        width = att_hbm[0].shape[1]
        groups = parts // n_t
        for k in range(n_t):
            for g in range(groups):
                col = pl.multiple_of(((mine ^ order[k]) * groups + g) * width, width)
                pltpu.make_async_copy(
                    att_hbm[k * groups + g], att_own.at[:, pl.ds(col, width)], att_sem
                ).start()
    else:
        pltpu.make_async_copy(att_hbm[0], att_own, att_sem).start()
    for i, j, row, col in each_block(counts, places):
        fetch(first_hbm[i], j, wide, narrow, wo_t, row, col, wo_sem)
    for i, j, row, col in each_block(counts, places):
        fetch(first_hbm[i], j, 0, wide, w1, row, col, w1_sem.at[col])
    for i, j, row, col in each_block(counts2, places2):
        fetch(second_hbm[i], j, 0, wide, w2_t, row, col, w2_sem.at[col])

    pltpu.make_async_copy(att_own, att_own, att_sem).wait()
    pltpu.make_async_copy(wo_t, wo_t, wo_sem).wait()
    att = att_own[...]
    u_out = mm_nt(att, down_out[...]).astype(BF)
    first = x_ref[...].astype(F32) + mm_nt(att, wo_t[...]) + mm(u_out, up_out[...])
    normal, scale1 = normalize(first)
    normal1[...] = normal
    full = normal * gain1[...].astype(F32) + bias1[...].astype(F32)
    normed[...] = full
    low_rows[...] = full.astype(BF)
    u_fc1 = mm_nt(low_rows[...], down_fc1[...]).astype(BF)

    blocks = units // hidden_block
    per_cut = wide // hidden_block

    def before(i):
        cols = slice(i * hidden_block, (i + 1) * hidden_block)
        if i % per_cut == 0:
            b = i // per_cut
            for target, sem in ((w1, w1_sem), (w2_t, w2_sem)):
                view = target.at[:, b * wide : (b + 1) * wide]
                pltpu.make_async_copy(view, view, sem.at[b]).wait()
        return mm(low_rows[...], w1[:, cols]) + mm(u_fc1, up_fc1[:, cols])

    z = before(0)
    u_sum = None
    for i in range(blocks):
        cols = slice(i * hidden_block, (i + 1) * hidden_block)
        following = before(i + 1) if i + 1 < blocks else None
        phi_sum, phi = normal_parts(z)
        act = (z * phi_sum).astype(BF)
        hidden[:, cols] = act
        slope[:, cols] = phi_sum + z * phi
        part = mm_nt(act, w2_t[:, cols])
        total[...] = part if i == 0 else total[...] + part
        part = mm_nt(act, down_fc2[:, cols])
        u_sum = part if u_sum is None else u_sum + part
        z = following
    u_fc2 = u_sum.astype(BF)
    second = normed[...] + total[...] + mm(u_fc2, up_fc2[...])
    normal2, scale2 = normalize(second)
    gain = gain2[...].astype(F32)
    out_ref[...] = (normal2 * gain + bias2[...].astype(F32)).astype(BF)
    d_second = normalize_back(cot_ref[...].astype(F32) * gain, normal2, scale2)
    total[...] = d_second
    d_ffn = d_second.astype(BF)
    d_u2 = mm_nt(d_ffn, up_fc2[...]).astype(BF)
    d_u2_t = transpose_small(d_u2)
    g_up_fc2[...] = mm(transpose_small(u_fc2), d_ffn).astype(BF)
    u_fc1_t = transpose_small(u_fc1)

    def before_back(i):
        cols = slice(i * hidden_block, (i + 1) * hidden_block)
        return mm(d_ffn, w2_t[:, cols]) + mm(d_u2, down_fc2[:, cols])

    d_hidden = before_back(0)
    u_sum = None
    for i in range(blocks):
        cols = slice(i * hidden_block, (i + 1) * hidden_block)
        following = before_back(i + 1) if i + 1 < blocks else None
        d_pre = (d_hidden * slope[:, cols]).astype(BF)
        g_down_fc2[:, cols] = mm(d_u2_t, hidden[:, cols]).astype(BF)
        g_up_fc1[:, cols] = mm(u_fc1_t, d_pre).astype(BF)
        total[...] += mm_nt(d_pre, w1[:, cols])
        part = mm_nt(d_pre, up_fc1[:, cols])
        u_sum = part if u_sum is None else u_sum + part
        d_hidden = following
    d_u1 = u_sum.astype(BF)
    d_normed = total[...] + mm(d_u1, down_fc1[...])
    g_down_fc1[...] = mm(transpose_small(d_u1), low_rows[...]).astype(BF)
    d_first = normalize_back(d_normed * gain1[...].astype(F32), normal1[...], scale1)
    dy1_ref[...] = d_first
    d_a = d_first.astype(BF)
    d_uo = mm_nt(d_a, up_out[...]).astype(BF)
    g_up_out[...] = mm(transpose_small(u_out), d_a).astype(BF)
    g_down_out[...] = mm(transpose_small(d_uo), att).astype(BF)
    att_own[...] = (mm(d_a, wo_t[...]) + mm(d_uo, down_out[...])).astype(BF)
    width = model // cuts
    for k in range(cuts):
        col = pl.multiple_of((mine ^ order[k]) * width, width) if cuts > 1 else 0
        d_att_refs[k][...] = att_own[:, pl.ds(col, width)]


def cut_order(n_t):
    order = [0]
    bit = n_t // 2
    while bit:
        order = order + [k ^ bit for k in order]
        bit //= 2
    return order


def middle(atts, cuts, x, cot, adapters, norms, firsts, seconds, sizes):
    rows, model = x.shape
    rank, units = adapters[3].shape
    height, wide, narrow = sizes
    counts = [f.shape[0] // height for f in firsts]
    counts2 = [f.shape[0] // height for f in seconds]
    hidden_block = min(512, wide)
    cols = units // wide
    vmem = pl.BlockSpec(memory_space=pltpu.VMEM)
    anywhere = pl.BlockSpec(memory_space=pl.ANY)
    long = jax.ShapeDtypeStruct((rank, units), BF)
    short = jax.ShapeDtypeStruct((rank, model), BF)
    out_shape = (
        [jax.ShapeDtypeStruct((rows, model), BF), jax.ShapeDtypeStruct((rows, model), F32)]
        + [jax.ShapeDtypeStruct((rows, model // cuts), BF)] * cuts
        + [short, long, long, short, short, short]
    )
    return pl.pallas_call(
        functools.partial(
            middle_kernel, cuts, len(atts), counts, counts2, sizes, hidden_block
        ),
        in_specs=[vmem] * 12 + [anywhere] * (len(atts) + len(firsts) + len(seconds)),
        out_specs=[vmem] * len(out_shape),
        out_shape=out_shape,
        scratch_shapes=[
            pltpu.VMEM((rows, model), BF),
            pltpu.VMEM((model, model), BF),
            pltpu.VMEM((model, units), BF),
            pltpu.VMEM((model, units), BF),
            pltpu.VMEM((rows, units), BF),
            pltpu.VMEM((rows, units), F32),
            pltpu.VMEM((rows, model), F32),
            pltpu.VMEM((rows, model), F32),
            pltpu.VMEM((rows, model), BF),
            pltpu.VMEM((rows, model), F32),
            pltpu.SemaphoreType.DMA,
            pltpu.SemaphoreType.DMA,
            pltpu.SemaphoreType.DMA((cols,)),
            pltpu.SemaphoreType.DMA((cols,)),
        ],
        compiler_params=pltpu.CompilerParams(vmem_limit_bytes=VMEM_LIMIT),
        cost_estimate=BRIEF,
        name="middle",
    )(x, cot, *adapters, *norms, *atts, *firsts, *seconds)


class Spread:
    def __init__(self):
        self.n_dp, self.n_t = lax.axis_size("dp"), lax.axis_size("tensor")
        self.devices = [(d, t) for d in range(self.n_dp) for t in range(self.n_t)]

    def send(self, value, target):
        n_t = self.n_t
        pairs = []
        for d, t in self.devices:
            to_d, to_t = target(d, t)
            pairs.append((d * n_t + t, to_d * n_t + to_t))
        return lax.ppermute(value, ("dp", "tensor"), pairs)

    def along_z(self, value):
        count = self.n_dp // 2
        return [value] + [
            self.send(value, lambda d, t, j=j: ((d + 2 * j) % self.n_dp, t))
            for j in range(1, count)
        ]

    def cross(self, value, core):
        return self.send(value, lambda d, t: (d ^ 1, t) if t % 2 == core else (d, t ^ 2))

    def core(self, value):
        return self.send(value, lambda d, t: (d, t ^ 1))


def spread_places():
    n_dp = lax.axis_size("dp")
    d = lax.axis_index("dp")
    mine = lax.axis_index("tensor")
    found = []
    for t in (mine, mine ^ 1):
        even = (t % 2) == 0
        for to_d, to_t in (
            (d, t),
            (jnp.where(even, d ^ 1, d), jnp.where(even, t, t ^ 2)),
            (jnp.where(even, d, d ^ 1), jnp.where(even, t ^ 2, t)),
            (d ^ 1, t ^ 2),
        ):
            found += [((to_d + n_dp - 2 * j) % n_dp, to_t) for j in range(n_dp // 2)]
    return found


def shards(
    inputs, cotangent, lengths, adapter_index, w_qkv, w_out, w_fc1, w_fc2,
    ln1_gain, ln1_bias, ln2_gain, ln2_bias, down_qkv, up_qkv, down_out, up_out,
    down_fc1, up_fc1, down_fc2, up_fc2,
):
    n_dp = lax.axis_size("dp")
    n_t = lax.axis_size("tensor")
    every = ("dp", "tensor")
    mine = lax.axis_index("tensor")
    rows, model = inputs.shape
    length = rows * n_t
    n_set = down_qkv.shape[1]
    rank = down_qkv.shape[3]
    r_dp = rank // n_dp
    r_t = rank // n_t
    d_dp = model // n_dp
    c_t = model // n_t
    f_t = w_fc1.shape[1]
    f_all = f_t * n_t

    def swap(value, bit):
        return lax.ppermute(value, "tensor", [(i, i ^ bit) for i in range(n_t)])

    bits = []
    bit = n_t // 2
    while bit:
        bits.append(bit)
        bit //= 2
    order = cut_order(n_t)

    x_parts = [inputs]
    for bit in bits[:-1]:
        x_parts = x_parts + [swap(part, bit) for part in x_parts]

    w_local = w_qkv.transpose(1, 0, 2).reshape(d_dp, 3 * c_t)
    packed = jnp.concatenate([w_fc1, w_out.T], axis=1)
    packed_second = w_fc2.T
    mine_dp = lax.axis_index("dp")
    if (n_dp, n_t) == (8, 4):
        spread = Spread()
        w_parts = spread.along_z(w_local)
        w_height = d_dp
        block_sizes = (d_dp, f_t, c_t)
    else:
        w_parts = [lax.all_gather(w_local, "dp", axis=0, tiled=True)]
        w_height = model
        firsts = lax.all_gather(packed, every, axis=0).reshape(n_dp, n_t, d_dp, f_t + c_t)
        seconds = lax.all_gather(packed_second, every, axis=0).reshape(n_dp, n_t, d_dp, f_t)

        def whole(value):
            return value.transpose(0, 2, 1, 3).reshape(model, -1)

        firsts = [
            jnp.concatenate(
                [whole(firsts[..., :f_t]), whole(firsts[..., f_t:])], axis=1
            )
        ]
        seconds = [whole(seconds)]
        block_sizes = (model, f_all, model)

    index_all = lax.all_to_all(
        jnp.broadcast_to(adapter_index, (n_dp,)), "dp", 0, 0, tiled=True
    )
    onehot_all = (index_all[:, None] == jnp.arange(n_set, dtype=jnp.int32)[None, :]).astype(BF)
    down_t = down_qkv.transpose(1, 0, 3, 2).reshape(n_set, 3 * rank, d_dp)
    if n_dp * r_dp == rank and d_dp == 128 and c_t == 256:
        up_rows = up_qkv.transpose(1, 0, 2, 3).reshape(n_set, 6 * r_dp, 128)
        fill = jnp.zeros((n_set, -6 * r_dp % 16, 128), BF)
        table = jnp.concatenate([down_t, up_rows, fill], axis=1)
        sets = jnp.einsum("ns,srl->nrl", onehot_all, table, preferred_element_type=F32).astype(BF)
        w_parts, sets, packed = lax.optimization_barrier((w_parts, sets, packed))
        w_near = jnp.concatenate(w_parts, axis=0)
        w_parts = [w_near, lax.ppermute(w_near, "dp", [(i, i ^ 1) for i in range(n_dp)])]
        first = spread.along_z(packed)
        sets = lax.all_to_all(sets, "dp", 0, 0, tiled=True)
        w_parts, sets, x_parts = lax.optimization_barrier((w_parts, sets, x_parts))
        sel_down_qkv, sel_up_qkv = assemble(sets, rank, r_dp)
    else:
        table = jnp.concatenate(
            [down_t.reshape(n_set, -1), up_qkv.transpose(1, 0, 2, 3).reshape(n_set, -1)], axis=1
        )
        came = lax.all_to_all(mm(onehot_all, table).astype(BF), "dp", 0, 0, tiled=True)
        cut = 3 * rank * d_dp
        sel_down_qkv = (
            came[:, :cut].reshape(n_dp, 3 * rank, d_dp).transpose(1, 0, 2).reshape(3 * rank, model)
        )
        up_cols = came[:, cut:].reshape(n_dp, 3, r_dp, c_t).transpose(1, 0, 2, 3)
        same = jnp.eye(3, dtype=BF).reshape(3, 1, 3, 1)
        sel_up_qkv = (up_cols.reshape(3, rank, 1, c_t) * same).reshape(3 * rank, 3 * c_t)
    def part_of_rank(value, axis):
        return lax.dynamic_slice_in_dim(value, mine * r_t, r_t, axis)

    tables = [
        down_out.transpose(0, 2, 1),
        part_of_rank(up_out, 1),
        part_of_rank(down_fc1.transpose(0, 2, 1), 1),
        up_fc1,
        down_fc2.transpose(0, 2, 1),
        part_of_rank(up_fc2, 1),
    ]
    sizes = [t.size // n_set for t in tables]
    table = jnp.concatenate([t.reshape(n_set, -1) for t in tables], axis=1)
    chosen = mm(onehot_all, table).astype(BF)
    norm_part = jnp.stack([ln1_gain, ln1_bias, ln2_gain, ln2_bias]).reshape(1, -1)
    chosen = jnp.concatenate([chosen, jnp.broadcast_to(norm_part, (n_dp, norm_part.size))], axis=1)
    sent = jnp.broadcast_to(chosen[:, None, :], (n_dp, n_t, chosen.shape[1])).reshape(n_dp * n_t, -1)
    staged = n_dp == 8 and n_t == 4
    x_parts = x_parts + [swap(part, bits[-1]) for part in x_parts]
    if staged:
        x_parts, first, sent, packed_second = lax.optimization_barrier(
            (x_parts, first, sent, packed_second)
        )
        first = jnp.concatenate(first, axis=0)
        first_one = spread.cross(first, 0)
        first_two = spread.cross(first, 1)
        second = spread.along_z(packed_second)
    came = lax.all_to_all(sent, every, 0, 0, tiled=True)
    *qkv, u_in, w_cols = project(
        w_height, sel_down_qkv, sel_up_qkv, x_parts, w_parts
    )
    def make_adapters(came):
        came = came.reshape(n_dp, n_t, -1)
        pieces = []
        start = 0
        for size in sizes:
            pieces.append(came[:, :, start : start + size])
            start += size
        norms = came[:, 0, start:].reshape(n_dp, 4, d_dp).transpose(1, 0, 2).reshape(4, 1, model)

        def from_rank_parts(piece):
            return piece.reshape(n_dp, n_t, r_t, d_dp).transpose(1, 2, 0, 3).reshape(rank, model)

        def from_blocks(piece, width):
            return piece.reshape(n_dp, n_t, r_dp, width).transpose(0, 2, 1, 3).reshape(rank, n_t * width)

        adapters = [
            from_blocks(pieces[0], c_t),
            from_rank_parts(pieces[1]),
            from_rank_parts(pieces[2]),
            from_blocks(pieces[3], f_t),
            from_blocks(pieces[4], f_t),
            from_rank_parts(pieces[5]),
        ]
        return adapters, norms

    heads = c_t // HD
    group_heads = 2 if heads % 2 == 0 else 1
    groups = heads // group_heads
    kept = []
    att_parts = [[] for _ in range(n_t)]
    for g in range(groups):
        kept.append([])
        for part in range(2):
            if staged and (g, part) == (1, 0):
                qkv, kept, first_one, first_two, second, came = lax.optimization_barrier(
                    (qkv, kept, first_one, first_two, second, came)
                )
                first_both = spread.cross(first_one, 1)
                second = jnp.concatenate(second, axis=0)
                second_one = spread.cross(second, 0)
                second_two = spread.cross(second, 1)
            elif staged and (g, part) == (1, 1):
                qkv, kept, adapters, first_both = lax.optimization_barrier(
                    (qkv, kept, make_adapters(came), first_both)
                )
            att, e, row_sum, *cut_rows = attend_forward(
                *qkv, lengths, g, group_heads, rows, part, 2, kept[-1]
            )
            kept[-1] = [att, e, row_sum]
            for i, value in enumerate(cut_rows):
                k = part * len(cut_rows) + i
                att_parts[k].append(value if order[k] == 0 else swap(value, order[k]))
    atts = [part for parts in att_parts for part in parts]

    if staged:
        kept, second_one, second_two = lax.optimization_barrier((kept, second_one, second_two))
        seconds = [second, second_one, second_two, spread.cross(second_one, 1)]
        seconds += [spread.core(value) for value in seconds]
        firsts = [first, first_one, first_two, first_both]
        firsts += [spread.core(value) for value in firsts]
    else:
        adapters = make_adapters(came)
    adapters, norms = adapters
    blocks_fit = c_t % 128 == 0
    if not blocks_fit:
        by_cut = jnp.concatenate(atts, axis=1).reshape(rows, n_t, c_t)
        to_cut = jnp.array([order.index(k) for k in range(n_t)], jnp.int32)
        to_cut = to_cut[jnp.arange(n_t, dtype=jnp.int32) ^ mine]
        atts = [jnp.take(by_cut, to_cut, axis=1).reshape(rows, model)]
    cuts = n_t if blocks_fit else 1
    done = middle(
        atts, cuts, inputs, cotangent, adapters, list(norms), firsts, seconds, block_sizes
    )
    output, d_first = done[0:2]
    d_att_blocks = done[2 : 2 + cuts]
    if not blocks_fit:
        by_owner = d_att_blocks[0].reshape(rows, n_t, c_t)
        d_att_blocks = [
            lax.dynamic_index_in_dim(by_owner, mine ^ order[k], 1, keepdims=False)
            for k in range(n_t)
        ]
    g_up_fc2, g_down_fc2, g_up_fc1, g_down_fc1, g_up_out, g_down_out = done[2 + cuts :]

    def share_cols(value):
        lead = value.size // model
        return (
            value.reshape(lead, n_dp, n_t, model // (n_dp * n_t))
            .transpose(1, 2, 0, 3)
            .reshape(n_dp * n_t, -1)
        )

    def share_blocks(value):
        width = value.shape[1] // n_t
        return (
            value.reshape(n_dp, r_dp, n_t, width).transpose(0, 2, 1, 3).reshape(n_dp * n_t, -1)
        )

    def exchange(parts):
        widths = [p.shape[1] for p in parts]
        got = lax.all_to_all(jnp.concatenate(parts, axis=1), every, 0, 0, tiled=True)
        return got, widths

    early, early_widths = exchange(
        [
            share_blocks(g_down_out),
            share_cols(g_up_out),
            share_cols(g_down_fc1),
            share_blocks(g_up_fc1),
            share_blocks(g_down_fc2),
            share_cols(g_up_fc2),
        ]
    )

    d_att_all = [
        d_att_blocks[k] if order[k] == 0 else swap(d_att_blocks[k], order[k]) for k in range(n_t)
    ]
    grads = []
    for g in range(groups):
        if g == groups - 1:
            d_att_all, early = lax.optimization_barrier((d_att_all, early))
        grads.append(
            attend_backward(*qkv, kept[g][0], d_att_all, kept[g][1], kept[g][2], g, group_heads)
        )

    def partly(half, dtype):
        xs = x_parts[half * n_t // 2 : (half + 1) * n_t // 2]
        return unproject(grads, u_in, w_cols, sel_down_qkv, sel_up_qkv, xs, half, 2, dtype)

    other, g_up_other, g_down_other = partly(1, BF)
    parts, g_up_own, g_down_own = partly(0, F32)
    other = swap(other, bits[-1])
    span = length // 2
    for bit in reversed(bits[:-1]):
        half = span // 2
        sent = (parts[half:] + other[half:].astype(F32)).astype(BF)
        parts = parts[:half] + other[:half].astype(F32)
        other = swap(sent, bit)
        span = half
    grad_input = d_first + parts + other.astype(F32)

    g_down_qkv = (g_down_own + g_down_other).astype(BF)
    g_up_all = (g_up_own + g_up_other).astype(BF)
    g_up_qkv = jnp.stack(
        [
            g_up_all[j * rank : (j + 1) * rank, j * c_t : (j + 1) * c_t]
            for j in range(3)
        ]
    )
    up_share = (
        g_up_qkv.reshape(3, n_dp, r_dp, c_t).transpose(1, 0, 2, 3).reshape(n_dp, 1, -1)
    )
    up_share = jnp.broadcast_to(up_share, (n_dp, n_t, up_share.shape[2])).reshape(n_dp * n_t, -1)
    late, late_widths = exchange([share_cols(g_down_qkv), up_share])

    by_sender = jnp.broadcast_to(onehot_all[:, None, :], (n_dp, n_t, n_set)).reshape(-1, n_set)
    same_cols = (jnp.arange(n_dp * n_t, dtype=jnp.int32) % n_t == mine).astype(BF)

    tn = (((0,), (0,)), ((), ()))

    def total(got, weights):
        return lax.dot_general(weights, got, tn, preferred_element_type=F32)

    early_sum = total(early, by_sender)
    pieces = []
    start = 0
    for width in early_widths:
        pieces.append(early_sum[:, start : start + width])
        start += width
    d_all = model // (n_dp * n_t)
    sum_down_out = pieces[0].reshape(n_set, r_dp, c_t).transpose(0, 2, 1)
    sum_up_out = pieces[1].reshape(n_set, rank, d_all)
    sum_down_fc1 = pieces[2].reshape(n_set, rank, d_all).transpose(0, 2, 1)
    sum_up_fc1 = pieces[3].reshape(n_set, r_dp, f_t)
    sum_down_fc2 = pieces[4].reshape(n_set, r_dp, f_t).transpose(0, 2, 1)
    sum_up_fc2 = pieces[5].reshape(n_set, rank, d_all)
    sum_down_qkv = (
        total(late[:, : late_widths[0]], by_sender)
        .reshape(n_set, 3, rank, d_all)
        .transpose(1, 0, 3, 2)
    )
    sum_up_qkv = (
        total(late[:, late_widths[0] :], by_sender * same_cols[:, None])
        .reshape(n_set, 3, r_dp, c_t)
        .transpose(1, 0, 2, 3)
    )
    return (
        output,
        grad_input,
        sum_down_qkv,
        sum_up_qkv,
        sum_down_out,
        sum_up_out,
        sum_down_fc1,
        sum_up_fc1,
        sum_down_fc2,
        sum_up_fc2,
    )


def solution(mesh):
    both = ("dp", "tensor")
    in_specs = (
        P(both, None),
        P(both, None),
        P("dp", None),
        P("dp"),
        P(None, "dp", "tensor"),
        P("tensor", "dp"),
        P("dp", "tensor"),
        P("tensor", "dp"),
        P("dp"),
        P("dp"),
        P("dp"),
        P("dp"),
        P(None, None, "dp", None),
        P(None, None, "dp", "tensor"),
        P(None, "tensor", "dp"),
        P(None, None, "dp"),
        P(None, "dp", None),
        P(None, "dp", "tensor"),
        P(None, "tensor", "dp"),
        P(None, None, "dp"),
    )
    out_specs = (
        P(both, None),
        P(both, None),
        P(None, None, both, None),
        P(None, None, "dp", "tensor"),
        P(None, "tensor", "dp"),
        P(None, None, both),
        P(None, both, None),
        P(None, "dp", "tensor"),
        P(None, "tensor", "dp"),
        P(None, None, both),
    )
    return jax.shard_map(shards, mesh=mesh, in_specs=in_specs, out_specs=out_specs, check_vma=False)
```

```python
import functools

import jax
import jax.numpy as jnp
from jax import lax
from jax.experimental import pallas as pl
from jax.experimental.pallas import tpu as pltpu
from jax.sharding import PartitionSpec as P

HD = 64
EPS = 1e-05
NEG = -1000000000.0
LOG2E = 1.4426950408889634
BF = jnp.bfloat16
F32 = jnp.float32
VMEM_LIMIT = 60 * 2**20
BRIEF = pl.CostEstimate(flops=1, bytes_accessed=1, transcendentals=0)


def mm(left, right):
    return jnp.dot(left, right, preferred_element_type=F32)


def mm_nt(left, right):
    return lax.dot_general(left, right, (((1,), (1,)), ((), ())), preferred_element_type=F32)


def transpose_small(value):
    return value.astype(F32).T.astype(BF)


def token_place(index, rows, cuts, mine):
    shift = rows.bit_length() - 1
    bits = cuts.bit_length() - 1
    block = index >> shift
    reverse = jnp.zeros_like(block)
    for i in range(bits):
        reverse = reverse | (((block >> i) & 1) << (bits - 1 - i))
    return ((reverse ^ mine) << shift) | (index & (rows - 1))


def ring_owners():
    n_dp = lax.axis_size("dp")
    mine = lax.axis_index("dp")
    return [
        (d + n_dp - 2 * j) % n_dp for d in (mine, mine ^ 1) for j in range(n_dp // 2)
    ]


def attend_forward_kernel(
    heads, block, chunk, rows, group, cuts, parts, counts, lengths_ref, *rest
):
    projecting = parts > 0
    if projecting:
        down_ref, up_ref = rest[0:2]
        x_hbm = rest[2 : 2 + parts]
        w_hbm = rest[2 + parts : 2 + parts + len(counts)]
        rest = rest[2 + parts + len(counts) :]
    else:
        q_ref, k_ref, v_ref = rest[0:3]
        rest = rest[3:]
    att_ref, e_ref, l_ref = rest[0:3]
    cut_refs = rest[3 : 3 + cuts]
    rest = rest[3 + cuts :]
    if projecting:
        qkv_hbm, u_ref, w_out_hbm = rest[0:3], rest[3], rest[4]
        keys_wide, values_t, scores, x, w_ref, qkv, x_sem, w_sem, out_sem, w_out_sem = rest[5:]
    else:
        keys_wide, values_t, scores = rest
    length = keys_wide.shape[1]
    width = heads * HD
    mine = lax.axis_index("tensor")
    step = pl.program_id(0)
    steps = pl.num_programs(0)
    ends = [lengths_ref[0, 0]]
    for d in range(1, lengths_ref.shape[1]):
        ends.append(ends[-1] + lengths_ref[0, d])

    @pl.when(step == 0)
    def _():
        if projecting:
            owners = ring_owners() if len(counts) > 1 else [0]
            height = w_ref.shape[0] // sum(counts)
            for i, count in enumerate(counts):
                for j in range(count):
                    row = pl.multiple_of(owners[i * count + j] * height, height)
                    pltpu.make_async_copy(
                        w_hbm[i].at[j * height : (j + 1) * height, :],
                        w_ref.at[pl.ds(row, height), :],
                        w_sem,
                    ).start()
            copies = []
            begin = 0
            for i in range(parts):
                size = x_hbm[i].shape[0]
                copies.append(
                    pltpu.make_async_copy(x_hbm[i], x.at[begin : begin + size], x_sem.at[i])
                )
                copies[-1].start()
                begin += size
        lane = lax.broadcasted_iota(jnp.int32, (1, 128), 1)
        begin = jnp.zeros_like(lane)
        end = jnp.zeros_like(lane)
        for d in range(len(ends)):
            begin = jnp.where(lane == d, ends[d - 1] if d else 0, begin)
            end = jnp.where(lane == d, ends[d], end)
        place = token_place(
            lax.broadcasted_iota(jnp.int32, (length, 128), 0), rows, cuts, mine
        )
        onehot = jnp.where((place >= begin) & (place < end), 1.0, 0.0).astype(BF)
        for h in range(heads):
            keys_wide[h, :, 2 * HD :] = onehot
        if projecting:
            all_heads = qkv.shape[2]
            first = 0
            pltpu.make_async_copy(w_ref, w_ref, w_sem).wait()
            pltpu.make_async_copy(w_ref, w_out_hbm, w_out_sem).start()
            for i in range(parts):
                size = x_hbm[i].shape[0]
                copies[i].wait()
                step_rows = min(512, size)
                for r in range(first, first + size, step_rows):
                    here = x[r : r + step_rows, :]
                    u = mm_nt(here, down_ref[...]).astype(BF)
                    u_ref[r : r + step_rows, :] = u
                    for j in range(3):
                        cols = slice(j * all_heads, (j + 1) * all_heads)
                        qkv[j, r : r + step_rows, :] = (
                            mm(here, w_ref[:, cols]) + mm(u, up_ref[:, cols])
                        ).astype(BF)
                first += size
            for j in range(3):
                pltpu.make_async_copy(qkv.at[j], qkv_hbm[j], out_sem.at[j]).start()
        ones = (lax.broadcasted_iota(jnp.int32, (16, length), 0) == 0).astype(BF)
        values = qkv[2, :, group * width : (group + 1) * width] if projecting else v_ref[...]
        flipped = values.T
        for h in range(heads):
            own = slice(group * width + h * HD, group * width + (h + 1) * HD)
            key = qkv[1, :, own] if projecting else k_ref[:, h * HD : (h + 1) * HD]
            keys_wide[h, :, 0:HD] = key
            keys_wide[h, :, HD : 2 * HD] = key
            values_t[h, 0:HD, :] = flipped[h * HD : (h + 1) * HD, :]
            values_t[h, HD:, :] = ones

    if projecting:
        query_rows = qkv[0, pl.ds(pl.multiple_of(step * block, block), block), :]
        query_rows = query_rows[:, group * width : (group + 1) * width]
    else:
        query_rows = q_ref[...]
    flipped_q = query_rows.astype(F32).T * (HD ** (-0.5) * LOG2E)
    place = token_place(
        lax.broadcasted_iota(jnp.int32, (1, block), 1) + step * block, rows, cuts, mine
    )
    segment = jnp.zeros_like(place)
    for end in ends:
        segment = segment + (place >= end).astype(jnp.int32)
    mask = jnp.where(
        lax.broadcasted_iota(jnp.int32, (128, block), 0) == segment, 0.0, NEG
    ).astype(BF)
    mixed = []
    for h in range(heads):
        query = flipped_q[h * HD : (h + 1) * HD, :]
        high = query.astype(BF)
        low = (query - high.astype(F32)).astype(BF)
        right = jnp.concatenate([high, low, mask], axis=0)
        top = None
        for c in range(length // chunk):
            part = mm(keys_wide[h, c * chunk : (c + 1) * chunk, :], right)
            scores[h, c * chunk : (c + 1) * chunk, :] = part
            part = jnp.max(part.reshape(chunk // 8, 8, block), axis=0)
            top = part if top is None else jnp.maximum(top, part)
        top = jnp.max(top, axis=0, keepdims=True)
        total = None
        for c in range(length // chunk):
            e = jnp.exp2(scores[h, c * chunk : (c + 1) * chunk, :] - top).astype(BF)
            e_ref[h, 0, c * chunk : (c + 1) * chunk, :] = e
            part = mm(values_t[h, :, c * chunk : (c + 1) * chunk], e)
            total = part if total is None else total + part
        row_sum = total[HD : HD + 1, :]
        l_ref[h, 0] = jnp.broadcast_to(row_sum, (8, block))
        mixed.append(total[0:HD, :] / row_sum)
    att = jnp.concatenate(mixed, axis=0).T.astype(BF)
    att_ref[...] = att
    for k in range(cuts):

        @pl.when(step == k * rows // block)
        def _():
            begin = k * rows % block
            cut_refs[k][...] = att[begin : begin + rows, :]

    if projecting:

        @pl.when(step == steps - 1)
        def _():
            for j in range(3):
                pltpu.make_async_copy(qkv.at[j], qkv_hbm[j], out_sem.at[j]).wait()
            pltpu.make_async_copy(w_ref, w_out_hbm, w_out_sem).wait()


def attend_forward(lengths, group, heads, rows, cuts, qkv=None, source=None):
    length = rows * cuts
    width = heads * HD
    block = min(512, length)
    chunk = min(512, length)
    count = length // block
    vmem = pl.BlockSpec(memory_space=pltpu.VMEM)
    anywhere = pl.BlockSpec(memory_space=pl.ANY)
    in_specs = [pl.BlockSpec(memory_space=pltpu.SMEM)]
    out_specs = [
        pl.BlockSpec((block, width), lambda i: (i, 0)),
        pl.BlockSpec((heads, 1, length, block), lambda i: (0, i, 0, 0)),
        pl.BlockSpec((heads, 1, 8, block), lambda i: (0, i, 0, 0)),
    ] + [pl.BlockSpec((rows, width), lambda i: (0, 0))] * cuts
    out_shape = [
        jax.ShapeDtypeStruct((length, width), BF),
        jax.ShapeDtypeStruct((heads, count, length, block), BF),
        jax.ShapeDtypeStruct((heads, count, 8, block), F32),
    ] + [jax.ShapeDtypeStruct((rows, width), BF)] * cuts
    scratch = [
        pltpu.VMEM((heads, length, 256), BF),
        pltpu.VMEM((heads, HD + 16, length), BF),
        pltpu.VMEM((heads, length, block), F32),
    ]
    if source is not None:
        down, up, xs, ws, height = source
        parts = len(xs)
        counts = [w.shape[0] // height for w in ws]
        model = sum(w.shape[0] for w in ws)
        all_heads = ws[0].shape[1] // 3
        args = [down, up, *xs, *ws]
        in_specs += [vmem] * 2 + [anywhere] * (parts + len(ws))
        out_specs += [anywhere] * 3 + [vmem, anywhere]
        out_shape += [jax.ShapeDtypeStruct((length, all_heads), BF)] * 3
        out_shape += [jax.ShapeDtypeStruct((length, down.shape[0]), BF)]
        out_shape += [jax.ShapeDtypeStruct((model, 3 * all_heads), BF)]
        scratch += [
            pltpu.VMEM((length, model), BF),
            pltpu.VMEM((model, 3 * all_heads), BF),
            pltpu.VMEM((3, length, all_heads), BF),
            pltpu.SemaphoreType.DMA((parts,)),
            pltpu.SemaphoreType.DMA,
            pltpu.SemaphoreType.DMA((3,)),
            pltpu.SemaphoreType.DMA,
        ]
    else:
        parts = 0
        counts = []
        args = list(qkv)
        in_specs += [
            pl.BlockSpec((block, width), lambda i: (i, group)),
            pl.BlockSpec((length, width), lambda i: (0, group)),
            pl.BlockSpec((length, width), lambda i: (0, group)),
        ]
    return pl.pallas_call(
        functools.partial(
            attend_forward_kernel, heads, block, chunk, rows, group, cuts, parts, counts
        ),
        grid=(count,),
        in_specs=in_specs,
        out_specs=out_specs,
        out_shape=out_shape,
        scratch_shapes=scratch,
        compiler_params=pltpu.CompilerParams(
            vmem_limit_bytes=VMEM_LIMIT, dimension_semantics=("arbitrary",)
        ),
        cost_estimate=BRIEF,
        name="project_attend_forward" if parts else "attend_forward",
    )(lengths, *args)


def attend_backward_kernel(
    heads, block, chunk, cuts, q_ref, k_ref, v_ref, o_ref, e_ref, l_ref, *rest
):
    cut_refs = rest[0:cuts]
    dq_ref, dk_ref, dv_ref, do_rows_ref, values_wide, keys_t, dk_sum, dv_sum = rest[cuts:]
    length = k_ref.shape[0]
    rows = length // cuts
    width = heads * HD
    i = pl.program_id(0)
    for k in range(cuts):

        @pl.when(i == k * rows // block)
        def _():
            begin = k * rows % block
            do_rows_ref[begin : begin + rows, :] = cut_refs[k][...]

    @pl.when(i == 0)
    def _():
        ones = (lax.broadcasted_iota(jnp.int32, (length, 128), 1) < 2).astype(BF)
        for h in range(heads):
            value = v_ref[:, h * HD : (h + 1) * HD]
            values_wide[h, :, 0:HD] = value
            values_wide[h, :, HD : 2 * HD] = value
            values_wide[h, :, 2 * HD :] = ones
        keys_t[...] = k_ref[...].T
        dk_sum[...] = jnp.zeros_like(dk_sum)
        dv_sum[...] = jnp.zeros_like(dv_sum)

    q = q_ref[...]
    flipped_do = do_rows_ref[...].astype(F32).T
    flipped_o = o_ref[...].astype(F32).T
    lane = lax.broadcasted_iota(jnp.int32, (block, width), 1)
    row = lax.broadcasted_iota(jnp.int32, (128, block), 0)
    grads = []
    for h in range(heads):
        own = slice(h * HD, (h + 1) * HD)
        inverse = 1.0 / l_ref[h, 0, 0:1, :]
        dot = -jnp.sum(flipped_do[own] * flipped_o[own], axis=0, keepdims=True) * inverse
        scaled = flipped_do[own] * inverse
        high = scaled.astype(BF)
        low = (scaled - high.astype(F32)).astype(BF)
        dot_high = dot.astype(BF)
        dot_low = (dot - dot_high.astype(F32)).astype(BF)
        dots = jnp.where(row == 0, dot_high, jnp.where(row == 1, dot_low, jnp.zeros_like(dot_low)))
        right = jnp.concatenate([high, low, dots], axis=0)
        do_rows = high.T
        if heads == 2:
            empty = jnp.zeros_like(do_rows)
            do_rows = jnp.concatenate([do_rows, empty] if h == 0 else [empty, do_rows], axis=1)
        query = jnp.where((lane >= h * HD) & (lane < (h + 1) * HD), q, jnp.zeros_like(q))
        total = None
        for c in range(length // chunk):
            rows = slice(c * chunk, (c + 1) * chunk)
            e = e_ref[h, 0, rows, :]
            part = mm(values_wide[h, rows, :], right)
            ds = (e.astype(F32) * part).astype(BF)
            dv_sum[rows, :] += mm(e, do_rows)
            dk_sum[rows, :] += mm(ds, query)
            part = mm(keys_t[own, rows], ds)
            total = part if total is None else total + part
        grads.append(total * HD ** (-0.5))
    dq_ref[...] = jnp.concatenate(grads, axis=0).T.astype(BF)

    @pl.when(i == pl.num_programs(0) - 1)
    def _():
        dk_ref[...] = (dk_sum[...] * HD ** (-0.5)).astype(BF)
        dv_ref[...] = dv_sum[...].astype(BF)


def attend_backward(q, k, v, att, d_att, e, row_sum, group, heads):
    length = q.shape[0]
    width = heads * HD
    block = e.shape[3]
    cuts = len(d_att)
    rows = length // cuts
    chunk = min(512, length)
    count = length // block
    whole = pl.BlockSpec((length, width), lambda i: (0, group))
    return pl.pallas_call(
        functools.partial(attend_backward_kernel, heads, block, chunk, cuts),
        grid=(count,),
        in_specs=[
            pl.BlockSpec((block, width), lambda i: (i, group)),
            whole,
            whole,
            pl.BlockSpec((block, width), lambda i: (i, 0)),
            pl.BlockSpec((heads, 1, length, block), lambda i: (0, i, 0, 0)),
            pl.BlockSpec((heads, 1, 8, block), lambda i: (0, i, 0, 0)),
        ]
        + [pl.BlockSpec((rows, width), lambda i: (0, group))] * cuts,
        out_specs=[
            pl.BlockSpec((block, width), lambda i: (i, 0)),
            pl.BlockSpec((length, width), lambda i: (0, 0)),
            pl.BlockSpec((length, width), lambda i: (0, 0)),
        ],
        out_shape=[jax.ShapeDtypeStruct((length, width), BF)] * 3,
        scratch_shapes=[
            pltpu.VMEM((block, width), BF),
            pltpu.VMEM((heads, length, 256), BF),
            pltpu.VMEM((width, length), BF),
            pltpu.VMEM((length, width), F32),
            pltpu.VMEM((length, width), F32),
        ],
        compiler_params=pltpu.CompilerParams(
            vmem_limit_bytes=VMEM_LIMIT, dimension_semantics=("arbitrary",)
        ),
        cost_estimate=BRIEF,
        name="attend_backward",
    )(q, k, v, att, e, row_sum, *d_att)


def normal_parts(z):
    density = jnp.exp2(z * z * (-0.5 * LOG2E))
    t = 1.0 / (1.0 + (0.3275911 * 0.5**0.5) * jnp.abs(z))
    poly = t * (
        0.254829592 * 0.5
        + t
        * (
            -0.284496736 * 0.5
            + t * (1.421413741 * 0.5 + t * (-1.453152027 * 0.5 + t * (1.061405429 * 0.5)))
        )
    )
    tail = poly * density
    return jnp.where(z < 0.0, tail, 1.0 - tail), density * 0.3989422804014327


def normalize(values):
    center = values - jnp.mean(values, axis=-1, keepdims=True)
    scale = lax.rsqrt(jnp.mean(center * center, axis=-1, keepdims=True) + EPS)
    return center * scale, scale


def normalize_back(e, normal, scale):
    return scale * (
        e
        - jnp.mean(e, axis=-1, keepdims=True)
        - normal * jnp.mean(e * normal, axis=-1, keepdims=True)
    )


def assemble_kernel(rank, share, used, sets, down_ref, up_ref):
    ranks = 3 * rank
    count, tail = sets.shape[0], used - ranks
    for k in range(count):
        down_ref[:, k * 128 : (k + 1) * 128] = sets[k, 0:ranks, :]
    row = lax.broadcasted_iota(jnp.int32, (ranks, tail), 0)
    source = lax.broadcasted_iota(jnp.int32, (ranks, tail), 1)
    for j in range(3):
        for half in range(2):
            total = None
            for k in range(count):
                wanted = row < 0
                for r in range(share):
                    target = j * rank + k * share + r
                    wanted = wanted | (
                        (row == target) & (source == (j * share + r) * 2 + half)
                    )
                part = mm(jnp.where(wanted, 1.0, 0.0).astype(BF), sets[k, ranks:used, :])
                total = part if total is None else total + part
            begin = (j * 2 + half) * 128
            up_ref[:, begin : begin + 128] = total.astype(BF)


def assemble(sets, rank, share, used):
    count = sets.shape[0]
    vmem = pl.BlockSpec(memory_space=pltpu.VMEM)
    return pl.pallas_call(
        functools.partial(assemble_kernel, rank, share, used),
        in_specs=[vmem],
        out_specs=[vmem] * 2,
        out_shape=[
            jax.ShapeDtypeStruct((3 * rank, count * 128), BF),
            jax.ShapeDtypeStruct((3 * rank, 6 * 128), BF),
        ],
        name="assemble",
    )(sets)


def unproject_kernel(parts, groups, u_ref, w_ref, down_ref, up_ref, *rest):
    x_hbm = rest[0:parts]
    grads = rest[parts : parts + 3 * groups]
    out_ref, g_up_ref, g_down_ref, x, x_sem = rest[parts + 3 * groups :]
    width = w_ref.shape[1] // 3
    step = pl.program_id(0)
    rows = x.shape[1]
    copies = [pltpu.make_async_copy(x_hbm[i], x.at[i], x_sem.at[i]) for i in range(parts)]

    @pl.when(step == 0)
    def _():
        for copy in copies:
            copy.start()
        g_up_ref[...] = jnp.zeros_like(g_up_ref)
        g_down_ref[...] = jnp.zeros_like(g_down_ref)

    values = [
        jnp.concatenate([grads[g * 3 + j][...] for g in range(groups)], axis=1) for j in range(3)
    ]
    d_u = None
    for j in range(3):
        part = mm_nt(values[j], up_ref[:, j * width : (j + 1) * width])
        d_u = part if d_u is None else d_u + part
    d_u = d_u.astype(BF)
    total = mm(d_u, down_ref[...])
    for j in range(3):
        total = total + mm_nt(values[j], w_ref[:, j * width : (j + 1) * width])
    out_ref[...] = total.astype(BF)
    u_t = transpose_small(u_ref[...])
    for j in range(3):
        g_up_ref[:, j * width : (j + 1) * width] += mm(u_t, values[j])
    for i in range(parts):

        @pl.when(step == i)
        def _():
            copies[i].wait()

    g_down_ref[...] += mm(transpose_small(d_u), x[step])


def unproject(grads, u, w, down, up, xs, half):
    model = w.shape[0]
    width = w.shape[1] // 3
    rows = xs[0].shape[0]
    steps = len(xs)
    ranks = down.shape[0]
    grads = [value for group in grads for value in group]
    vmem = pl.BlockSpec(memory_space=pltpu.VMEM)
    return pl.pallas_call(
        functools.partial(unproject_kernel, steps, len(grads) // 3),
        grid=(steps,),
        in_specs=[pl.BlockSpec((rows, ranks), lambda i: (half * steps + i, 0))]
        + [vmem] * 3
        + [pl.BlockSpec(memory_space=pl.ANY)] * steps
        + [pl.BlockSpec((rows, g.shape[1]), lambda i: (half * steps + i, 0)) for g in grads],
        out_specs=[pl.BlockSpec((rows, model), lambda i: (i, 0)), vmem, vmem],
        out_shape=[
            jax.ShapeDtypeStruct((rows * steps, model), BF),
            jax.ShapeDtypeStruct((ranks, 3 * width), F32),
            jax.ShapeDtypeStruct((ranks, model), F32),
        ],
        scratch_shapes=[
            pltpu.VMEM((steps, rows, model), BF),
            pltpu.SemaphoreType.DMA((steps,)),
        ],
        compiler_params=pltpu.CompilerParams(
            vmem_limit_bytes=VMEM_LIMIT, dimension_semantics=("arbitrary",)
        ),
        cost_estimate=BRIEF,
        name="unproject",
    )(u, w, down, up, *xs, *grads)


def middle_kernel(
    cuts, parts, counts, sizes, hidden_block, x_ref, cot_ref,
    down_out, up_out, down_fc1, up_fc1, down_fc2, up_fc2, gain1, bias1, gain2, bias2, *rest
):
    att_hbm = rest[0:parts]
    rest = rest[parts:]
    first_hbm = rest[0 : len(counts)]
    second_hbm = rest[len(counts) : 2 * len(counts)]
    rest = rest[2 * len(counts) :]
    out_ref, dy1_ref = rest[0:2]
    d_att_refs = rest[2 : 2 + cuts]
    (
        g_up_fc2, g_down_fc2, g_up_fc1, g_down_fc1, g_up_out, g_down_out,
        att_own, wo_t, w1, w2_t, hidden, slope, normal1, normed, low_rows, total,
        att_sem, wo_sem, w1_sem, w2_sem,
    ) = rest[2 + cuts :]
    rows, model = x_ref.shape
    units = w1.shape[1]
    height, wide, narrow = sizes
    mine = lax.axis_index("tensor")
    n_t = lax.axis_size("tensor")
    order = cut_order(n_t)
    places = spread_places() if sum(counts) > 1 else [(0, 0)]

    def fetch(source, j, begin, width, target, row, col, sem):
        pltpu.make_async_copy(
            source.at[j * height : (j + 1) * height, begin : begin + width],
            target.at[
                pl.ds(pl.multiple_of(row * height, height), height),
                pl.ds(pl.multiple_of(col * width, width), width),
            ],
            sem,
        ).start()

    def each_block():
        block = 0
        for i, count in enumerate(counts):
            for j in range(count):
                yield (i, j) + places[block]
                block += 1

    if parts > 1:
        width = att_hbm[0].shape[1]
        groups = parts // n_t
        for k in range(n_t):
            for g in range(groups):
                col = pl.multiple_of(((mine ^ order[k]) * groups + g) * width, width)
                pltpu.make_async_copy(
                    att_hbm[k * groups + g], att_own.at[:, pl.ds(col, width)], att_sem
                ).start()
    else:
        pltpu.make_async_copy(att_hbm[0], att_own, att_sem).start()
    for i, j, row, col in each_block():
        fetch(first_hbm[i], j, wide, narrow, wo_t, row, col, wo_sem)
    for i, j, row, col in each_block():
        fetch(first_hbm[i], j, 0, wide, w1, row, col, w1_sem.at[col])
    for i, j, row, col in each_block():
        fetch(second_hbm[i], j, 0, wide, w2_t, row, col, w2_sem.at[col])

    pltpu.make_async_copy(att_own, att_own, att_sem).wait()
    pltpu.make_async_copy(wo_t, wo_t, wo_sem).wait()
    att = att_own[...]
    u_out = mm_nt(att, down_out[...]).astype(BF)
    first = x_ref[...].astype(F32) + mm_nt(att, wo_t[...]) + mm(u_out, up_out[...])
    normal, scale1 = normalize(first)
    normal1[...] = normal
    full = normal * gain1[...].astype(F32) + bias1[...].astype(F32)
    normed[...] = full
    low_rows[...] = full.astype(BF)
    u_fc1 = mm_nt(low_rows[...], down_fc1[...]).astype(BF)

    blocks = units // hidden_block
    per_cut = wide // hidden_block

    def before(i):
        cols = slice(i * hidden_block, (i + 1) * hidden_block)
        if i % per_cut == 0:
            b = i // per_cut
            for target, sem in ((w1, w1_sem), (w2_t, w2_sem)):
                view = target.at[:, b * wide : (b + 1) * wide]
                pltpu.make_async_copy(view, view, sem.at[b]).wait()
        return mm(low_rows[...], w1[:, cols]) + mm(u_fc1, up_fc1[:, cols])

    z = before(0)
    u_sum = None
    for i in range(blocks):
        cols = slice(i * hidden_block, (i + 1) * hidden_block)
        following = before(i + 1) if i + 1 < blocks else None
        phi_sum, phi = normal_parts(z)
        act = (z * phi_sum).astype(BF)
        hidden[:, cols] = act
        slope[:, cols] = phi_sum + z * phi
        part = mm_nt(act, w2_t[:, cols])
        total[...] = part if i == 0 else total[...] + part
        part = mm_nt(act, down_fc2[:, cols])
        u_sum = part if u_sum is None else u_sum + part
        z = following
    u_fc2 = u_sum.astype(BF)
    second = normed[...] + total[...] + mm(u_fc2, up_fc2[...])
    normal2, scale2 = normalize(second)
    gain = gain2[...].astype(F32)
    out_ref[...] = (normal2 * gain + bias2[...].astype(F32)).astype(BF)
    d_second = normalize_back(cot_ref[...].astype(F32) * gain, normal2, scale2)
    total[...] = d_second
    d_ffn = d_second.astype(BF)
    d_u2 = mm_nt(d_ffn, up_fc2[...]).astype(BF)
    d_u2_t = transpose_small(d_u2)
    g_up_fc2[...] = mm(transpose_small(u_fc2), d_ffn).astype(BF)
    u_fc1_t = transpose_small(u_fc1)

    def before_back(i):
        cols = slice(i * hidden_block, (i + 1) * hidden_block)
        return mm(d_ffn, w2_t[:, cols]) + mm(d_u2, down_fc2[:, cols])

    d_hidden = before_back(0)
    u_sum = None
    for i in range(blocks):
        cols = slice(i * hidden_block, (i + 1) * hidden_block)
        following = before_back(i + 1) if i + 1 < blocks else None
        d_pre = (d_hidden * slope[:, cols]).astype(BF)
        g_down_fc2[:, cols] = mm(d_u2_t, hidden[:, cols]).astype(BF)
        g_up_fc1[:, cols] = mm(u_fc1_t, d_pre).astype(BF)
        total[...] += mm_nt(d_pre, w1[:, cols])
        part = mm_nt(d_pre, up_fc1[:, cols])
        u_sum = part if u_sum is None else u_sum + part
        d_hidden = following
    d_u1 = u_sum.astype(BF)
    d_normed = total[...] + mm(d_u1, down_fc1[...])
    g_down_fc1[...] = mm(transpose_small(d_u1), low_rows[...]).astype(BF)
    d_first = normalize_back(d_normed * gain1[...].astype(F32), normal1[...], scale1)
    dy1_ref[...] = d_first
    d_a = d_first.astype(BF)
    d_uo = mm_nt(d_a, up_out[...]).astype(BF)
    g_up_out[...] = mm(transpose_small(u_out), d_a).astype(BF)
    g_down_out[...] = mm(transpose_small(d_uo), att).astype(BF)
    att_own[...] = (mm(d_a, wo_t[...]) + mm(d_uo, down_out[...])).astype(BF)
    width = model // cuts
    for k in range(cuts):
        col = pl.multiple_of((mine ^ order[k]) * width, width) if cuts > 1 else 0
        d_att_refs[k][...] = att_own[:, pl.ds(col, width)]


def cut_order(n_t):
    order = [0]
    bit = n_t // 2
    while bit:
        order = order + [k ^ bit for k in order]
        bit //= 2
    return order


def middle(atts, cuts, x, cot, adapters, norms, firsts, seconds, sizes):
    rows, model = x.shape
    rank, units = adapters[3].shape
    height, wide, narrow = sizes
    counts = [value.shape[0] // height for value in firsts]
    hidden_block = min(512, wide)
    cols = units // wide
    vmem = pl.BlockSpec(memory_space=pltpu.VMEM)
    anywhere = pl.BlockSpec(memory_space=pl.ANY)
    long = jax.ShapeDtypeStruct((rank, units), BF)
    short = jax.ShapeDtypeStruct((rank, model), BF)
    out_shape = (
        [jax.ShapeDtypeStruct((rows, model), BF), jax.ShapeDtypeStruct((rows, model), F32)]
        + [jax.ShapeDtypeStruct((rows, model // cuts), BF)] * cuts
        + [short, long, long, short, short, short]
    )
    return pl.pallas_call(
        functools.partial(middle_kernel, cuts, len(atts), counts, sizes, hidden_block),
        in_specs=[vmem] * 12 + [anywhere] * (len(atts) + len(firsts) + len(seconds)),
        out_specs=[vmem] * len(out_shape),
        out_shape=out_shape,
        scratch_shapes=[
            pltpu.VMEM((rows, model), BF),
            pltpu.VMEM((model, model), BF),
            pltpu.VMEM((model, units), BF),
            pltpu.VMEM((model, units), BF),
            pltpu.VMEM((rows, units), BF),
            pltpu.VMEM((rows, units), F32),
            pltpu.VMEM((rows, model), F32),
            pltpu.VMEM((rows, model), F32),
            pltpu.VMEM((rows, model), BF),
            pltpu.VMEM((rows, model), F32),
            pltpu.SemaphoreType.DMA,
            pltpu.SemaphoreType.DMA,
            pltpu.SemaphoreType.DMA((cols,)),
            pltpu.SemaphoreType.DMA((cols,)),
        ],
        compiler_params=pltpu.CompilerParams(vmem_limit_bytes=VMEM_LIMIT),
        cost_estimate=BRIEF,
        name="middle",
    )(x, cot, *adapters, *norms, *atts, *firsts, *seconds)


class Spread:
    def __init__(self):
        self.n_dp, self.n_t = lax.axis_size("dp"), lax.axis_size("tensor")
        self.devices = [(d, t) for d in range(self.n_dp) for t in range(self.n_t)]

    def send(self, value, target):
        n_t = self.n_t
        pairs = []
        for d, t in self.devices:
            to_d, to_t = target(d, t)
            pairs.append((d * n_t + t, to_d * n_t + to_t))
        return lax.ppermute(value, ("dp", "tensor"), pairs)

    def ring(self, value):
        return self.send(value, lambda d, t: ((d + 2) % self.n_dp, t))

    def along_z(self, value):
        count = self.n_dp // 2
        return [value] + [
            self.send(value, lambda d, t, j=j: ((d + 2 * j) % self.n_dp, t))
            for j in range(1, count)
        ]

    def cross(self, value, core):
        return self.send(value, lambda d, t: (d ^ 1, t) if t % 2 == core else (d, t ^ 2))

    def core(self, value):
        return self.send(value, lambda d, t: (d, t ^ 1))


def spread_places():
    n_dp = lax.axis_size("dp")
    d = lax.axis_index("dp")
    mine = lax.axis_index("tensor")
    found = []
    for t in (mine, mine ^ 1):
        even = (t % 2) == 0
        for to_d, to_t in (
            (d, t),
            (jnp.where(even, d ^ 1, d), jnp.where(even, t, t ^ 2)),
            (jnp.where(even, d, d ^ 1), jnp.where(even, t ^ 2, t)),
            (d ^ 1, t ^ 2),
        ):
            found += [((to_d + n_dp - 2 * j) % n_dp, to_t) for j in range(n_dp // 2)]
    return found


def shards(
    inputs, cotangent, lengths, adapter_index, w_qkv, w_out, w_fc1, w_fc2,
    ln1_gain, ln1_bias, ln2_gain, ln2_bias, down_qkv, up_qkv, down_out, up_out,
    down_fc1, up_fc1, down_fc2, up_fc2,
):
    n_dp = lax.axis_size("dp")
    n_t = lax.axis_size("tensor")
    every = ("dp", "tensor")
    mine = lax.axis_index("tensor")
    rows, model = inputs.shape
    length = rows * n_t
    n_set = down_qkv.shape[1]
    rank = down_qkv.shape[3]
    r_dp = rank // n_dp
    r_t = rank // n_t
    d_dp = model // n_dp
    c_t = model // n_t
    f_t = w_fc1.shape[1]
    f_all = f_t * n_t

    def swap(value, bit):
        return lax.ppermute(value, "tensor", [(i, i ^ bit) for i in range(n_t)])

    bits = []
    bit = n_t // 2
    while bit:
        bits.append(bit)
        bit //= 2
    order = cut_order(n_t)

    x_parts = [inputs]
    for bit in bits[:-1]:
        x_parts = x_parts + [swap(part, bit) for part in x_parts]

    w_local = w_qkv.transpose(1, 0, 2).reshape(d_dp, 3 * c_t)
    packed_second = w_fc2.T
    staged = n_dp == 8 and n_t == 4
    if staged:
        spread = Spread()
        packed = jnp.concatenate([w_fc1, w_out.T, w_local], axis=1)
        hops = [packed, spread.ring(packed)]
        block_sizes = (d_dp, f_t, c_t)
    else:

        def whole(value):
            blocks = lax.all_gather(value, every, axis=0).reshape(n_dp, n_t, d_dp, -1)
            return blocks.transpose(0, 2, 1, 3).reshape(model, -1)

        firsts = [jnp.concatenate([whole(w_fc1), whole(w_out.T)], axis=1)]
        seconds = [whole(packed_second)]
        w_parts = [lax.all_gather(w_local, "dp", axis=0, tiled=True)]
        w_height = model
        block_sizes = (model, f_all, model)

    index_all = lax.all_to_all(
        jnp.broadcast_to(adapter_index, (n_dp,)), "dp", 0, 0, tiled=True
    )
    onehot_all = (index_all[:, None] == jnp.arange(n_set, dtype=jnp.int32)[None, :]).astype(BF)
    def part_of_rank(value):
        return lax.dynamic_slice_in_dim(value, mine * r_t, r_t, 1)

    down_t = down_qkv.transpose(1, 0, 3, 2).reshape(n_set, 3 * rank, d_dp)
    up_first = up_qkv.transpose(1, 0, 2, 3)
    tables = [
        down_out.transpose(0, 2, 1),
        part_of_rank(up_out),
        part_of_rank(down_fc1.transpose(0, 2, 1)),
        up_fc1,
        down_fc2.transpose(0, 2, 1),
        part_of_rank(up_fc2),
    ]
    sizes = [t.size // n_set for t in tables]
    norm_part = jnp.stack([ln1_gain, ln1_bias, ln2_gain, ln2_bias])
    in_rows = staged and d_dp == 128 and c_t == 256
    if in_rows:
        parts = [down_t, up_first.reshape(n_set, -1, 128)]
        parts.append(jnp.zeros((n_set, -parts[1].shape[1] % 16, 128), BF))
        qkv_rows = sum(p.shape[1] for p in parts)
        parts += [t.reshape(n_set, -1, 128) for t in tables]
        parts.append(jnp.broadcast_to(norm_part, (n_set, 4, d_dp)))
        parts.append(jnp.zeros((n_set, -sum(p.shape[1] for p in parts) % 16, 128), BF))
        table = jnp.concatenate(parts, axis=1)
        sets = jnp.einsum("ns,srl->nrl", onehot_all, table, preferred_element_type=F32).astype(BF)
        hops[1], sets = lax.optimization_barrier((hops[1], sets))
        hops.append(spread.ring(hops[1]))
        sets = lax.all_to_all(sets, "dp", 0, 0, tiled=True)
        hops[2], sets, packed_second = lax.optimization_barrier((hops[2], sets, packed_second))
        hops.append(spread.ring(hops[2]))
        second = spread.along_z(packed_second)
        sel_down_qkv, sel_up_qkv = assemble(sets, rank, r_dp, qkv_rows)
        begin = qkv_rows + sum(sizes) // 128
        came = sets[:, qkv_rows:begin]
        norms = sets[:, begin : begin + 4].transpose(1, 0, 2).reshape(4, 1, model)
    else:
        flat = [t.reshape(n_set, -1) for t in (down_t, up_first, *tables)]
        flat.append(jnp.broadcast_to(norm_part.reshape(1, -1), (n_set, 4 * d_dp)))
        table = jnp.concatenate(flat, axis=1)
        sets = lax.all_to_all(mm(onehot_all, table).astype(BF), "dp", 0, 0, tiled=True)
        cut = 3 * rank * d_dp
        cut_up = cut + up_first.size // n_set
        sel_down_qkv = (
            sets[:, :cut].reshape(n_dp, 3 * rank, d_dp).transpose(1, 0, 2).reshape(3 * rank, model)
        )
        up_cols = sets[:, cut:cut_up].reshape(n_dp, 3, r_dp, c_t).transpose(1, 0, 2, 3)
        same = jnp.eye(3, dtype=BF).reshape(3, 1, 3, 1)
        sel_up_qkv = (up_cols.reshape(3, rank, 1, c_t) * same).reshape(3 * rank, 3 * c_t)
        came = sets[:, cut_up : cut_up + sum(sizes)]
        norms = sets[:, cut_up + sum(sizes) :].reshape(n_dp, 4, d_dp)
        norms = norms.transpose(1, 0, 2).reshape(4, 1, model)
    shares = [came]
    for bit in bits:
        shares = shares + [swap(share, bit) for share in shares]
    of_owner = jnp.array([order.index(k) for k in range(n_t)], jnp.int32)
    of_owner = of_owner[jnp.arange(n_t, dtype=jnp.int32) ^ mine]

    def make_adapters(shares):
        stacked = jnp.stack(shares)
        came = jnp.concatenate(
            [
                lax.dynamic_index_in_dim(stacked, of_owner[t], 0, keepdims=True)
                for t in range(n_t)
            ]
        )
        came = came.reshape(n_t, n_dp, -1)
        pieces = []
        start = 0
        for size in sizes:
            pieces.append(came[:, :, start : start + size])
            start += size

        def from_rank_parts(piece):
            return piece.reshape(n_t, n_dp, r_t, d_dp).transpose(0, 2, 1, 3).reshape(rank, model)

        def from_blocks(piece, width):
            return (
                piece.reshape(n_t, n_dp, r_dp, width)
                .transpose(1, 2, 0, 3)
                .reshape(rank, n_t * width)
            )

        return [
            from_blocks(pieces[0], c_t),
            from_rank_parts(pieces[1]),
            from_rank_parts(pieces[2]),
            from_blocks(pieces[3], f_t),
            from_blocks(pieces[4], f_t),
            from_rank_parts(pieces[5]),
        ]

    x_parts = x_parts + [swap(part, bits[-1]) for part in x_parts]
    if staged:
        w_near = jnp.concatenate([hop[:, f_t + c_t :] for hop in hops], axis=0)
        w_parts = [w_near, lax.ppermute(w_near, "dp", [(i, i ^ 1) for i in range(n_dp)])]
        w_height = d_dp
        first = jnp.concatenate([hop[:, : f_t + c_t] for hop in hops], axis=0)
        first_one = spread.cross(first, 0)
        first_two = spread.cross(first, 1)
        second = jnp.concatenate(second, axis=0)
        first, second, x_parts, shares, w_parts = lax.optimization_barrier(
            (first, second, x_parts, shares, w_parts)
        )
        second_one = spread.cross(second, 0)
        second_two = spread.cross(second, 1)
    heads = c_t // HD
    group_heads = 2 if heads % 2 == 0 else 1
    groups = heads // group_heads
    kept = []
    att_parts = [[] for _ in range(n_t)]
    for g in range(groups):
        if g == 0:
            att, e, row_sum, *more = attend_forward(
                lengths, g, group_heads, rows, n_t,
                source=(sel_down_qkv, sel_up_qkv, x_parts, w_parts, w_height),
            )
            cut_rows, qkv, u_in, w_cols = more[:n_t], more[n_t : n_t + 3], *more[n_t + 3 :]
        else:
            if staged and g == 1:
                near = [first, first_one, first_two, second, second_one, second_two]
                qkv, near = lax.optimization_barrier((qkv, near))
                first_both = spread.cross(near[1], 1)
                second_both = spread.cross(near[4], 1)
                over = [spread.core(value) for value in near]
            att, e, row_sum, *cut_rows = attend_forward(
                lengths, g, group_heads, rows, n_t, qkv=qkv
            )
        kept.append((att, e, row_sum))
        for k in range(n_t):
            att_parts[k].append(cut_rows[k] if order[k] == 0 else swap(cut_rows[k], order[k]))
    atts = [part for parts in att_parts for part in parts]

    if staged:
        kept, over, first_both, second_both = lax.optimization_barrier(
            (kept, over, first_both, second_both)
        )
        firsts = near[:3] + [first_both] + over[:3] + [spread.core(first_both)]
        seconds = near[3:] + [second_both] + over[3:] + [spread.core(second_both)]
    adapters = make_adapters(shares)
    blocks_fit = c_t % 128 == 0
    if not blocks_fit:
        by_cut = jnp.concatenate(atts, axis=1).reshape(rows, n_t, c_t)
        atts = [jnp.take(by_cut, of_owner, axis=1).reshape(rows, model)]
    cuts = n_t if blocks_fit else 1
    done = middle(
        atts, cuts, inputs, cotangent, adapters, list(norms), firsts, seconds, block_sizes
    )
    output, d_first = done[0:2]
    d_att_blocks = done[2 : 2 + cuts]
    if not blocks_fit:
        by_owner = d_att_blocks[0].reshape(rows, n_t, c_t)
        d_att_blocks = [
            lax.dynamic_index_in_dim(by_owner, mine ^ order[k], 1, keepdims=False)
            for k in range(n_t)
        ]
    g_up_fc2, g_down_fc2, g_up_fc1, g_down_fc1, g_up_out, g_down_out = done[2 + cuts :]

    def share_cols(value):
        lead = value.size // model
        return (
            value.reshape(lead, n_dp, n_t, model // (n_dp * n_t))
            .transpose(1, 2, 0, 3)
            .reshape(n_dp * n_t, -1)
        )

    def share_blocks(value):
        width = value.shape[1] // n_t
        return (
            value.reshape(n_dp, r_dp, n_t, width).transpose(0, 2, 1, 3).reshape(n_dp * n_t, -1)
        )

    early = [
        share_blocks(g_down_out),
        share_cols(g_up_out),
        share_cols(g_down_fc1),
        share_blocks(g_up_fc1),
        share_blocks(g_down_fc2),
        share_cols(g_up_fc2),
    ]
    early = jnp.concatenate(early, axis=1)

    d_att_all = [
        d_att_blocks[k] if order[k] == 0 else swap(d_att_blocks[k], order[k]) for k in range(n_t)
    ]
    d_att_all, early = lax.optimization_barrier((d_att_all, early))
    grads = []
    for g in range(groups):
        grads.append(
            attend_backward(*qkv, kept[g][0], d_att_all, kept[g][1], kept[g][2], g, group_heads)
        )

    def partly(half):
        xs = x_parts[half * n_t // 2 : (half + 1) * n_t // 2]
        return unproject(grads, u_in, w_cols, sel_down_qkv, sel_up_qkv, xs, half)

    other, g_up_other, g_down_other = partly(1)
    parts, g_up_own, g_down_own = partly(0)
    pending = [parts, swap(other, bits[-1])]
    span = length // 2
    for bit in reversed(bits[:-1]):
        half = span // 2
        sent = sum(value[half:].astype(F32) for value in pending).astype(BF)
        sent, pending = lax.optimization_barrier((sent, pending))
        pending = [value[:half] for value in pending] + [swap(sent, bit)]
        span = half
    g_down_qkv = (g_down_own + g_down_other).astype(BF)
    g_up_all = (g_up_own + g_up_other).astype(BF)
    g_up_qkv = jnp.stack(
        [
            g_up_all[j * rank : (j + 1) * rank, j * c_t : (j + 1) * c_t]
            for j in range(3)
        ]
    )
    up_share = (
        g_up_qkv.reshape(3, n_dp, r_dp, c_t).transpose(1, 0, 2, 3).reshape(n_dp, 1, -1)
    )
    up_share = jnp.broadcast_to(up_share, (n_dp, n_t, up_share.shape[2])).reshape(n_dp * n_t, -1)
    late = [share_cols(g_down_qkv), up_share]
    every_grad = jnp.concatenate([early, *late], axis=1)
    every_grad, pending[:-1] = lax.optimization_barrier((every_grad, pending[:-1]))
    got = lax.all_to_all(every_grad, every, 0, 0, tiled=True)
    grad_input = d_first
    for value in pending:
        grad_input = grad_input + value.astype(F32)

    by_sender = jnp.broadcast_to(onehot_all[:, None, :], (n_dp, n_t, n_set)).reshape(-1, n_set)
    same_cols = (jnp.arange(n_dp * n_t, dtype=jnp.int32) % n_t == mine).astype(BF)
    tn = (((0,), (0,)), ((), ()))

    def total(got, weights):
        return lax.dot_general(weights, got, tn, preferred_element_type=F32)

    up_begin = got.shape[1] - up_share.shape[1]
    sums = total(got[:, :up_begin], by_sender)
    pieces = []
    start = 0
    for size in sizes + [3 * rank * model // (n_dp * n_t)]:
        pieces.append(sums[:, start : start + size])
        start += size
    d_all = model // (n_dp * n_t)
    sum_down_out = pieces[0].reshape(n_set, r_dp, c_t).transpose(0, 2, 1)
    sum_up_out = pieces[1].reshape(n_set, rank, d_all)
    sum_down_fc1 = pieces[2].reshape(n_set, rank, d_all).transpose(0, 2, 1)
    sum_up_fc1 = pieces[3].reshape(n_set, r_dp, f_t)
    sum_down_fc2 = pieces[4].reshape(n_set, r_dp, f_t).transpose(0, 2, 1)
    sum_up_fc2 = pieces[5].reshape(n_set, rank, d_all)
    sum_down_qkv = pieces[6].reshape(n_set, 3, rank, d_all).transpose(1, 0, 3, 2)
    sum_up_qkv = (
        total(got[:, up_begin:], by_sender * same_cols[:, None])
        .reshape(n_set, 3, r_dp, c_t)
        .transpose(1, 0, 2, 3)
    )
    return (
        output,
        grad_input,
        sum_down_qkv,
        sum_up_qkv,
        sum_down_out,
        sum_up_out,
        sum_down_fc1,
        sum_up_fc1,
        sum_down_fc2,
        sum_up_fc2,
    )


def solution(mesh):
    both = ("dp", "tensor")
    in_specs = (
        P(both, None),
        P(both, None),
        P("dp", None),
        P("dp"),
        P(None, "dp", "tensor"),
        P("tensor", "dp"),
        P("dp", "tensor"),
        P("tensor", "dp"),
        P("dp"),
        P("dp"),
        P("dp"),
        P("dp"),
        P(None, None, "dp", None),
        P(None, None, "dp", "tensor"),
        P(None, "tensor", "dp"),
        P(None, None, "dp"),
        P(None, "dp", None),
        P(None, "dp", "tensor"),
        P(None, "tensor", "dp"),
        P(None, None, "dp"),
    )
    out_specs = (
        P(both, None),
        P(both, None),
        P(None, None, both, None),
        P(None, None, "dp", "tensor"),
        P(None, "tensor", "dp"),
        P(None, None, both),
        P(None, both, None),
        P(None, "dp", "tensor"),
        P(None, "tensor", "dp"),
        P(None, None, both),
    )
    return jax.shard_map(shards, mesh=mesh, in_specs=in_specs, out_specs=out_specs, check_vma=False)
```

```python
import functools

import jax
import jax.numpy as jnp
from jax import lax
from jax.experimental import pallas as pl
from jax.experimental.pallas import tpu as pltpu
from jax.sharding import PartitionSpec as P

HD = 64
EPS = 1e-05
NEG = -1000000000.0
LOG2E = 1.4426950408889634
BF = jnp.bfloat16
F32 = jnp.float32
VMEM_LIMIT = 60 * 2**20
BRIEF = pl.CostEstimate(flops=1, bytes_accessed=1, transcendentals=0)


def mm(left, right):
    return jnp.dot(left, right, preferred_element_type=F32)


def mm_nt(left, right):
    return lax.dot_general(left, right, (((1,), (1,)), ((), ())), preferred_element_type=F32)


def transpose_small(value):
    return value.astype(F32).T.astype(BF)


def token_place(index, rows, cuts, mine):
    shift = rows.bit_length() - 1
    bits = cuts.bit_length() - 1
    block = index >> shift
    reverse = jnp.zeros_like(block)
    for i in range(bits):
        reverse = reverse | (((block >> i) & 1) << (bits - 1 - i))
    return ((reverse ^ mine) << shift) | (index & (rows - 1))


def ring_owners():
    n_dp = lax.axis_size("dp")
    mine = lax.axis_index("dp")
    return [
        (d + n_dp - 2 * j) % n_dp for d in (mine, mine ^ 1) for j in range(n_dp // 2)
    ]


def attend_forward_kernel(
    heads, block, chunk, rows, group, cuts, parts, counts, lengths_ref, *rest
):
    projecting = parts > 0
    if projecting:
        down_ref, up_ref = rest[0:2]
        x_hbm = rest[2 : 2 + parts]
        w_hbm = rest[2 + parts : 2 + parts + len(counts)]
        rest = rest[2 + parts + len(counts) :]
    else:
        q_ref, k_ref, v_ref = rest[0:3]
        rest = rest[3:]
    att_ref, e_ref, l_ref = rest[0:3]
    cut_refs = rest[3 : 3 + cuts]
    rest = rest[3 + cuts :]
    if projecting:
        qkv_hbm, u_ref, w_out_hbm = rest[0:3], rest[3], rest[4]
        keys_wide, values_t, scores, x, w_ref, qkv, x_sem, w_sem, out_sem, w_out_sem = rest[5:]
    else:
        keys_wide, values_t, scores = rest
    length = keys_wide.shape[1]
    width = heads * HD
    mine = lax.axis_index("tensor")
    step = pl.program_id(0)
    steps = pl.num_programs(0)
    ends = [lengths_ref[0, 0]]
    for d in range(1, lengths_ref.shape[1]):
        ends.append(ends[-1] + lengths_ref[0, d])

    @pl.when(step == 0)
    def _():
        if projecting:
            owners = ring_owners() if len(counts) > 1 else [0]
            height = w_ref.shape[0] // sum(counts)
            for i, count in enumerate(counts):
                for j in range(count):
                    row = pl.multiple_of(owners[i * count + j] * height, height)
                    pltpu.make_async_copy(
                        w_hbm[i].at[j * height : (j + 1) * height, :],
                        w_ref.at[pl.ds(row, height), :],
                        w_sem,
                    ).start()
            copies = []
            begin = 0
            for i in range(parts):
                size = x_hbm[i].shape[0]
                copies.append(
                    pltpu.make_async_copy(x_hbm[i], x.at[begin : begin + size], x_sem.at[i])
                )
                copies[-1].start()
                begin += size
        lane = lax.broadcasted_iota(jnp.int32, (1, 128), 1)
        begin = jnp.zeros_like(lane)
        end = jnp.zeros_like(lane)
        for d in range(len(ends)):
            begin = jnp.where(lane == d, ends[d - 1] if d else 0, begin)
            end = jnp.where(lane == d, ends[d], end)
        place = token_place(
            lax.broadcasted_iota(jnp.int32, (length, 128), 0), rows, cuts, mine
        )
        onehot = jnp.where((place >= begin) & (place < end), 1.0, 0.0).astype(BF)
        for h in range(heads):
            keys_wide[h, :, 2 * HD :] = onehot
        if projecting:
            all_heads = qkv.shape[2]
            first = 0
            pltpu.make_async_copy(w_ref, w_ref, w_sem).wait()
            pltpu.make_async_copy(w_ref, w_out_hbm, w_out_sem).start()
            for i in range(parts):
                size = x_hbm[i].shape[0]
                copies[i].wait()
                step_rows = min(512, size)
                for r in range(first, first + size, step_rows):
                    here = x[r : r + step_rows, :]
                    u = mm_nt(here, down_ref[...]).astype(BF)
                    u_ref[r : r + step_rows, :] = u
                    for j in range(3):
                        cols = slice(j * all_heads, (j + 1) * all_heads)
                        qkv[j, r : r + step_rows, :] = (
                            mm(here, w_ref[:, cols]) + mm(u, up_ref[:, cols])
                        ).astype(BF)
                first += size
            for j in range(3):
                pltpu.make_async_copy(qkv.at[j], qkv_hbm[j], out_sem.at[j]).start()
        ones = (lax.broadcasted_iota(jnp.int32, (16, length), 0) == 0).astype(BF)
        values = qkv[2, :, group * width : (group + 1) * width] if projecting else v_ref[...]
        flipped = values.T
        for h in range(heads):
            own = slice(group * width + h * HD, group * width + (h + 1) * HD)
            key = qkv[1, :, own] if projecting else k_ref[:, h * HD : (h + 1) * HD]
            keys_wide[h, :, 0:HD] = key
            keys_wide[h, :, HD : 2 * HD] = key
            values_t[h, 0:HD, :] = flipped[h * HD : (h + 1) * HD, :]
            values_t[h, HD:, :] = ones

    if projecting:
        query_rows = qkv[0, pl.ds(pl.multiple_of(step * block, block), block), :]
        query_rows = query_rows[:, group * width : (group + 1) * width]
    else:
        query_rows = q_ref[...]
    flipped_q = query_rows.astype(F32).T * (HD ** (-0.5) * LOG2E)
    place = token_place(
        lax.broadcasted_iota(jnp.int32, (1, block), 1) + step * block, rows, cuts, mine
    )
    segment = jnp.zeros_like(place)
    for end in ends:
        segment = segment + (place >= end).astype(jnp.int32)
    mask = jnp.where(
        lax.broadcasted_iota(jnp.int32, (128, block), 0) == segment, 0.0, NEG
    ).astype(BF)
    mixed = []
    for h in range(heads):
        query = flipped_q[h * HD : (h + 1) * HD, :]
        high = query.astype(BF)
        low = (query - high.astype(F32)).astype(BF)
        right = jnp.concatenate([high, low, mask], axis=0)
        top = None
        for c in range(length // chunk):
            part = mm(keys_wide[h, c * chunk : (c + 1) * chunk, :], right)
            scores[h, c * chunk : (c + 1) * chunk, :] = part
            part = jnp.max(part.reshape(chunk // 8, 8, block), axis=0)
            top = part if top is None else jnp.maximum(top, part)
        top = jnp.max(top, axis=0, keepdims=True)
        total = None
        for c in range(length // chunk):
            e = jnp.exp2(scores[h, c * chunk : (c + 1) * chunk, :] - top).astype(BF)
            e_ref[h, 0, c * chunk : (c + 1) * chunk, :] = e
            part = mm(values_t[h, :, c * chunk : (c + 1) * chunk], e)
            total = part if total is None else total + part
        row_sum = total[HD : HD + 1, :]
        l_ref[h, 0] = jnp.broadcast_to(row_sum, (8, block))
        mixed.append(total[0:HD, :] / row_sum)
    att = jnp.concatenate(mixed, axis=0).T.astype(BF)
    att_ref[...] = att
    for k in range(cuts):

        @pl.when(step == k * rows // block)
        def _():
            begin = k * rows % block
            cut_refs[k][...] = att[begin : begin + rows, :]

    if projecting:

        @pl.when(step == steps - 1)
        def _():
            for j in range(3):
                pltpu.make_async_copy(qkv.at[j], qkv_hbm[j], out_sem.at[j]).wait()
            pltpu.make_async_copy(w_ref, w_out_hbm, w_out_sem).wait()


def attend_forward(lengths, group, heads, rows, cuts, qkv=None, source=None):
    length = rows * cuts
    width = heads * HD
    block = min(512, length)
    chunk = min(512, length)
    count = length // block
    vmem = pl.BlockSpec(memory_space=pltpu.VMEM)
    anywhere = pl.BlockSpec(memory_space=pl.ANY)
    in_specs = [pl.BlockSpec(memory_space=pltpu.SMEM)]
    out_specs = [
        pl.BlockSpec((block, width), lambda i: (i, 0)),
        pl.BlockSpec((heads, 1, length, block), lambda i: (0, i, 0, 0)),
        pl.BlockSpec((heads, 1, 8, block), lambda i: (0, i, 0, 0)),
    ] + [pl.BlockSpec((rows, width), lambda i: (0, 0))] * cuts
    out_shape = [
        jax.ShapeDtypeStruct((length, width), BF),
        jax.ShapeDtypeStruct((heads, count, length, block), BF),
        jax.ShapeDtypeStruct((heads, count, 8, block), F32),
    ] + [jax.ShapeDtypeStruct((rows, width), BF)] * cuts
    scratch = [
        pltpu.VMEM((heads, length, 256), BF),
        pltpu.VMEM((heads, HD + 16, length), BF),
        pltpu.VMEM((heads, length, block), F32),
    ]
    if source is not None:
        down, up, xs, ws, height = source
        parts = len(xs)
        counts = [w.shape[0] // height for w in ws]
        model = sum(w.shape[0] for w in ws)
        all_heads = ws[0].shape[1] // 3
        args = [down, up, *xs, *ws]
        in_specs += [vmem] * 2 + [anywhere] * (parts + len(ws))
        out_specs += [anywhere] * 3 + [vmem, anywhere]
        out_shape += [jax.ShapeDtypeStruct((length, all_heads), BF)] * 3
        out_shape += [jax.ShapeDtypeStruct((length, down.shape[0]), BF)]
        out_shape += [jax.ShapeDtypeStruct((model, 3 * all_heads), BF)]
        scratch += [
            pltpu.VMEM((length, model), BF),
            pltpu.VMEM((model, 3 * all_heads), BF),
            pltpu.VMEM((3, length, all_heads), BF),
            pltpu.SemaphoreType.DMA((parts,)),
            pltpu.SemaphoreType.DMA,
            pltpu.SemaphoreType.DMA((3,)),
            pltpu.SemaphoreType.DMA,
        ]
    else:
        parts = 0
        counts = []
        args = list(qkv)
        in_specs += [
            pl.BlockSpec((block, width), lambda i: (i, group)),
            pl.BlockSpec((length, width), lambda i: (0, group)),
            pl.BlockSpec((length, width), lambda i: (0, group)),
        ]
    return pl.pallas_call(
        functools.partial(
            attend_forward_kernel, heads, block, chunk, rows, group, cuts, parts, counts
        ),
        grid=(count,),
        in_specs=in_specs,
        out_specs=out_specs,
        out_shape=out_shape,
        scratch_shapes=scratch,
        compiler_params=pltpu.CompilerParams(
            vmem_limit_bytes=VMEM_LIMIT, dimension_semantics=("arbitrary",)
        ),
        cost_estimate=BRIEF,
        name="project_attend_forward" if parts else "attend_forward",
    )(lengths, *args)


def attend_backward_kernel(
    heads, block, chunk, cuts, q_ref, k_ref, v_ref, o_ref, e_ref, l_ref, *rest
):
    cut_refs = rest[0:cuts]
    dq_ref, dk_ref, dv_ref, do_rows_ref, values_wide, keys_t, dk_sum, dv_sum = rest[cuts:]
    length = k_ref.shape[0]
    rows = length // cuts
    width = heads * HD
    i = pl.program_id(0)
    for k in range(cuts):

        @pl.when(i == k * rows // block)
        def _():
            begin = k * rows % block
            do_rows_ref[begin : begin + rows, :] = cut_refs[k][...]

    @pl.when(i == 0)
    def _():
        ones = (lax.broadcasted_iota(jnp.int32, (length, 128), 1) < 2).astype(BF)
        for h in range(heads):
            value = v_ref[:, h * HD : (h + 1) * HD]
            values_wide[h, :, 0:HD] = value
            values_wide[h, :, HD : 2 * HD] = value
            values_wide[h, :, 2 * HD :] = ones
        keys_t[...] = k_ref[...].T
        dk_sum[...] = jnp.zeros_like(dk_sum)
        dv_sum[...] = jnp.zeros_like(dv_sum)

    q = q_ref[...]
    flipped_do = do_rows_ref[...].astype(F32).T
    flipped_o = o_ref[...].astype(F32).T
    lane = lax.broadcasted_iota(jnp.int32, (block, width), 1)
    row = lax.broadcasted_iota(jnp.int32, (128, block), 0)
    grads = []
    for h in range(heads):
        own = slice(h * HD, (h + 1) * HD)
        inverse = 1.0 / l_ref[h, 0, 0:1, :]
        dot = -jnp.sum(flipped_do[own] * flipped_o[own], axis=0, keepdims=True) * inverse
        scaled = flipped_do[own] * inverse
        high = scaled.astype(BF)
        low = (scaled - high.astype(F32)).astype(BF)
        dot_high = dot.astype(BF)
        dot_low = (dot - dot_high.astype(F32)).astype(BF)
        dots = jnp.where(row == 0, dot_high, jnp.where(row == 1, dot_low, jnp.zeros_like(dot_low)))
        right = jnp.concatenate([high, low, dots], axis=0)
        do_rows = high.T
        if heads == 2:
            empty = jnp.zeros_like(do_rows)
            do_rows = jnp.concatenate([do_rows, empty] if h == 0 else [empty, do_rows], axis=1)
        query = jnp.where((lane >= h * HD) & (lane < (h + 1) * HD), q, jnp.zeros_like(q))
        total = None
        for c in range(length // chunk):
            rows = slice(c * chunk, (c + 1) * chunk)
            e = e_ref[h, 0, rows, :]
            part = mm(values_wide[h, rows, :], right)
            ds = (e.astype(F32) * part).astype(BF)
            dv_sum[rows, :] += mm(e, do_rows)
            dk_sum[rows, :] += mm(ds, query)
            part = mm(keys_t[own, rows], ds)
            total = part if total is None else total + part
        grads.append(total * HD ** (-0.5))
    dq_ref[...] = jnp.concatenate(grads, axis=0).T.astype(BF)

    @pl.when(i == pl.num_programs(0) - 1)
    def _():
        dk_ref[...] = (dk_sum[...] * HD ** (-0.5)).astype(BF)
        dv_ref[...] = dv_sum[...].astype(BF)


def attend_backward(q, k, v, att, d_att, e, row_sum, group, heads):
    length = q.shape[0]
    width = heads * HD
    block = e.shape[3]
    cuts = len(d_att)
    rows = length // cuts
    chunk = min(512, length)
    count = length // block
    whole = pl.BlockSpec((length, width), lambda i: (0, group))
    return pl.pallas_call(
        functools.partial(attend_backward_kernel, heads, block, chunk, cuts),
        grid=(count,),
        in_specs=[
            pl.BlockSpec((block, width), lambda i: (i, group)),
            whole,
            whole,
            pl.BlockSpec((block, width), lambda i: (i, 0)),
            pl.BlockSpec((heads, 1, length, block), lambda i: (0, i, 0, 0)),
            pl.BlockSpec((heads, 1, 8, block), lambda i: (0, i, 0, 0)),
        ]
        + [pl.BlockSpec((rows, width), lambda i: (0, group))] * cuts,
        out_specs=[
            pl.BlockSpec((block, width), lambda i: (i, 0)),
            pl.BlockSpec((length, width), lambda i: (0, 0)),
            pl.BlockSpec((length, width), lambda i: (0, 0)),
        ],
        out_shape=[jax.ShapeDtypeStruct((length, width), BF)] * 3,
        scratch_shapes=[
            pltpu.VMEM((block, width), BF),
            pltpu.VMEM((heads, length, 256), BF),
            pltpu.VMEM((width, length), BF),
            pltpu.VMEM((length, width), F32),
            pltpu.VMEM((length, width), F32),
        ],
        compiler_params=pltpu.CompilerParams(
            vmem_limit_bytes=VMEM_LIMIT, dimension_semantics=("arbitrary",)
        ),
        cost_estimate=BRIEF,
        name="attend_backward",
    )(q, k, v, att, e, row_sum, *d_att)


def normal_parts(z):
    density = jnp.exp2(z * z * (-0.5 * LOG2E))
    t = 1.0 / (1.0 + (0.3275911 * 0.5**0.5) * jnp.abs(z))
    poly = t * (
        0.254829592 * 0.5
        + t
        * (
            -0.284496736 * 0.5
            + t * (1.421413741 * 0.5 + t * (-1.453152027 * 0.5 + t * (1.061405429 * 0.5)))
        )
    )
    tail = poly * density
    return jnp.where(z < 0.0, tail, 1.0 - tail), density * 0.3989422804014327


def normalize(values):
    center = values - jnp.mean(values, axis=-1, keepdims=True)
    scale = lax.rsqrt(jnp.mean(center * center, axis=-1, keepdims=True) + EPS)
    return center * scale, scale


def normalize_back(e, normal, scale):
    return scale * (
        e
        - jnp.mean(e, axis=-1, keepdims=True)
        - normal * jnp.mean(e * normal, axis=-1, keepdims=True)
    )


def assemble_kernel(rank, share, used, sets, down_ref, up_ref):
    ranks = 3 * rank
    count, tail = sets.shape[0], used - ranks
    for k in range(count):
        down_ref[:, k * 128 : (k + 1) * 128] = sets[k, 0:ranks, :]
    row = lax.broadcasted_iota(jnp.int32, (ranks, tail), 0)
    source = lax.broadcasted_iota(jnp.int32, (ranks, tail), 1)
    for j in range(3):
        for half in range(2):
            total = None
            for k in range(count):
                wanted = row < 0
                for r in range(share):
                    target = j * rank + k * share + r
                    wanted = wanted | (
                        (row == target) & (source == (j * share + r) * 2 + half)
                    )
                part = mm(jnp.where(wanted, 1.0, 0.0).astype(BF), sets[k, ranks:used, :])
                total = part if total is None else total + part
            begin = (j * 2 + half) * 128
            up_ref[:, begin : begin + 128] = total.astype(BF)


def assemble(sets, rank, share, used):
    count = sets.shape[0]
    vmem = pl.BlockSpec(memory_space=pltpu.VMEM)
    return pl.pallas_call(
        functools.partial(assemble_kernel, rank, share, used),
        in_specs=[vmem],
        out_specs=[vmem] * 2,
        out_shape=[
            jax.ShapeDtypeStruct((3 * rank, count * 128), BF),
            jax.ShapeDtypeStruct((3 * rank, 6 * 128), BF),
        ],
        name="assemble",
    )(sets)


def unproject_kernel(parts, groups, u_ref, w_ref, down_ref, up_ref, *rest):
    x_hbm = rest[0:parts]
    grads = rest[parts : parts + 3 * groups]
    stay_ref, go_ref, g_up_ref, g_down_ref, x, x_sem = rest[parts + 3 * groups :]
    width = w_ref.shape[1] // 3
    step = pl.program_id(0)
    rows = x.shape[1]
    copies = [pltpu.make_async_copy(x_hbm[i], x.at[i], x_sem.at[i]) for i in range(parts)]

    @pl.when(step == 0)
    def _():
        for copy in copies:
            copy.start()
        g_up_ref[...] = jnp.zeros_like(g_up_ref)
        g_down_ref[...] = jnp.zeros_like(g_down_ref)

    values = [
        jnp.concatenate([grads[g * 3 + j][...] for g in range(groups)], axis=1) for j in range(3)
    ]
    d_u = None
    for j in range(3):
        part = mm_nt(values[j], up_ref[:, j * width : (j + 1) * width])
        d_u = part if d_u is None else d_u + part
    d_u = d_u.astype(BF)
    total = mm(d_u, down_ref[...])
    for j in range(3):
        total = total + mm_nt(values[j], w_ref[:, j * width : (j + 1) * width])
    total = total.astype(BF)

    @pl.when(step < parts // 2)
    def _():
        stay_ref[...] = total

    @pl.when(step >= parts // 2)
    def _():
        go_ref[...] = total

    u_t = transpose_small(u_ref[...])
    for j in range(3):
        g_up_ref[:, j * width : (j + 1) * width] += mm(u_t, values[j])
    for i in range(parts):

        @pl.when(step == i)
        def _():
            copies[i].wait()

    g_down_ref[...] += mm(transpose_small(d_u), x[step])


def unproject(grads, u, w, down, up, xs, odd):
    model = w.shape[0]
    width = w.shape[1] // 3
    rows = xs[0].shape[0]
    steps = len(xs)
    ranks = down.shape[0]
    grads = [value for group in grads for value in group]
    vmem = pl.BlockSpec(memory_space=pltpu.VMEM)
    return pl.pallas_call(
        functools.partial(unproject_kernel, steps, len(grads) // 3),
        grid=(steps,),
        in_specs=[pl.BlockSpec((rows, ranks), lambda i: (2 * i + odd, 0))]
        + [vmem] * 3
        + [pl.BlockSpec(memory_space=pl.ANY)] * steps
        + [pl.BlockSpec((rows, g.shape[1]), lambda i: (2 * i + odd, 0)) for g in grads],
        out_specs=[
            pl.BlockSpec((rows, model), lambda i: (jnp.minimum(i, steps // 2 - 1), 0)),
            pl.BlockSpec((rows, model), lambda i: (jnp.maximum(i - steps // 2, 0), 0)),
            vmem,
            vmem,
        ],
        out_shape=[
            jax.ShapeDtypeStruct((rows * steps // 2, model), BF),
            jax.ShapeDtypeStruct((rows * steps // 2, model), BF),
            jax.ShapeDtypeStruct((ranks, 3 * width), F32),
            jax.ShapeDtypeStruct((ranks, model), F32),
        ],
        scratch_shapes=[
            pltpu.VMEM((steps, rows, model), BF),
            pltpu.SemaphoreType.DMA((steps,)),
        ],
        compiler_params=pltpu.CompilerParams(
            vmem_limit_bytes=VMEM_LIMIT, dimension_semantics=("arbitrary",)
        ),
        cost_estimate=BRIEF,
        name="unproject",
    )(u, w, down, up, *xs, *grads)


def middle_kernel(
    cuts, parts, counts, sizes, hidden_block, x_ref, cot_ref,
    down_out, up_out, down_fc1, up_fc1, down_fc2, up_fc2, gain1, bias1, gain2, bias2, *rest
):
    att_hbm = rest[0:parts]
    rest = rest[parts:]
    first_hbm = rest[0 : len(counts)]
    second_hbm = rest[len(counts) : 2 * len(counts)]
    rest = rest[2 * len(counts) :]
    out_ref, dy1_ref = rest[0:2]
    d_att_refs = rest[2 : 2 + cuts]
    (
        g_up_fc2, g_down_fc2, g_up_fc1, g_down_fc1, g_up_out, g_down_out,
        att_own, wo_t, w1, w2_t, hidden, slope, normal1, normed, low_rows, total,
        att_sem, wo_sem, w1_sem, w2_sem,
    ) = rest[2 + cuts :]
    rows, model = x_ref.shape
    units = w1.shape[1]
    height, wide, narrow = sizes
    mine = lax.axis_index("tensor")
    n_t = lax.axis_size("tensor")
    order = cut_order(n_t)
    places = spread_places() if sum(counts) > 1 else [(0, 0)]

    def fetch(source, j, begin, width, target, row, col, sem):
        pltpu.make_async_copy(
            source.at[j * height : (j + 1) * height, begin : begin + width],
            target.at[
                pl.ds(pl.multiple_of(row * height, height), height),
                pl.ds(pl.multiple_of(col * width, width), width),
            ],
            sem,
        ).start()

    def each_block():
        block = 0
        for i, count in enumerate(counts):
            for j in range(count):
                yield (i, j) + places[block]
                block += 1

    if parts > 1:
        width = att_hbm[0].shape[1]
        groups = parts // n_t
        for k in range(n_t):
            for g in range(groups):
                col = pl.multiple_of(((mine ^ order[k]) * groups + g) * width, width)
                pltpu.make_async_copy(
                    att_hbm[k * groups + g], att_own.at[:, pl.ds(col, width)], att_sem
                ).start()
    else:
        pltpu.make_async_copy(att_hbm[0], att_own, att_sem).start()
    for i, j, row, col in each_block():
        fetch(first_hbm[i], j, wide, narrow, wo_t, row, col, wo_sem)
    for i, j, row, col in each_block():
        fetch(first_hbm[i], j, 0, wide, w1, row, col, w1_sem.at[col])
    for i, j, row, col in each_block():
        fetch(second_hbm[i], j, 0, wide, w2_t, row, col, w2_sem.at[col])

    pltpu.make_async_copy(att_own, att_own, att_sem).wait()
    pltpu.make_async_copy(wo_t, wo_t, wo_sem).wait()
    att = att_own[...]
    u_out = mm_nt(att, down_out[...]).astype(BF)
    first = x_ref[...].astype(F32) + mm_nt(att, wo_t[...]) + mm(u_out, up_out[...])
    normal, scale1 = normalize(first)
    normal1[...] = normal
    full = normal * gain1[...].astype(F32) + bias1[...].astype(F32)
    normed[...] = full
    low_rows[...] = full.astype(BF)
    u_fc1 = mm_nt(low_rows[...], down_fc1[...]).astype(BF)

    blocks = units // hidden_block
    per_cut = wide // hidden_block

    def before(i):
        cols = slice(i * hidden_block, (i + 1) * hidden_block)
        if i % per_cut == 0:
            b = i // per_cut
            for target, sem in ((w1, w1_sem), (w2_t, w2_sem)):
                view = target.at[:, b * wide : (b + 1) * wide]
                pltpu.make_async_copy(view, view, sem.at[b]).wait()
        return mm(low_rows[...], w1[:, cols]) + mm(u_fc1, up_fc1[:, cols])

    z = before(0)
    u_sum = None
    for i in range(blocks):
        cols = slice(i * hidden_block, (i + 1) * hidden_block)
        following = before(i + 1) if i + 1 < blocks else None
        phi_sum, phi = normal_parts(z)
        act = (z * phi_sum).astype(BF)
        hidden[:, cols] = act
        slope[:, cols] = phi_sum + z * phi
        part = mm_nt(act, w2_t[:, cols])
        total[...] = part if i == 0 else total[...] + part
        part = mm_nt(act, down_fc2[:, cols])
        u_sum = part if u_sum is None else u_sum + part
        z = following
    u_fc2 = u_sum.astype(BF)
    second = normed[...] + total[...] + mm(u_fc2, up_fc2[...])
    normal2, scale2 = normalize(second)
    gain = gain2[...].astype(F32)
    out_ref[...] = (normal2 * gain + bias2[...].astype(F32)).astype(BF)
    d_second = normalize_back(cot_ref[...].astype(F32) * gain, normal2, scale2)
    total[...] = d_second
    d_ffn = d_second.astype(BF)
    d_u2 = mm_nt(d_ffn, up_fc2[...]).astype(BF)
    d_u2_t = transpose_small(d_u2)
    g_up_fc2[...] = mm(transpose_small(u_fc2), d_ffn).astype(BF)
    u_fc1_t = transpose_small(u_fc1)

    def before_back(i):
        cols = slice(i * hidden_block, (i + 1) * hidden_block)
        return mm(d_ffn, w2_t[:, cols]) + mm(d_u2, down_fc2[:, cols])

    d_hidden = before_back(0)
    u_sum = None
    for i in range(blocks):
        cols = slice(i * hidden_block, (i + 1) * hidden_block)
        following = before_back(i + 1) if i + 1 < blocks else None
        d_pre = (d_hidden * slope[:, cols]).astype(BF)
        g_down_fc2[:, cols] = mm(d_u2_t, hidden[:, cols]).astype(BF)
        g_up_fc1[:, cols] = mm(u_fc1_t, d_pre).astype(BF)
        total[...] += mm_nt(d_pre, w1[:, cols])
        part = mm_nt(d_pre, up_fc1[:, cols])
        u_sum = part if u_sum is None else u_sum + part
        d_hidden = following
    d_u1 = u_sum.astype(BF)
    d_normed = total[...] + mm(d_u1, down_fc1[...])
    g_down_fc1[...] = mm(transpose_small(d_u1), low_rows[...]).astype(BF)
    d_first = normalize_back(d_normed * gain1[...].astype(F32), normal1[...], scale1)
    dy1_ref[...] = d_first
    d_a = d_first.astype(BF)
    d_uo = mm_nt(d_a, up_out[...]).astype(BF)
    g_up_out[...] = mm(transpose_small(u_out), d_a).astype(BF)
    g_down_out[...] = mm(transpose_small(d_uo), att).astype(BF)
    att_own[...] = (mm(d_a, wo_t[...]) + mm(d_uo, down_out[...])).astype(BF)
    width = model // cuts
    for k in range(cuts):
        col = pl.multiple_of((mine ^ order[k]) * width, width) if cuts > 1 else 0
        d_att_refs[k][...] = att_own[:, pl.ds(col, width)]


def cut_order(n_t):
    order = [0]
    bit = n_t // 2
    while bit:
        order = order + [k ^ bit for k in order]
        bit //= 2
    return order


def middle(atts, cuts, x, cot, adapters, norms, firsts, seconds, sizes):
    rows, model = x.shape
    rank, units = adapters[3].shape
    height, wide, narrow = sizes
    counts = [value.shape[0] // height for value in firsts]
    hidden_block = min(512, wide)
    cols = units // wide
    vmem = pl.BlockSpec(memory_space=pltpu.VMEM)
    anywhere = pl.BlockSpec(memory_space=pl.ANY)
    long = jax.ShapeDtypeStruct((rank, units), BF)
    short = jax.ShapeDtypeStruct((rank, model), BF)
    out_shape = (
        [jax.ShapeDtypeStruct((rows, model), BF), jax.ShapeDtypeStruct((rows, model), F32)]
        + [jax.ShapeDtypeStruct((rows, model // cuts), BF)] * cuts
        + [short, long, long, short, short, short]
    )
    return pl.pallas_call(
        functools.partial(middle_kernel, cuts, len(atts), counts, sizes, hidden_block),
        in_specs=[vmem] * 12 + [anywhere] * (len(atts) + len(firsts) + len(seconds)),
        out_specs=[vmem] * len(out_shape),
        out_shape=out_shape,
        scratch_shapes=[
            pltpu.VMEM((rows, model), BF),
            pltpu.VMEM((model, model), BF),
            pltpu.VMEM((model, units), BF),
            pltpu.VMEM((model, units), BF),
            pltpu.VMEM((rows, units), BF),
            pltpu.VMEM((rows, units), F32),
            pltpu.VMEM((rows, model), F32),
            pltpu.VMEM((rows, model), F32),
            pltpu.VMEM((rows, model), BF),
            pltpu.VMEM((rows, model), F32),
            pltpu.SemaphoreType.DMA,
            pltpu.SemaphoreType.DMA,
            pltpu.SemaphoreType.DMA((cols,)),
            pltpu.SemaphoreType.DMA((cols,)),
        ],
        compiler_params=pltpu.CompilerParams(vmem_limit_bytes=VMEM_LIMIT),
        cost_estimate=BRIEF,
        name="middle",
    )(x, cot, *adapters, *norms, *atts, *firsts, *seconds)


class Spread:
    def __init__(self):
        self.n_dp, self.n_t = lax.axis_size("dp"), lax.axis_size("tensor")
        self.devices = [(d, t) for d in range(self.n_dp) for t in range(self.n_t)]

    def send(self, value, target):
        n_t = self.n_t
        pairs = []
        for d, t in self.devices:
            to_d, to_t = target(d, t)
            pairs.append((d * n_t + t, to_d * n_t + to_t))
        return lax.ppermute(value, ("dp", "tensor"), pairs)

    def ring(self, value):
        return self.send(value, lambda d, t: ((d + 2) % self.n_dp, t))

    def along_z(self, value):
        count = self.n_dp // 2
        return [value] + [
            self.send(value, lambda d, t, j=j: ((d + 2 * j) % self.n_dp, t))
            for j in range(1, count)
        ]

    def cross(self, value, core):
        return self.send(value, lambda d, t: (d ^ 1, t) if t % 2 == core else (d, t ^ 2))

    def core(self, value):
        return self.send(value, lambda d, t: (d, t ^ 1))


def spread_places():
    n_dp = lax.axis_size("dp")
    d = lax.axis_index("dp")
    mine = lax.axis_index("tensor")
    found = []
    for t in (mine, mine ^ 1):
        even = (t % 2) == 0
        for to_d, to_t in (
            (d, t),
            (jnp.where(even, d ^ 1, d), jnp.where(even, t, t ^ 2)),
            (jnp.where(even, d, d ^ 1), jnp.where(even, t ^ 2, t)),
            (d ^ 1, t ^ 2),
        ):
            found += [((to_d + n_dp - 2 * j) % n_dp, to_t) for j in range(n_dp // 2)]
    return found


def shards(
    inputs, cotangent, lengths, adapter_index, w_qkv, w_out, w_fc1, w_fc2,
    ln1_gain, ln1_bias, ln2_gain, ln2_bias, down_qkv, up_qkv, down_out, up_out,
    down_fc1, up_fc1, down_fc2, up_fc2,
):
    n_dp = lax.axis_size("dp")
    n_t = lax.axis_size("tensor")
    every = ("dp", "tensor")
    mine = lax.axis_index("tensor")
    rows, model = inputs.shape
    length = rows * n_t
    n_set = down_qkv.shape[1]
    rank = down_qkv.shape[3]
    r_dp = rank // n_dp
    r_t = rank // n_t
    d_dp = model // n_dp
    c_t = model // n_t
    f_t = w_fc1.shape[1]
    f_all = f_t * n_t

    def swap(value, bit):
        return lax.ppermute(value, "tensor", [(i, i ^ bit) for i in range(n_t)])

    bits = []
    bit = n_t // 2
    while bit:
        bits.append(bit)
        bit //= 2
    order = cut_order(n_t)

    x_parts = [inputs]
    for bit in bits[:-1]:
        x_parts = x_parts + [swap(part, bit) for part in x_parts]

    w_local = w_qkv.transpose(1, 0, 2).reshape(d_dp, 3 * c_t)
    packed_second = w_fc2.T
    staged = n_dp == 8 and n_t == 4
    if staged:
        spread = Spread()
        packed = jnp.concatenate([w_fc1, w_out.T, w_local], axis=1)
        hops = [packed, spread.ring(packed)]
        block_sizes = (d_dp, f_t, c_t)
    else:

        def whole(value):
            blocks = lax.all_gather(value, every, axis=0).reshape(n_dp, n_t, d_dp, -1)
            return blocks.transpose(0, 2, 1, 3).reshape(model, -1)

        firsts = [jnp.concatenate([whole(w_fc1), whole(w_out.T)], axis=1)]
        seconds = [whole(packed_second)]
        w_parts = [lax.all_gather(w_local, "dp", axis=0, tiled=True)]
        w_height = model
        block_sizes = (model, f_all, model)

    index_all = lax.all_to_all(
        jnp.broadcast_to(adapter_index, (n_dp,)), "dp", 0, 0, tiled=True
    )
    onehot_all = (index_all[:, None] == jnp.arange(n_set, dtype=jnp.int32)[None, :]).astype(BF)
    def part_of_rank(value):
        return lax.dynamic_slice_in_dim(value, mine * r_t, r_t, 1)

    down_t = down_qkv.transpose(1, 0, 3, 2).reshape(n_set, 3 * rank, d_dp)
    up_first = up_qkv.transpose(1, 0, 2, 3)
    tables = [
        down_out.transpose(0, 2, 1),
        part_of_rank(up_out),
        part_of_rank(down_fc1.transpose(0, 2, 1)),
        up_fc1,
        down_fc2.transpose(0, 2, 1),
        part_of_rank(up_fc2),
    ]
    sizes = [t.size // n_set for t in tables]
    norm_part = jnp.stack([ln1_gain, ln1_bias, ln2_gain, ln2_bias])
    in_rows = staged and d_dp == 128 and c_t == 256
    if in_rows:
        parts = [down_t, up_first.reshape(n_set, -1, 128)]
        parts.append(jnp.zeros((n_set, -parts[1].shape[1] % 16, 128), BF))
        qkv_rows = sum(p.shape[1] for p in parts)
        parts += [t.reshape(n_set, -1, 128) for t in tables]
        parts.append(jnp.broadcast_to(norm_part, (n_set, 4, d_dp)))
        parts.append(jnp.zeros((n_set, -sum(p.shape[1] for p in parts) % 16, 128), BF))
        table = jnp.concatenate(parts, axis=1)
        sets = jnp.einsum("ns,srl->nrl", onehot_all, table, preferred_element_type=F32).astype(BF)
        hops[1], sets = lax.optimization_barrier((hops[1], sets))
        hops.append(spread.ring(hops[1]))
        sets = lax.all_to_all(sets, "dp", 0, 0, tiled=True)
        hops[2], sets, packed_second = lax.optimization_barrier((hops[2], sets, packed_second))
        hops.append(spread.ring(hops[2]))
        second = spread.along_z(packed_second)
        sel_down_qkv, sel_up_qkv = assemble(sets, rank, r_dp, qkv_rows)
        begin = qkv_rows + sum(sizes) // 128
        came = sets[:, qkv_rows:begin]
        norms = sets[:, begin : begin + 4].transpose(1, 0, 2).reshape(4, 1, model)
    else:
        flat = [t.reshape(n_set, -1) for t in (down_t, up_first, *tables)]
        flat.append(jnp.broadcast_to(norm_part.reshape(1, -1), (n_set, 4 * d_dp)))
        table = jnp.concatenate(flat, axis=1)
        sets = lax.all_to_all(mm(onehot_all, table).astype(BF), "dp", 0, 0, tiled=True)
        cut = 3 * rank * d_dp
        cut_up = cut + up_first.size // n_set
        sel_down_qkv = (
            sets[:, :cut].reshape(n_dp, 3 * rank, d_dp).transpose(1, 0, 2).reshape(3 * rank, model)
        )
        up_cols = sets[:, cut:cut_up].reshape(n_dp, 3, r_dp, c_t).transpose(1, 0, 2, 3)
        same = jnp.eye(3, dtype=BF).reshape(3, 1, 3, 1)
        sel_up_qkv = (up_cols.reshape(3, rank, 1, c_t) * same).reshape(3 * rank, 3 * c_t)
        came = sets[:, cut_up : cut_up + sum(sizes)]
        norms = sets[:, cut_up + sum(sizes) :].reshape(n_dp, 4, d_dp)
        norms = norms.transpose(1, 0, 2).reshape(4, 1, model)
    shares = [came]
    for bit in bits:
        shares = shares + [swap(share, bit) for share in shares]
    of_owner = jnp.array([order.index(k) for k in range(n_t)], jnp.int32)
    of_owner = of_owner[jnp.arange(n_t, dtype=jnp.int32) ^ mine]

    def make_adapters(shares):
        came = []
        for t in range(n_t):
            value = shares[0]
            for k in range(1, n_t):
                value = jnp.where((mine ^ order[k]) == t, shares[k], value)
            came.append(value)
        came = jnp.stack(came).reshape(n_t, n_dp, -1)
        pieces = []
        start = 0
        for size in sizes:
            pieces.append(came[:, :, start : start + size])
            start += size

        def from_rank_parts(piece):
            return piece.reshape(n_t, n_dp, r_t, d_dp).transpose(0, 2, 1, 3).reshape(rank, model)

        def from_blocks(piece, width):
            return (
                piece.reshape(n_t, n_dp, r_dp, width)
                .transpose(1, 2, 0, 3)
                .reshape(rank, n_t * width)
            )

        return [
            from_blocks(pieces[0], c_t),
            from_rank_parts(pieces[1]),
            from_rank_parts(pieces[2]),
            from_blocks(pieces[3], f_t),
            from_blocks(pieces[4], f_t),
            from_rank_parts(pieces[5]),
        ]

    x_parts = x_parts + [swap(part, bits[-1]) for part in x_parts]
    if staged:
        w_near = jnp.concatenate([hop[:, f_t + c_t :] for hop in hops], axis=0)
        w_parts = [w_near, lax.ppermute(w_near, "dp", [(i, i ^ 1) for i in range(n_dp)])]
        w_height = d_dp
        first = jnp.concatenate([hop[:, : f_t + c_t] for hop in hops], axis=0)
        first_one = spread.cross(first, 0)
        first_two = spread.cross(first, 1)
        second = jnp.concatenate(second, axis=0)
        first, second, x_parts, shares, w_parts = lax.optimization_barrier(
            (first, second, x_parts, shares, w_parts)
        )
        second_one = spread.cross(second, 0)
        second_two = spread.cross(second, 1)
    heads = c_t // HD
    group_heads = 2 if heads % 2 == 0 else 1
    groups = heads // group_heads
    kept = []
    att_parts = [[] for _ in range(n_t)]
    for g in range(groups):
        if g == 0:
            att, e, row_sum, *more = attend_forward(
                lengths, g, group_heads, rows, n_t,
                source=(sel_down_qkv, sel_up_qkv, x_parts, w_parts, w_height),
            )
            cut_rows, qkv, u_in, w_cols = more[:n_t], more[n_t : n_t + 3], *more[n_t + 3 :]
        else:
            if staged and g == 1:
                near = [first, first_one, first_two, second, second_one, second_two]
                qkv, near = lax.optimization_barrier((qkv, near))
                first_both = spread.cross(near[1], 1)
                second_both = spread.cross(near[4], 1)
                over = [spread.core(value) for value in near]
            att, e, row_sum, *cut_rows = attend_forward(
                lengths, g, group_heads, rows, n_t, qkv=qkv
            )
        kept.append((att, e, row_sum))
        for k in range(n_t):
            att_parts[k].append(cut_rows[k] if order[k] == 0 else swap(cut_rows[k], order[k]))
    atts = [part for parts in att_parts for part in parts]

    if staged:
        kept, over, first_both, second_both, shares = lax.optimization_barrier(
            (kept, over, first_both, second_both, shares)
        )
        firsts = near[:3] + [first_both] + over[:3] + [spread.core(first_both)]
        seconds = near[3:] + [second_both] + over[3:] + [spread.core(second_both)]
    adapters = make_adapters(shares)
    blocks_fit = c_t % 128 == 0
    if not blocks_fit:
        by_cut = jnp.concatenate(atts, axis=1).reshape(rows, n_t, c_t)
        atts = [jnp.take(by_cut, of_owner, axis=1).reshape(rows, model)]
    cuts = n_t if blocks_fit else 1
    done = middle(
        atts, cuts, inputs, cotangent, adapters, list(norms), firsts, seconds, block_sizes
    )
    output, d_first = done[0:2]
    d_att_blocks = done[2 : 2 + cuts]
    if not blocks_fit:
        by_owner = d_att_blocks[0].reshape(rows, n_t, c_t)
        d_att_blocks = [
            lax.dynamic_index_in_dim(by_owner, mine ^ order[k], 1, keepdims=False)
            for k in range(n_t)
        ]
    g_up_fc2, g_down_fc2, g_up_fc1, g_down_fc1, g_up_out, g_down_out = done[2 + cuts :]

    def share_cols(value):
        lead = value.size // model
        return (
            value.reshape(lead, n_dp, n_t, model // (n_dp * n_t))
            .transpose(1, 2, 0, 3)
            .reshape(n_dp * n_t, -1)
        )

    def share_blocks(value):
        width = value.shape[1] // n_t
        return (
            value.reshape(n_dp, r_dp, n_t, width).transpose(0, 2, 1, 3).reshape(n_dp * n_t, -1)
        )

    d_att_all = [
        d_att_blocks[k] if order[k] == 0 else swap(d_att_blocks[k], order[k]) for k in range(n_t)
    ]
    near_cut = order.index(1)
    adapter_grads = [g_down_out, g_up_out, g_down_fc1, g_up_fc1, g_down_fc2, g_up_fc2]
    d_att_all[near_cut], adapter_grads = lax.optimization_barrier(
        (d_att_all[near_cut], adapter_grads)
    )
    g_down_out, g_up_out, g_down_fc1, g_up_fc1, g_down_fc2, g_up_fc2 = adapter_grads
    early = [
        share_blocks(g_down_out),
        share_cols(g_up_out),
        share_cols(g_down_fc1),
        share_blocks(g_up_fc1),
        share_blocks(g_down_fc2),
        share_cols(g_up_fc2),
    ]
    early = jnp.concatenate(early, axis=1)

    d_att_all, early = lax.optimization_barrier((d_att_all, early))
    grads = []
    for g in range(groups):
        if g == groups - 1:
            d_att_all, grads, early = lax.optimization_barrier((d_att_all, grads, early))
            early_got = lax.all_to_all(early, every, 0, 0, tiled=True)
        grads.append(
            attend_backward(*qkv, kept[g][0], d_att_all, kept[g][1], kept[g][2], g, group_heads)
        )
    grads, early_got = lax.optimization_barrier((grads, early_got))

    def partly(odd):
        stay, go, g_up, g_down = unproject(
            grads, u_in, w_cols, sel_down_qkv, sel_up_qkv, x_parts[odd::2], odd
        )
        value = [stay, swap(go, bits[-1])]
        for bit in reversed(bits[1:-1]):
            value = sum(v.astype(F32) for v in value).astype(BF)
            half = value.shape[0] // 2
            value = [value[:half], swap(value[half:], bit)]
        return value, g_up, g_down

    odd_sum, g_up_other, g_down_other = partly(1)
    odd_sum = (odd_sum[0].astype(F32) + odd_sum[1].astype(F32)).astype(BF)
    grads, odd_sum = lax.optimization_barrier((grads, odd_sum))
    cut = rows // 2
    far_first = swap(odd_sum[:cut], bits[0])
    even_sum, g_up_own, g_down_own = partly(0)
    here = d_first + even_sum[0].astype(F32) + even_sum[1].astype(F32)

    g_down_qkv = (g_down_own + g_down_other).astype(BF)
    g_up_all = (g_up_own + g_up_other).astype(BF)
    g_up_qkv = jnp.stack(
        [
            g_up_all[j * rank : (j + 1) * rank, j * c_t : (j + 1) * c_t]
            for j in range(3)
        ]
    )
    up_share = (
        g_up_qkv.reshape(3, n_dp, r_dp, c_t).transpose(1, 0, 2, 3).reshape(n_dp, 1, -1)
    )
    up_share = jnp.broadcast_to(up_share, (n_dp, n_t, up_share.shape[2])).reshape(n_dp * n_t, -1)
    late = [share_cols(g_down_qkv), up_share]
    late = jnp.concatenate(late, axis=1)
    late, far_first, odd_sum = lax.optimization_barrier((late, far_first, odd_sum))
    far_second = swap(odd_sum[cut:], bits[0])
    late_got = lax.all_to_all(late, every, 0, 0, tiled=True)

    by_sender = jnp.broadcast_to(onehot_all[:, None, :], (n_dp, n_t, n_set)).reshape(-1, n_set)
    same_cols = (jnp.arange(n_dp * n_t, dtype=jnp.int32) % n_t == mine).astype(BF)
    tn = (((0,), (0,)), ((), ()))

    def total(got, weights):
        return lax.dot_general(weights, got, tn, preferred_element_type=F32)

    up_begin = late_got.shape[1] - up_share.shape[1]
    sums = total(early_got, by_sender)
    pieces = []
    start = 0
    for size in sizes:
        pieces.append(sums[:, start : start + size])
        start += size
    d_all = model // (n_dp * n_t)
    sum_down_out = pieces[0].reshape(n_set, r_dp, c_t).transpose(0, 2, 1)
    sum_up_out = pieces[1].reshape(n_set, rank, d_all)
    sum_down_fc1 = pieces[2].reshape(n_set, rank, d_all).transpose(0, 2, 1)
    sum_up_fc1 = pieces[3].reshape(n_set, r_dp, f_t)
    sum_down_fc2 = pieces[4].reshape(n_set, r_dp, f_t).transpose(0, 2, 1)
    sum_up_fc2 = pieces[5].reshape(n_set, rank, d_all)
    sum_down_qkv = (
        total(late_got[:, :up_begin], by_sender)
        .reshape(n_set, 3, rank, d_all)
        .transpose(1, 0, 3, 2)
    )
    sum_up_qkv = (
        total(late_got[:, up_begin:], by_sender * same_cols[:, None])
        .reshape(n_set, 3, r_dp, c_t)
        .transpose(1, 0, 2, 3)
    )
    here, sum_up_fc1 = lax.optimization_barrier((here, sum_up_fc1))
    grad_input = here + jnp.concatenate([far_first, far_second]).astype(F32)
    return (
        output,
        grad_input,
        sum_down_qkv,
        sum_up_qkv,
        sum_down_out,
        sum_up_out,
        sum_down_fc1,
        sum_up_fc1,
        sum_down_fc2,
        sum_up_fc2,
    )


def solution(mesh):
    both = ("dp", "tensor")
    in_specs = (
        P(both, None),
        P(both, None),
        P("dp", None),
        P("dp"),
        P(None, "dp", "tensor"),
        P("tensor", "dp"),
        P("dp", "tensor"),
        P("tensor", "dp"),
        P("dp"),
        P("dp"),
        P("dp"),
        P("dp"),
        P(None, None, "dp", None),
        P(None, None, "dp", "tensor"),
        P(None, "tensor", "dp"),
        P(None, None, "dp"),
        P(None, "dp", None),
        P(None, "dp", "tensor"),
        P(None, "tensor", "dp"),
        P(None, None, "dp"),
    )
    out_specs = (
        P(both, None),
        P(both, None),
        P(None, None, both, None),
        P(None, None, "dp", "tensor"),
        P(None, "tensor", "dp"),
        P(None, None, both),
        P(None, both, None),
        P(None, "dp", "tensor"),
        P(None, "tensor", "dp"),
        P(None, None, both),
    )
    return jax.shard_map(shards, mesh=mesh, in_specs=in_specs, out_specs=out_specs, check_vma=False)
```

```python
import functools

import jax
import jax.numpy as jnp
from jax import lax
from jax.experimental import pallas as pl
from jax.experimental.pallas import tpu as pltpu
from jax.sharding import PartitionSpec as P

HD = 64
EPS = 1e-05
NEG = -1000000000.0
LOG2E = 1.4426950408889634
BF = jnp.bfloat16
F32 = jnp.float32
VMEM_LIMIT = 60 * 2**20
BRIEF = pl.CostEstimate(flops=1, bytes_accessed=1, transcendentals=0)


def mm(left, right):
    return jnp.dot(left, right, preferred_element_type=F32)


def mm_nt(left, right):
    return lax.dot_general(left, right, (((1,), (1,)), ((), ())), preferred_element_type=F32)


def transpose_small(value):
    return value.astype(F32).T.astype(BF)


def token_place(index, rows, cuts, mine):
    shift = rows.bit_length() - 1
    bits = cuts.bit_length() - 1
    block = index >> shift
    reverse = jnp.zeros_like(block)
    for i in range(bits):
        reverse = reverse | (((block >> i) & 1) << (bits - 1 - i))
    return ((reverse ^ mine) << shift) | (index & (rows - 1))


def ring_owners():
    n_dp = lax.axis_size("dp")
    mine = lax.axis_index("dp")
    return [
        (d + n_dp - 2 * j) % n_dp for d in (mine, mine ^ 1) for j in range(n_dp // 2)
    ]


def attend_forward_kernel(
    heads, block, chunk, rows, group, cuts, parts, counts, lengths_ref, *rest
):
    projecting = parts > 0
    if projecting:
        down_ref, up_ref = rest[0:2]
        x_hbm = rest[2 : 2 + parts]
        w_hbm = rest[2 + parts : 2 + parts + len(counts)]
        rest = rest[2 + parts + len(counts) :]
    else:
        q_ref, k_ref, v_ref = rest[0:3]
        rest = rest[3:]
    att_ref, e_ref, l_ref = rest[0:3]
    cut_refs = rest[3 : 3 + cuts]
    rest = rest[3 + cuts :]
    if projecting:
        qkv_hbm, u_ref, w_out_hbm = rest[0:3], rest[3], rest[4]
        keys_wide, values_t, scores, x, w_ref, qkv, x_sem, w_sem, out_sem, w_out_sem = rest[5:]
    else:
        keys_wide, values_t, scores = rest
    length = keys_wide.shape[1]
    width = heads * HD
    mine = lax.axis_index("tensor")
    step = pl.program_id(0)
    steps = pl.num_programs(0)
    ends = [lengths_ref[0, 0]]
    for d in range(1, lengths_ref.shape[1]):
        ends.append(ends[-1] + lengths_ref[0, d])

    @pl.when(step == 0)
    def _():
        if projecting:
            owners = ring_owners() if len(counts) > 1 else [0]
            height = w_ref.shape[0] // sum(counts)
            for i, count in enumerate(counts):
                for j in range(count):
                    row = pl.multiple_of(owners[i * count + j] * height, height)
                    pltpu.make_async_copy(
                        w_hbm[i].at[j * height : (j + 1) * height, :],
                        w_ref.at[pl.ds(row, height), :],
                        w_sem,
                    ).start()
            copies = []
            begin = 0
            for i in range(parts):
                size = x_hbm[i].shape[0]
                copies.append(
                    pltpu.make_async_copy(x_hbm[i], x.at[begin : begin + size], x_sem.at[i])
                )
                copies[-1].start()
                begin += size
        lane = lax.broadcasted_iota(jnp.int32, (1, 128), 1)
        begin = jnp.zeros_like(lane)
        end = jnp.zeros_like(lane)
        for d in range(len(ends)):
            begin = jnp.where(lane == d, ends[d - 1] if d else 0, begin)
            end = jnp.where(lane == d, ends[d], end)
        place = token_place(
            lax.broadcasted_iota(jnp.int32, (length, 128), 0), rows, cuts, mine
        )
        onehot = jnp.where((place >= begin) & (place < end), 1.0, 0.0).astype(BF)
        for h in range(heads):
            keys_wide[h, :, 2 * HD :] = onehot
        if projecting:
            all_heads = qkv.shape[2]
            first = 0
            pltpu.make_async_copy(w_ref, w_ref, w_sem).wait()
            pltpu.make_async_copy(w_ref, w_out_hbm, w_out_sem).start()
            for i in range(parts):
                size = x_hbm[i].shape[0]
                copies[i].wait()
                step_rows = min(512, size)
                for r in range(first, first + size, step_rows):
                    here = x[r : r + step_rows, :]
                    u = mm_nt(here, down_ref[...]).astype(BF)
                    u_ref[r : r + step_rows, :] = u
                    for j in range(3):
                        cols = slice(j * all_heads, (j + 1) * all_heads)
                        qkv[j, r : r + step_rows, :] = (
                            mm(here, w_ref[:, cols]) + mm(u, up_ref[:, cols])
                        ).astype(BF)
                first += size
            for j in range(3):
                pltpu.make_async_copy(qkv.at[j], qkv_hbm[j], out_sem.at[j]).start()
        ones = (lax.broadcasted_iota(jnp.int32, (16, length), 0) == 0).astype(BF)
        values = qkv[2, :, group * width : (group + 1) * width] if projecting else v_ref[...]
        flipped = values.T
        for h in range(heads):
            own = slice(group * width + h * HD, group * width + (h + 1) * HD)
            key = qkv[1, :, own] if projecting else k_ref[:, h * HD : (h + 1) * HD]
            keys_wide[h, :, 0:HD] = key
            keys_wide[h, :, HD : 2 * HD] = key
            values_t[h, 0:HD, :] = flipped[h * HD : (h + 1) * HD, :]
            values_t[h, HD:, :] = ones

    if projecting:
        query_rows = qkv[0, pl.ds(pl.multiple_of(step * block, block), block), :]
        query_rows = query_rows[:, group * width : (group + 1) * width]
    else:
        query_rows = q_ref[...]
    flipped_q = query_rows.astype(F32).T * (HD ** (-0.5) * LOG2E)
    place = token_place(
        lax.broadcasted_iota(jnp.int32, (1, block), 1) + step * block, rows, cuts, mine
    )
    segment = jnp.zeros_like(place)
    for end in ends:
        segment = segment + (place >= end).astype(jnp.int32)
    mask = jnp.where(
        lax.broadcasted_iota(jnp.int32, (128, block), 0) == segment, 0.0, NEG
    ).astype(BF)
    mixed = []
    for h in range(heads):
        query = flipped_q[h * HD : (h + 1) * HD, :]
        high = query.astype(BF)
        low = (query - high.astype(F32)).astype(BF)
        right = jnp.concatenate([high, low, mask], axis=0)
        top = None
        for c in range(length // chunk):
            part = mm(keys_wide[h, c * chunk : (c + 1) * chunk, :], right)
            scores[h, c * chunk : (c + 1) * chunk, :] = part
            part = jnp.max(part.reshape(chunk // 8, 8, block), axis=0)
            top = part if top is None else jnp.maximum(top, part)
        top = jnp.max(top, axis=0, keepdims=True)
        total = None
        for c in range(length // chunk):
            e = jnp.exp2(scores[h, c * chunk : (c + 1) * chunk, :] - top).astype(BF)
            e_ref[h, 0, c * chunk : (c + 1) * chunk, :] = e
            part = mm(values_t[h, :, c * chunk : (c + 1) * chunk], e)
            total = part if total is None else total + part
        row_sum = total[HD : HD + 1, :]
        l_ref[h, 0] = jnp.broadcast_to(row_sum, (8, block))
        mixed.append(total[0:HD, :] / row_sum)
    att = jnp.concatenate(mixed, axis=0).T.astype(BF)
    att_ref[...] = att
    for k in range(cuts):

        @pl.when(step == k * rows // block)
        def _():
            begin = k * rows % block
            cut_refs[k][...] = att[begin : begin + rows, :]

    if projecting:

        @pl.when(step == steps - 1)
        def _():
            for j in range(3):
                pltpu.make_async_copy(qkv.at[j], qkv_hbm[j], out_sem.at[j]).wait()
            pltpu.make_async_copy(w_ref, w_out_hbm, w_out_sem).wait()


def attend_forward(lengths, group, heads, rows, cuts, qkv=None, source=None):
    length = rows * cuts
    width = heads * HD
    block = min(512, length)
    chunk = min(512, length)
    count = length // block
    vmem = pl.BlockSpec(memory_space=pltpu.VMEM)
    anywhere = pl.BlockSpec(memory_space=pl.ANY)
    in_specs = [pl.BlockSpec(memory_space=pltpu.SMEM)]
    out_specs = [
        pl.BlockSpec((block, width), lambda i: (i, 0)),
        pl.BlockSpec((heads, 1, length, block), lambda i: (0, i, 0, 0)),
        pl.BlockSpec((heads, 1, 8, block), lambda i: (0, i, 0, 0)),
    ] + [pl.BlockSpec((rows, width), lambda i: (0, 0))] * cuts
    out_shape = [
        jax.ShapeDtypeStruct((length, width), BF),
        jax.ShapeDtypeStruct((heads, count, length, block), BF),
        jax.ShapeDtypeStruct((heads, count, 8, block), F32),
    ] + [jax.ShapeDtypeStruct((rows, width), BF)] * cuts
    scratch = [
        pltpu.VMEM((heads, length, 256), BF),
        pltpu.VMEM((heads, HD + 16, length), BF),
        pltpu.VMEM((heads, length, block), F32),
    ]
    if source is not None:
        down, up, xs, ws, height = source
        parts = len(xs)
        counts = [w.shape[0] // height for w in ws]
        model = sum(w.shape[0] for w in ws)
        all_heads = ws[0].shape[1] // 3
        args = [down, up, *xs, *ws]
        in_specs += [vmem] * 2 + [anywhere] * (parts + len(ws))
        out_specs += [anywhere] * 3 + [vmem, anywhere]
        out_shape += [jax.ShapeDtypeStruct((length, all_heads), BF)] * 3
        out_shape += [jax.ShapeDtypeStruct((length, down.shape[0]), BF)]
        out_shape += [jax.ShapeDtypeStruct((model, 3 * all_heads), BF)]
        scratch += [
            pltpu.VMEM((length, model), BF),
            pltpu.VMEM((model, 3 * all_heads), BF),
            pltpu.VMEM((3, length, all_heads), BF),
            pltpu.SemaphoreType.DMA((parts,)),
            pltpu.SemaphoreType.DMA,
            pltpu.SemaphoreType.DMA((3,)),
            pltpu.SemaphoreType.DMA,
        ]
    else:
        parts = 0
        counts = []
        args = list(qkv)
        in_specs += [
            pl.BlockSpec((block, width), lambda i: (i, group)),
            pl.BlockSpec((length, width), lambda i: (0, group)),
            pl.BlockSpec((length, width), lambda i: (0, group)),
        ]
    return pl.pallas_call(
        functools.partial(
            attend_forward_kernel, heads, block, chunk, rows, group, cuts, parts, counts
        ),
        grid=(count,),
        in_specs=in_specs,
        out_specs=out_specs,
        out_shape=out_shape,
        scratch_shapes=scratch,
        compiler_params=pltpu.CompilerParams(
            vmem_limit_bytes=VMEM_LIMIT, dimension_semantics=("arbitrary",)
        ),
        cost_estimate=BRIEF,
        name="project_attend_forward" if parts else "attend_forward",
    )(lengths, *args)


def attend_backward_kernel(
    heads, block, chunk, cuts, q_ref, k_ref, v_ref, o_ref, e_ref, l_ref, *rest
):
    cut_refs = rest[0:cuts]
    dq_ref, dk_ref, dv_ref, do_rows_ref, values_wide, keys_t, dk_sum, dv_sum = rest[cuts:]
    length = k_ref.shape[0]
    rows = length // cuts
    width = heads * HD
    i = pl.program_id(0)
    for k in range(cuts):

        @pl.when(i == k * rows // block)
        def _():
            begin = k * rows % block
            do_rows_ref[begin : begin + rows, :] = cut_refs[k][...]

    @pl.when(i == 0)
    def _():
        ones = (lax.broadcasted_iota(jnp.int32, (length, 128), 1) < 2).astype(BF)
        for h in range(heads):
            value = v_ref[:, h * HD : (h + 1) * HD]
            values_wide[h, :, 0:HD] = value
            values_wide[h, :, HD : 2 * HD] = value
            values_wide[h, :, 2 * HD :] = ones
        keys_t[...] = k_ref[...].T
        dk_sum[...] = jnp.zeros_like(dk_sum)
        dv_sum[...] = jnp.zeros_like(dv_sum)

    q = q_ref[...]
    flipped_do = do_rows_ref[...].astype(F32).T
    flipped_o = o_ref[...].astype(F32).T
    lane = lax.broadcasted_iota(jnp.int32, (block, width), 1)
    row = lax.broadcasted_iota(jnp.int32, (128, block), 0)
    grads = []
    for h in range(heads):
        own = slice(h * HD, (h + 1) * HD)
        inverse = 1.0 / l_ref[h, 0, 0:1, :]
        dot = -jnp.sum(flipped_do[own] * flipped_o[own], axis=0, keepdims=True) * inverse
        scaled = flipped_do[own] * inverse
        high = scaled.astype(BF)
        low = (scaled - high.astype(F32)).astype(BF)
        dot_high = dot.astype(BF)
        dot_low = (dot - dot_high.astype(F32)).astype(BF)
        dots = jnp.where(row == 0, dot_high, jnp.where(row == 1, dot_low, jnp.zeros_like(dot_low)))
        right = jnp.concatenate([high, low, dots], axis=0)
        do_rows = high.T
        if heads == 2:
            empty = jnp.zeros_like(do_rows)
            do_rows = jnp.concatenate([do_rows, empty] if h == 0 else [empty, do_rows], axis=1)
        query = jnp.where((lane >= h * HD) & (lane < (h + 1) * HD), q, jnp.zeros_like(q))
        total = None
        for c in range(length // chunk):
            rows = slice(c * chunk, (c + 1) * chunk)
            e = e_ref[h, 0, rows, :]
            part = mm(values_wide[h, rows, :], right)
            ds = (e.astype(F32) * part).astype(BF)
            dv_sum[rows, :] += mm(e, do_rows)
            dk_sum[rows, :] += mm(ds, query)
            part = mm(keys_t[own, rows], ds)
            total = part if total is None else total + part
        grads.append(total * HD ** (-0.5))
    dq_ref[...] = jnp.concatenate(grads, axis=0).T.astype(BF)

    @pl.when(i == pl.num_programs(0) - 1)
    def _():
        dk_ref[...] = (dk_sum[...] * HD ** (-0.5)).astype(BF)
        dv_ref[...] = dv_sum[...].astype(BF)


def attend_backward(q, k, v, att, d_att, e, row_sum, group, heads):
    length = q.shape[0]
    width = heads * HD
    block = e.shape[3]
    cuts = len(d_att)
    rows = length // cuts
    chunk = min(512, length)
    count = length // block
    whole = pl.BlockSpec((length, width), lambda i: (0, group))
    return pl.pallas_call(
        functools.partial(attend_backward_kernel, heads, block, chunk, cuts),
        grid=(count,),
        in_specs=[
            pl.BlockSpec((block, width), lambda i: (i, group)),
            whole,
            whole,
            pl.BlockSpec((block, width), lambda i: (i, 0)),
            pl.BlockSpec((heads, 1, length, block), lambda i: (0, i, 0, 0)),
            pl.BlockSpec((heads, 1, 8, block), lambda i: (0, i, 0, 0)),
        ]
        + [pl.BlockSpec((rows, width), lambda i: (0, group))] * cuts,
        out_specs=[
            pl.BlockSpec((block, width), lambda i: (i, 0)),
            pl.BlockSpec((length, width), lambda i: (0, 0)),
            pl.BlockSpec((length, width), lambda i: (0, 0)),
        ],
        out_shape=[jax.ShapeDtypeStruct((length, width), BF)] * 3,
        scratch_shapes=[
            pltpu.VMEM((block, width), BF),
            pltpu.VMEM((heads, length, 256), BF),
            pltpu.VMEM((width, length), BF),
            pltpu.VMEM((length, width), F32),
            pltpu.VMEM((length, width), F32),
        ],
        compiler_params=pltpu.CompilerParams(
            vmem_limit_bytes=VMEM_LIMIT, dimension_semantics=("arbitrary",)
        ),
        cost_estimate=BRIEF,
        name="attend_backward",
    )(q, k, v, att, e, row_sum, *d_att)


def normal_parts(z):
    density = jnp.exp2(z * z * (-0.5 * LOG2E))
    t = 1.0 / (1.0 + (0.3275911 * 0.5**0.5) * jnp.abs(z))
    poly = t * (
        0.254829592 * 0.5
        + t
        * (
            -0.284496736 * 0.5
            + t * (1.421413741 * 0.5 + t * (-1.453152027 * 0.5 + t * (1.061405429 * 0.5)))
        )
    )
    tail = poly * density
    return jnp.where(z < 0.0, tail, 1.0 - tail), density * 0.3989422804014327


def normalize(values):
    center = values - jnp.mean(values, axis=-1, keepdims=True)
    scale = lax.rsqrt(jnp.mean(center * center, axis=-1, keepdims=True) + EPS)
    return center * scale, scale


def normalize_back(e, normal, scale):
    return scale * (
        e
        - jnp.mean(e, axis=-1, keepdims=True)
        - normal * jnp.mean(e * normal, axis=-1, keepdims=True)
    )


def assemble_kernel(rank, share, used, sets, down_ref, up_ref):
    ranks = 3 * rank
    count, tail = sets.shape[0], used - ranks
    for k in range(count):
        down_ref[:, k * 128 : (k + 1) * 128] = sets[k, 0:ranks, :]
    row = lax.broadcasted_iota(jnp.int32, (ranks, tail), 0)
    source = lax.broadcasted_iota(jnp.int32, (ranks, tail), 1)
    for j in range(3):
        for half in range(2):
            total = None
            for k in range(count):
                wanted = row < 0
                for r in range(share):
                    target = j * rank + k * share + r
                    wanted = wanted | (
                        (row == target) & (source == (j * share + r) * 2 + half)
                    )
                part = mm(jnp.where(wanted, 1.0, 0.0).astype(BF), sets[k, ranks:used, :])
                total = part if total is None else total + part
            begin = (j * 2 + half) * 128
            up_ref[:, begin : begin + 128] = total.astype(BF)


def assemble(sets, rank, share, used):
    count = sets.shape[0]
    vmem = pl.BlockSpec(memory_space=pltpu.VMEM)
    return pl.pallas_call(
        functools.partial(assemble_kernel, rank, share, used),
        in_specs=[vmem],
        out_specs=[vmem] * 2,
        out_shape=[
            jax.ShapeDtypeStruct((3 * rank, count * 128), BF),
            jax.ShapeDtypeStruct((3 * rank, 6 * 128), BF),
        ],
        name="assemble",
    )(sets)


def unproject_kernel(parts, groups, u_ref, w_ref, down_ref, up_ref, *rest):
    x_hbm = rest[0:parts]
    grads = rest[parts : parts + 3 * groups]
    stay_ref, go_ref, g_up_ref, g_down_ref, x, x_sem = rest[parts + 3 * groups :]
    width = w_ref.shape[1] // 3
    step = pl.program_id(0)
    rows = x.shape[1]
    copies = [pltpu.make_async_copy(x_hbm[i], x.at[i], x_sem.at[i]) for i in range(parts)]

    @pl.when(step == 0)
    def _():
        for copy in copies:
            copy.start()
        g_up_ref[...] = jnp.zeros_like(g_up_ref)
        g_down_ref[...] = jnp.zeros_like(g_down_ref)

    values = [
        jnp.concatenate([grads[g * 3 + j][...] for g in range(groups)], axis=1) for j in range(3)
    ]
    d_u = None
    for j in range(3):
        part = mm_nt(values[j], up_ref[:, j * width : (j + 1) * width])
        d_u = part if d_u is None else d_u + part
    d_u = d_u.astype(BF)
    total = mm(d_u, down_ref[...])
    for j in range(3):
        total = total + mm_nt(values[j], w_ref[:, j * width : (j + 1) * width])
    total = total.astype(BF)

    @pl.when(step < parts // 2)
    def _():
        stay_ref[...] = total

    @pl.when(step >= parts // 2)
    def _():
        go_ref[...] = total

    u_t = transpose_small(u_ref[...])
    for j in range(3):
        g_up_ref[:, j * width : (j + 1) * width] += mm(u_t, values[j])
    for i in range(parts):

        @pl.when(step == i)
        def _():
            copies[i].wait()

    g_down_ref[...] += mm(transpose_small(d_u), x[step])


def unproject(grads, u, w, down, up, xs, odd):
    model = w.shape[0]
    width = w.shape[1] // 3
    rows = xs[0].shape[0]
    steps = len(xs)
    ranks = down.shape[0]
    grads = [value for group in grads for value in group]
    vmem = pl.BlockSpec(memory_space=pltpu.VMEM)
    return pl.pallas_call(
        functools.partial(unproject_kernel, steps, len(grads) // 3),
        grid=(steps,),
        in_specs=[pl.BlockSpec((rows, ranks), lambda i: (2 * i + odd, 0))]
        + [vmem] * 3
        + [pl.BlockSpec(memory_space=pl.ANY)] * steps
        + [pl.BlockSpec((rows, g.shape[1]), lambda i: (2 * i + odd, 0)) for g in grads],
        out_specs=[
            pl.BlockSpec((rows, model), lambda i: (jnp.minimum(i, steps // 2 - 1), 0)),
            pl.BlockSpec((rows, model), lambda i: (jnp.maximum(i - steps // 2, 0), 0)),
            vmem,
            vmem,
        ],
        out_shape=[
            jax.ShapeDtypeStruct((rows * steps // 2, model), BF),
            jax.ShapeDtypeStruct((rows * steps // 2, model), BF),
            jax.ShapeDtypeStruct((ranks, 3 * width), F32),
            jax.ShapeDtypeStruct((ranks, model), F32),
        ],
        scratch_shapes=[
            pltpu.VMEM((steps, rows, model), BF),
            pltpu.SemaphoreType.DMA((steps,)),
        ],
        compiler_params=pltpu.CompilerParams(
            vmem_limit_bytes=VMEM_LIMIT, dimension_semantics=("arbitrary",)
        ),
        cost_estimate=BRIEF,
        name="unproject",
    )(u, w, down, up, *xs, *grads)


def middle_kernel(
    cuts, parts, counts, sizes, hidden_block, x_ref, cot_ref,
    down_out, up_out, down_fc1, up_fc1, down_fc2, up_fc2, gain1, bias1, gain2, bias2, *rest
):
    att_hbm = rest[0:parts]
    rest = rest[parts:]
    first_hbm = rest[0 : len(counts)]
    second_hbm = rest[len(counts) : 2 * len(counts)]
    rest = rest[2 * len(counts) :]
    out_ref, dy1_ref = rest[0:2]
    d_att_refs = rest[2 : 2 + cuts]
    (
        g_up_fc2, g_down_fc2, g_up_fc1, g_down_fc1, g_up_out, g_down_out,
        att_own, wo_t, w1, w2_t, hidden, slope, normal1, normed, low_rows, total,
        att_sem, wo_sem, w1_sem, w2_sem,
    ) = rest[2 + cuts :]
    rows, model = x_ref.shape
    units = w1.shape[1]
    height, wide, narrow = sizes
    mine = lax.axis_index("tensor")
    n_t = lax.axis_size("tensor")
    order = cut_order(n_t)
    places = spread_places() if sum(counts) > 1 else [(0, 0)]
    places2 = spread_places_second() if sum(counts) > 1 else [(0, 0)]

    def fetch(source, j, begin, width, target, row, col, sem):
        pltpu.make_async_copy(
            source.at[j * height : (j + 1) * height, begin : begin + width],
            target.at[
                pl.ds(pl.multiple_of(row * height, height), height),
                pl.ds(pl.multiple_of(col * width, width), width),
            ],
            sem,
        ).start()

    def each_block(places):
        block = 0
        for i, count in enumerate(counts):
            for j in range(count):
                yield (i, j) + places[block]
                block += 1

    if parts > 1:
        width = att_hbm[0].shape[1]
        groups = parts // n_t
        for k in range(n_t):
            for g in range(groups):
                col = pl.multiple_of(((mine ^ order[k]) * groups + g) * width, width)
                pltpu.make_async_copy(
                    att_hbm[k * groups + g], att_own.at[:, pl.ds(col, width)], att_sem
                ).start()
    else:
        pltpu.make_async_copy(att_hbm[0], att_own, att_sem).start()
    for i, j, row, col in each_block(places):
        fetch(first_hbm[i], j, wide, narrow, wo_t, row, col, wo_sem)
    for i, j, row, col in each_block(places):
        fetch(first_hbm[i], j, 0, wide, w1, row, col, w1_sem.at[col])
    for i, j, row, col in each_block(places2):
        fetch(second_hbm[i], j, 0, wide, w2_t, row, col, w2_sem.at[col])

    pltpu.make_async_copy(att_own, att_own, att_sem).wait()
    pltpu.make_async_copy(wo_t, wo_t, wo_sem).wait()
    att = att_own[...]
    u_out = mm_nt(att, down_out[...]).astype(BF)
    first = x_ref[...].astype(F32) + mm_nt(att, wo_t[...]) + mm(u_out, up_out[...])
    normal, scale1 = normalize(first)
    normal1[...] = normal
    full = normal * gain1[...].astype(F32) + bias1[...].astype(F32)
    normed[...] = full
    low_rows[...] = full.astype(BF)
    u_fc1 = mm_nt(low_rows[...], down_fc1[...]).astype(BF)

    blocks = units // hidden_block
    per_cut = wide // hidden_block

    def before(i):
        cols = slice(i * hidden_block, (i + 1) * hidden_block)
        if i % per_cut == 0:
            b = i // per_cut
            for target, sem in ((w1, w1_sem), (w2_t, w2_sem)):
                view = target.at[:, b * wide : (b + 1) * wide]
                pltpu.make_async_copy(view, view, sem.at[b]).wait()
        return mm(low_rows[...], w1[:, cols]) + mm(u_fc1, up_fc1[:, cols])

    z = before(0)
    u_sum = None
    for i in range(blocks):
        cols = slice(i * hidden_block, (i + 1) * hidden_block)
        following = before(i + 1) if i + 1 < blocks else None
        phi_sum, phi = normal_parts(z)
        act = (z * phi_sum).astype(BF)
        hidden[:, cols] = act
        slope[:, cols] = phi_sum + z * phi
        part = mm_nt(act, w2_t[:, cols])
        total[...] = part if i == 0 else total[...] + part
        part = mm_nt(act, down_fc2[:, cols])
        u_sum = part if u_sum is None else u_sum + part
        z = following
    u_fc2 = u_sum.astype(BF)
    second = normed[...] + total[...] + mm(u_fc2, up_fc2[...])
    normal2, scale2 = normalize(second)
    gain = gain2[...].astype(F32)
    out_ref[...] = (normal2 * gain + bias2[...].astype(F32)).astype(BF)
    d_second = normalize_back(cot_ref[...].astype(F32) * gain, normal2, scale2)
    total[...] = d_second
    d_ffn = d_second.astype(BF)
    d_u2 = mm_nt(d_ffn, up_fc2[...]).astype(BF)
    d_u2_t = transpose_small(d_u2)
    g_up_fc2[...] = mm(transpose_small(u_fc2), d_ffn).astype(BF)
    u_fc1_t = transpose_small(u_fc1)

    def before_back(i):
        cols = slice(i * hidden_block, (i + 1) * hidden_block)
        return mm(d_ffn, w2_t[:, cols]) + mm(d_u2, down_fc2[:, cols])

    d_hidden = before_back(0)
    u_sum = None
    for i in range(blocks):
        cols = slice(i * hidden_block, (i + 1) * hidden_block)
        following = before_back(i + 1) if i + 1 < blocks else None
        d_pre = (d_hidden * slope[:, cols]).astype(BF)
        g_down_fc2[:, cols] = mm(d_u2_t, hidden[:, cols]).astype(BF)
        g_up_fc1[:, cols] = mm(u_fc1_t, d_pre).astype(BF)
        total[...] += mm_nt(d_pre, w1[:, cols])
        part = mm_nt(d_pre, up_fc1[:, cols])
        u_sum = part if u_sum is None else u_sum + part
        d_hidden = following
    d_u1 = u_sum.astype(BF)
    d_normed = total[...] + mm(d_u1, down_fc1[...])
    g_down_fc1[...] = mm(transpose_small(d_u1), low_rows[...]).astype(BF)
    d_first = normalize_back(d_normed * gain1[...].astype(F32), normal1[...], scale1)
    dy1_ref[...] = d_first
    d_a = d_first.astype(BF)
    d_uo = mm_nt(d_a, up_out[...]).astype(BF)
    g_up_out[...] = mm(transpose_small(u_out), d_a).astype(BF)
    g_down_out[...] = mm(transpose_small(d_uo), att).astype(BF)
    att_own[...] = (mm(d_a, wo_t[...]) + mm(d_uo, down_out[...])).astype(BF)
    width = model // cuts
    for k in range(cuts):
        col = pl.multiple_of((mine ^ order[k]) * width, width) if cuts > 1 else 0
        d_att_refs[k][...] = att_own[:, pl.ds(col, width)]


def cut_order(n_t):
    order = [0]
    bit = n_t // 2
    while bit:
        order = order + [k ^ bit for k in order]
        bit //= 2
    return order


def middle(atts, cuts, x, cot, adapters, norms, firsts, seconds, sizes):
    rows, model = x.shape
    rank, units = adapters[3].shape
    height, wide, narrow = sizes
    counts = [value.shape[0] // height for value in firsts]
    hidden_block = min(512, wide)
    cols = units // wide
    vmem = pl.BlockSpec(memory_space=pltpu.VMEM)
    anywhere = pl.BlockSpec(memory_space=pl.ANY)
    long = jax.ShapeDtypeStruct((rank, units), BF)
    short = jax.ShapeDtypeStruct((rank, model), BF)
    out_shape = (
        [jax.ShapeDtypeStruct((rows, model), BF), jax.ShapeDtypeStruct((rows, model), F32)]
        + [jax.ShapeDtypeStruct((rows, model // cuts), BF)] * cuts
        + [short, long, long, short, short, short]
    )
    return pl.pallas_call(
        functools.partial(middle_kernel, cuts, len(atts), counts, sizes, hidden_block),
        in_specs=[vmem] * 12 + [anywhere] * (len(atts) + len(firsts) + len(seconds)),
        out_specs=[vmem] * len(out_shape),
        out_shape=out_shape,
        scratch_shapes=[
            pltpu.VMEM((rows, model), BF),
            pltpu.VMEM((model, model), BF),
            pltpu.VMEM((model, units), BF),
            pltpu.VMEM((model, units), BF),
            pltpu.VMEM((rows, units), BF),
            pltpu.VMEM((rows, units), F32),
            pltpu.VMEM((rows, model), F32),
            pltpu.VMEM((rows, model), F32),
            pltpu.VMEM((rows, model), BF),
            pltpu.VMEM((rows, model), F32),
            pltpu.SemaphoreType.DMA,
            pltpu.SemaphoreType.DMA,
            pltpu.SemaphoreType.DMA((cols,)),
            pltpu.SemaphoreType.DMA((cols,)),
        ],
        compiler_params=pltpu.CompilerParams(vmem_limit_bytes=VMEM_LIMIT),
        cost_estimate=BRIEF,
        name="middle",
    )(x, cot, *adapters, *norms, *atts, *firsts, *seconds)


class Spread:
    def __init__(self):
        self.n_dp, self.n_t = lax.axis_size("dp"), lax.axis_size("tensor")
        self.devices = [(d, t) for d in range(self.n_dp) for t in range(self.n_t)]

    def send(self, value, target):
        n_t = self.n_t
        pairs = []
        for d, t in self.devices:
            to_d, to_t = target(d, t)
            pairs.append((d * n_t + t, to_d * n_t + to_t))
        return lax.ppermute(value, ("dp", "tensor"), pairs)

    def ring(self, value):
        return self.send(value, lambda d, t: ((d + 2) % self.n_dp, t))

    def cross(self, value, core):
        return self.send(value, lambda d, t: (d ^ 1, t) if t % 2 == core else (d, t ^ 2))

    def core(self, value):
        return self.send(value, lambda d, t: (d, t ^ 1))


def spread_places():
    n_dp = lax.axis_size("dp")
    d = lax.axis_index("dp")
    mine = lax.axis_index("tensor")
    found = []
    for t in (mine, mine ^ 1):
        even = (t % 2) == 0
        for to_d, to_t in (
            (d, t),
            (jnp.where(even, d ^ 1, d), jnp.where(even, t, t ^ 2)),
            (jnp.where(even, d, d ^ 1), jnp.where(even, t ^ 2, t)),
            (d ^ 1, t ^ 2),
        ):
            found += [((to_d + n_dp - 2 * j) % n_dp, to_t) for j in range(n_dp // 2)]
    return found


def spread_places_second():
    n_dp = lax.axis_size("dp")
    d = lax.axis_index("dp")
    mine = lax.axis_index("tensor")
    found = []
    for t in (mine, mine ^ 1):
        even = (t % 2) == 0
        square = (
            (d, t),
            (jnp.where(even, d ^ 1, d), jnp.where(even, t, t ^ 2)),
            (jnp.where(even, d, d ^ 1), jnp.where(even, t ^ 2, t)),
            (d ^ 1, t ^ 2),
        )
        for j in range(n_dp // 2):
            found += [((to_d + n_dp - 2 * j) % n_dp, to_t) for to_d, to_t in square]
    return found


def shards(
    inputs, cotangent, lengths, adapter_index, w_qkv, w_out, w_fc1, w_fc2,
    ln1_gain, ln1_bias, ln2_gain, ln2_bias, down_qkv, up_qkv, down_out, up_out,
    down_fc1, up_fc1, down_fc2, up_fc2,
):
    n_dp = lax.axis_size("dp")
    n_t = lax.axis_size("tensor")
    every = ("dp", "tensor")
    mine = lax.axis_index("tensor")
    rows, model = inputs.shape
    length = rows * n_t
    n_set = down_qkv.shape[1]
    rank = down_qkv.shape[3]
    r_dp = rank // n_dp
    r_t = rank // n_t
    d_dp = model // n_dp
    c_t = model // n_t
    f_t = w_fc1.shape[1]
    f_all = f_t * n_t

    def swap(value, bit):
        return lax.ppermute(value, "tensor", [(i, i ^ bit) for i in range(n_t)])

    bits = []
    bit = n_t // 2
    while bit:
        bits.append(bit)
        bit //= 2
    order = cut_order(n_t)

    x_parts = [inputs]
    for bit in bits[:-1]:
        x_parts = x_parts + [swap(part, bit) for part in x_parts]

    w_local = w_qkv.transpose(1, 0, 2).reshape(d_dp, 3 * c_t)
    packed_second = w_fc2.T
    staged = n_dp == 8 and n_t == 4
    if staged:
        spread = Spread()
        packed = jnp.concatenate([w_fc1, w_out.T, w_local], axis=1)
        hops = [packed, spread.ring(packed)]
        square = [packed_second, spread.cross(packed_second, 0), spread.cross(packed_second, 1)]
        square.append(spread.cross(square[1], 1))
        block_sizes = (d_dp, f_t, c_t)
    else:

        def whole(value):
            blocks = lax.all_gather(value, every, axis=0).reshape(n_dp, n_t, d_dp, -1)
            return blocks.transpose(0, 2, 1, 3).reshape(model, -1)

        firsts = [jnp.concatenate([whole(w_fc1), whole(w_out.T)], axis=1)]
        seconds = [whole(packed_second)]
        w_parts = [lax.all_gather(w_local, "dp", axis=0, tiled=True)]
        w_height = model
        block_sizes = (model, f_all, model)

    index_all = lax.all_to_all(
        jnp.broadcast_to(adapter_index, (n_dp,)), "dp", 0, 0, tiled=True
    )
    onehot_all = (index_all[:, None] == jnp.arange(n_set, dtype=jnp.int32)[None, :]).astype(BF)
    def part_of_rank(value):
        return lax.dynamic_slice_in_dim(value, mine * r_t, r_t, 1)

    down_t = down_qkv.transpose(1, 0, 3, 2).reshape(n_set, 3 * rank, d_dp)
    up_first = up_qkv.transpose(1, 0, 2, 3)
    tables = [
        down_out.transpose(0, 2, 1),
        part_of_rank(up_out),
        part_of_rank(down_fc1.transpose(0, 2, 1)),
        up_fc1,
        down_fc2.transpose(0, 2, 1),
        part_of_rank(up_fc2),
    ]
    sizes = [t.size // n_set for t in tables]
    norm_part = jnp.stack([ln1_gain, ln1_bias, ln2_gain, ln2_bias])
    in_rows = staged and d_dp == 128 and c_t == 256
    if in_rows:
        parts = [down_t, up_first.reshape(n_set, -1, 128)]
        parts.append(jnp.zeros((n_set, -parts[1].shape[1] % 16, 128), BF))
        qkv_rows = sum(p.shape[1] for p in parts)
        parts += [t.reshape(n_set, -1, 128) for t in tables]
        parts.append(jnp.broadcast_to(norm_part, (n_set, 4, d_dp)))
        parts.append(jnp.zeros((n_set, -sum(p.shape[1] for p in parts) % 16, 128), BF))
        table = jnp.concatenate(parts, axis=1)
        sets = jnp.einsum("ns,srl->nrl", onehot_all, table, preferred_element_type=F32).astype(BF)
        hops[1], sets = lax.optimization_barrier((hops[1], sets))
        hops.append(spread.ring(hops[1]))
        sets = lax.all_to_all(sets, "dp", 0, 0, tiled=True)
        hops[2], sets, square = lax.optimization_barrier((hops[2], sets, square))
        hops.append(spread.ring(hops[2]))
        second = [jnp.concatenate(square, axis=0)]
        second.append(spread.ring(second[0]))
        sel_down_qkv, sel_up_qkv = assemble(sets, rank, r_dp, qkv_rows)
        begin = qkv_rows + sum(sizes) // 128
        came = sets[:, qkv_rows:begin]
        norms = sets[:, begin : begin + 4].transpose(1, 0, 2).reshape(4, 1, model)
    else:
        flat = [t.reshape(n_set, -1) for t in (down_t, up_first, *tables)]
        flat.append(jnp.broadcast_to(norm_part.reshape(1, -1), (n_set, 4 * d_dp)))
        table = jnp.concatenate(flat, axis=1)
        sets = lax.all_to_all(mm(onehot_all, table).astype(BF), "dp", 0, 0, tiled=True)
        cut = 3 * rank * d_dp
        cut_up = cut + up_first.size // n_set
        sel_down_qkv = (
            sets[:, :cut].reshape(n_dp, 3 * rank, d_dp).transpose(1, 0, 2).reshape(3 * rank, model)
        )
        up_cols = sets[:, cut:cut_up].reshape(n_dp, 3, r_dp, c_t).transpose(1, 0, 2, 3)
        same = jnp.eye(3, dtype=BF).reshape(3, 1, 3, 1)
        sel_up_qkv = (up_cols.reshape(3, rank, 1, c_t) * same).reshape(3 * rank, 3 * c_t)
        came = sets[:, cut_up : cut_up + sum(sizes)]
        norms = sets[:, cut_up + sum(sizes) :].reshape(n_dp, 4, d_dp)
        norms = norms.transpose(1, 0, 2).reshape(4, 1, model)
    shares = [came]
    for bit in bits:
        shares = shares + [swap(share, bit) for share in shares]
    of_owner = jnp.array([order.index(k) for k in range(n_t)], jnp.int32)
    of_owner = of_owner[jnp.arange(n_t, dtype=jnp.int32) ^ mine]

    def make_adapters(shares):
        came = []
        for t in range(n_t):
            value = shares[0]
            for k in range(1, n_t):
                value = jnp.where((mine ^ order[k]) == t, shares[k], value)
            came.append(value)
        came = jnp.stack(came).reshape(n_t, n_dp, -1)
        pieces = []
        start = 0
        for size in sizes:
            pieces.append(came[:, :, start : start + size])
            start += size

        def from_rank_parts(piece):
            return piece.reshape(n_t, n_dp, r_t, d_dp).transpose(0, 2, 1, 3).reshape(rank, model)

        def from_blocks(piece, width):
            return (
                piece.reshape(n_t, n_dp, r_dp, width)
                .transpose(1, 2, 0, 3)
                .reshape(rank, n_t * width)
            )

        return [
            from_blocks(pieces[0], c_t),
            from_rank_parts(pieces[1]),
            from_rank_parts(pieces[2]),
            from_blocks(pieces[3], f_t),
            from_blocks(pieces[4], f_t),
            from_rank_parts(pieces[5]),
        ]

    x_parts = x_parts + [swap(part, bits[-1]) for part in x_parts]
    if staged:
        w_near = jnp.concatenate([hop[:, f_t + c_t :] for hop in hops], axis=0)
        w_near, hops, shares = lax.optimization_barrier((w_near, hops, shares))
        w_parts = [w_near, lax.ppermute(w_near, "dp", [(i, i ^ 1) for i in range(n_dp)])]
        w_height = d_dp
        first = jnp.concatenate([hop[:, : f_t + c_t] for hop in hops], axis=0)
        adapters = make_adapters(shares)
        first, x_parts, adapters, w_parts, second = lax.optimization_barrier(
            (first, x_parts, adapters, w_parts, second)
        )
        second.append(spread.ring(second[1]))
        first_one = spread.cross(first, 0)
        first_two = spread.cross(first, 1)
        second_over = [spread.core(value) for value in second[:2]]
    else:
        adapters = make_adapters(shares)

    heads = c_t // HD
    group_heads = 2 if heads % 2 == 0 else 1
    groups = heads // group_heads
    kept = []
    att_parts = [[] for _ in range(n_t)]
    for g in range(groups):
        if g == 0:
            att, e, row_sum, *more = attend_forward(
                lengths, g, group_heads, rows, n_t,
                source=(sel_down_qkv, sel_up_qkv, x_parts, w_parts, w_height),
            )
            cut_rows, qkv, u_in, w_cols = more[:n_t], more[n_t : n_t + 3], *more[n_t + 3 :]
        else:
            if staged and g == 1:
                near = [first, first_one, first_two]
                qkv, near, second = lax.optimization_barrier((qkv, near, second))
                second.append(spread.ring(second[2]))
                first_both = spread.cross(near[1], 1)
            att, e, row_sum, *cut_rows = attend_forward(
                lengths, g, group_heads, rows, n_t, qkv=qkv
            )
        kept.append((att, e, row_sum))
        for k in range(n_t):
            att_parts[k].append(cut_rows[k] if order[k] == 0 else swap(cut_rows[k], order[k]))
    atts = [part for parts in att_parts for part in parts]

    if staged:
        kept, near, first_both, second, second_over = lax.optimization_barrier(
            (kept, near, first_both, second, second_over)
        )
        firsts = near + [first_both]
        firsts += [spread.core(value) for value in firsts]
        seconds = second + second_over + [spread.core(value) for value in second[2:]]
    blocks_fit = c_t % 128 == 0
    if not blocks_fit:
        by_cut = jnp.concatenate(atts, axis=1).reshape(rows, n_t, c_t)
        atts = [jnp.take(by_cut, of_owner, axis=1).reshape(rows, model)]
    cuts = n_t if blocks_fit else 1
    done = middle(
        atts, cuts, inputs, cotangent, adapters, list(norms), firsts, seconds, block_sizes
    )
    output, d_first = done[0:2]
    d_att_blocks = done[2 : 2 + cuts]
    if not blocks_fit:
        by_owner = d_att_blocks[0].reshape(rows, n_t, c_t)
        d_att_blocks = [
            lax.dynamic_index_in_dim(by_owner, mine ^ order[k], 1, keepdims=False)
            for k in range(n_t)
        ]
    g_up_fc2, g_down_fc2, g_up_fc1, g_down_fc1, g_up_out, g_down_out = done[2 + cuts :]

    def share_cols(value):
        lead = value.size // model
        return (
            value.reshape(lead, n_dp, n_t, model // (n_dp * n_t))
            .transpose(1, 2, 0, 3)
            .reshape(n_dp * n_t, -1)
        )

    def share_blocks(value):
        width = value.shape[1] // n_t
        return (
            value.reshape(n_dp, r_dp, n_t, width).transpose(0, 2, 1, 3).reshape(n_dp * n_t, -1)
        )

    d_att_all = [
        d_att_blocks[k] if order[k] == 0 else swap(d_att_blocks[k], order[k]) for k in range(n_t)
    ]
    near_cut = order.index(1)
    adapter_grads = [g_down_out, g_up_out, g_down_fc1, g_up_fc1, g_down_fc2, g_up_fc2]
    d_att_all[near_cut], adapter_grads = lax.optimization_barrier(
        (d_att_all[near_cut], adapter_grads)
    )
    g_down_out, g_up_out, g_down_fc1, g_up_fc1, g_down_fc2, g_up_fc2 = adapter_grads
    early = [
        share_blocks(g_down_out),
        share_cols(g_up_out),
        share_cols(g_down_fc1),
        share_blocks(g_up_fc1),
        share_blocks(g_down_fc2),
        share_cols(g_up_fc2),
    ]
    early = jnp.concatenate(early, axis=1)

    d_att_all, early = lax.optimization_barrier((d_att_all, early))
    grads = []
    for g in range(groups):
        if g == groups - 1:
            d_att_all, grads, early = lax.optimization_barrier((d_att_all, grads, early))
            early_got = lax.all_to_all(early, every, 0, 0, tiled=True)
        grads.append(
            attend_backward(*qkv, kept[g][0], d_att_all, kept[g][1], kept[g][2], g, group_heads)
        )
    grads, early_got = lax.optimization_barrier((grads, early_got))

    def partly(odd):
        stay, go, g_up, g_down = unproject(
            grads, u_in, w_cols, sel_down_qkv, sel_up_qkv, x_parts[odd::2], odd
        )
        value = [stay, swap(go, bits[-1])]
        for bit in reversed(bits[1:-1]):
            value = sum(v.astype(F32) for v in value).astype(BF)
            half = value.shape[0] // 2
            value = [value[:half], swap(value[half:], bit)]
        return value, g_up, g_down

    odd_sum, g_up_other, g_down_other = partly(1)
    odd_sum = (odd_sum[0].astype(F32) + odd_sum[1].astype(F32)).astype(BF)
    grads, odd_sum = lax.optimization_barrier((grads, odd_sum))
    cut = rows // 2
    far_first = swap(odd_sum[:cut], bits[0])
    even_sum, g_up_own, g_down_own = partly(0)
    here = d_first + even_sum[0].astype(F32) + even_sum[1].astype(F32)

    g_down_qkv = (g_down_own + g_down_other).astype(BF)
    g_up_all = (g_up_own + g_up_other).astype(BF)
    g_up_qkv = jnp.stack(
        [
            g_up_all[j * rank : (j + 1) * rank, j * c_t : (j + 1) * c_t]
            for j in range(3)
        ]
    )
    up_share = (
        g_up_qkv.reshape(3, n_dp, r_dp, c_t).transpose(1, 0, 2, 3).reshape(n_dp, 1, -1)
    )
    up_share = jnp.broadcast_to(up_share, (n_dp, n_t, up_share.shape[2])).reshape(n_dp * n_t, -1)
    late = [share_cols(g_down_qkv), up_share]
    late = jnp.concatenate(late, axis=1)
    late, far_first, odd_sum = lax.optimization_barrier((late, far_first, odd_sum))
    far_second = swap(odd_sum[cut:], bits[0])
    late_got = lax.all_to_all(late, every, 0, 0, tiled=True)

    by_sender = jnp.broadcast_to(onehot_all[:, None, :], (n_dp, n_t, n_set)).reshape(-1, n_set)
    same_cols = (jnp.arange(n_dp * n_t, dtype=jnp.int32) % n_t == mine).astype(BF)
    tn = (((0,), (0,)), ((), ()))

    def total(got, weights):
        return lax.dot_general(weights, got, tn, preferred_element_type=F32)

    up_begin = late_got.shape[1] - up_share.shape[1]
    sums = total(early_got, by_sender)
    pieces = []
    start = 0
    for size in sizes:
        pieces.append(sums[:, start : start + size])
        start += size
    d_all = model // (n_dp * n_t)
    sum_down_out = pieces[0].reshape(n_set, r_dp, c_t).transpose(0, 2, 1)
    sum_up_out = pieces[1].reshape(n_set, rank, d_all)
    sum_down_fc1 = pieces[2].reshape(n_set, rank, d_all).transpose(0, 2, 1)
    sum_up_fc1 = pieces[3].reshape(n_set, r_dp, f_t)
    sum_down_fc2 = pieces[4].reshape(n_set, r_dp, f_t).transpose(0, 2, 1)
    sum_up_fc2 = pieces[5].reshape(n_set, rank, d_all)
    sum_down_qkv = (
        total(late_got[:, :up_begin], by_sender)
        .reshape(n_set, 3, rank, d_all)
        .transpose(1, 0, 3, 2)
    )
    sum_up_qkv = (
        total(late_got[:, up_begin:], by_sender * same_cols[:, None])
        .reshape(n_set, 3, r_dp, c_t)
        .transpose(1, 0, 2, 3)
    )
    here, sum_up_fc1 = lax.optimization_barrier((here, sum_up_fc1))
    grad_input = here + jnp.concatenate([far_first, far_second]).astype(F32)
    return (
        output,
        grad_input,
        sum_down_qkv,
        sum_up_qkv,
        sum_down_out,
        sum_up_out,
        sum_down_fc1,
        sum_up_fc1,
        sum_down_fc2,
        sum_up_fc2,
    )


def solution(mesh):
    both = ("dp", "tensor")
    in_specs = (
        P(both, None),
        P(both, None),
        P("dp", None),
        P("dp"),
        P(None, "dp", "tensor"),
        P("tensor", "dp"),
        P("dp", "tensor"),
        P("tensor", "dp"),
        P("dp"),
        P("dp"),
        P("dp"),
        P("dp"),
        P(None, None, "dp", None),
        P(None, None, "dp", "tensor"),
        P(None, "tensor", "dp"),
        P(None, None, "dp"),
        P(None, "dp", None),
        P(None, "dp", "tensor"),
        P(None, "tensor", "dp"),
        P(None, None, "dp"),
    )
    out_specs = (
        P(both, None),
        P(both, None),
        P(None, None, both, None),
        P(None, None, "dp", "tensor"),
        P(None, "tensor", "dp"),
        P(None, None, both),
        P(None, both, None),
        P(None, "dp", "tensor"),
        P(None, "tensor", "dp"),
        P(None, None, both),
    )
    return jax.shard_map(shards, mesh=mesh, in_specs=in_specs, out_specs=out_specs, check_vma=False)
```
